32 devices in a mesh: dp: 4 (over y, core), fsdp: 8 (over z, x).
Axes of the slice: x: 2, y: 2, z: 4, core: 2. Of those that a mesh axis runs over, the one named last changes fastest.
Arguments:
- tokens_in: bfloat16 [2, 128, 784, 128], P(None, ('dp', 'fsdp')), may hold values from -6 to 6
- cotangent: bfloat16 [2, 128, 784, 128], P(None, ('dp', 'fsdp')), may hold values from -6 to 6
- crop_ids: int32 [2, 128, 784], P(None, ('dp', 'fsdp')), may hold values from 0 to 3, as said below
- weight_query: float32 [128, 128], P('dp', 'fsdp'), may hold values from -0.5 to 0.5
- moment_query: float32 [128, 128], P('dp', 'fsdp'), may hold values from -0.9 to 0.9
- rowvar_query: float32 [128], P('dp'), may hold values from 16725 to 66901
- colvar_query: float32 [128], P('fsdp'), may hold values from 16725 to 66901
- weight_pairs: float32 [128, 256], P('dp', 'fsdp'), may hold values from -0.5 to 0.5
- moment_pairs: float32 [128, 256], P('dp', 'fsdp'), may hold values from -0.9 to 0.9
- rowvar_pairs: float32 [128], P('dp'), may hold values from 100352 to 401408
- colvar_pairs: float32 [256], P('fsdp'), may hold values from 100352 to 401408
- weight_reduce: float32 [2048, 128], P('dp', 'fsdp'), may hold values from -0.125 to 0.125
- moment_reduce: float32 [2048, 128], P('dp', 'fsdp'), may hold values from -0.9 to 0.9
- rowvar_reduce: float32 [2048], P('dp'), may hold values from 66901 to 267605
- colvar_reduce: float32 [128], P('fsdp'), may hold values from 200704 to 802816
- weight_output: float32 [128, 128], P('dp', 'fsdp'), may hold values from -1.5 to 1.5
- moment_output: float32 [128, 128], P('dp', 'fsdp'), may hold values from -0.9 to 0.9
- rowvar_output: float32 [128], P('dp'), may hold values from 8028 to 32112
- colvar_output: float32 [128], P('fsdp'), may hold values from 8028 to 32112
- weight_expand: float32 [128, 1024], P('dp', 'fsdp'), may hold values from -0.5 to 0.5
- moment_expand: float32 [128, 1024], P('dp', 'fsdp'), may hold values from -0.9 to 0.9
- rowvar_expand: float32 [128], P('dp'), may hold values from 2007 to 8028
- colvar_expand: float32 [1024], P('fsdp'), may hold values from 2007 to 8028
- weight_shrink: float32 [1024, 128], P('dp', 'fsdp'), may hold values from -0.1875 to 0.1875
- moment_shrink: float32 [1024, 128], P('dp', 'fsdp'), may hold values from -0.9 to 0.9
- rowvar_shrink: float32 [1024], P('dp'), may hold values from 16725 to 66901
- colvar_shrink: float32 [128], P('fsdp'), may hold values from 16725 to 66901
- weight_narrow: float32 [11, 128], P(None, 'fsdp'), may hold values from -1.5 to 2.5
- moment_narrow: float32 [11, 128], P(None, 'fsdp'), may hold values from -0.9 to 0.9
- second_narrow: float32 [11, 128], P(None, 'fsdp'), may hold values from 2007 to 1404928
- weight_wide: float32 [11, 1024], P(None, ('dp', 'fsdp')), may hold values from -2 to 2
- moment_wide: float32 [11, 1024], P(None, ('dp', 'fsdp')), may hold values from -0.9 to 0.9
- second_wide: float32 [11, 1024], P(None, ('dp', 'fsdp')), may hold values from 1672 to 6690
Outputs:
- block_out: bfloat16 [2, 128, 784, 128], P(None, ('dp', 'fsdp'))
- grad_input: bfloat16 [2, 128, 784, 128], P(None, ('dp', 'fsdp'))
- next_moment_query: float32 [128, 128], P('dp', 'fsdp')
- next_rowvar_query: float32 [128], P('dp')
- next_colvar_query: float32 [128], P('fsdp')
- next_weight_query: float32 [128, 128], P('dp', 'fsdp')
- next_moment_pairs: float32 [128, 256], P('dp', 'fsdp')
- next_rowvar_pairs: float32 [128], P('dp')
- next_colvar_pairs: float32 [256], P('fsdp')
- next_weight_pairs: float32 [128, 256], P('dp', 'fsdp')
- next_moment_reduce: float32 [2048, 128], P('dp', 'fsdp')
- next_rowvar_reduce: float32 [2048], P('dp')
- next_colvar_reduce: float32 [128], P('fsdp')
- next_weight_reduce: float32 [2048, 128], P('dp', 'fsdp')
- next_moment_output: float32 [128, 128], P('dp', 'fsdp')
- next_rowvar_output: float32 [128], P('dp')
- next_colvar_output: float32 [128], P('fsdp')
- next_weight_output: float32 [128, 128], P('dp', 'fsdp')
- next_moment_expand: float32 [128, 1024], P('dp', 'fsdp')
- next_rowvar_expand: float32 [128], P('dp')
- next_colvar_expand: float32 [1024], P('fsdp')
- next_weight_expand: float32 [128, 1024], P('dp', 'fsdp')
- next_moment_shrink: float32 [1024, 128], P('dp', 'fsdp')
- next_rowvar_shrink: float32 [1024], P('dp')
- next_colvar_shrink: float32 [128], P('fsdp')
- next_weight_shrink: float32 [1024, 128], P('dp', 'fsdp')
- next_moment_narrow: float32 [11, 128], P(None, 'fsdp')
- next_second_narrow: float32 [11, 128], P(None, 'fsdp')
- next_weight_narrow: float32 [11, 128], P(None, 'fsdp')
- next_moment_wide: float32 [11, 1024], P(None, ('dp', 'fsdp'))
- next_second_wide: float32 [11, 1024], P(None, ('dp', 'fsdp'))
- next_weight_wide: float32 [11, 1024], P(None, ('dp', 'fsdp'))
The draws below stay inside these ranges and needn't reach their ends.
Inputs may be any that keep to these rules, and one draw needn't show every extreme that they name: `crop_ids`: in each canvas the ids mark rectangles made of whole 4 x 4 blocks of tokens, and every id from 0 to 3 marks one of them.
All inputs are finite; a program needn't handle non-finite values.
Results may differ from the reference program's by a relative error of at most 0.02.
Values may be sent and summed in bfloat16 or wider, within the bound.
A program may use at most 576 MiB of HBM per device.

```python
import math
import jax
import jax.numpy as jnp
from jax import lax

D = 128
HEADS = 2
FF = 1024
GRID = 28
MICRO = 2
STEP = 10
CANVASES = 128
ROWS_ALL = 200704


def draw_crop_ids(key, part):
    key = jax.random.fold_in(key, 11)
    blocks = GRID // 4
    canvases = MICRO * CANVASES
    key_column, key_left, key_right = jax.random.split(key, 3)
    cut_column = jax.random.randint(key_column, (canvases, 1, 1), 1, blocks)
    cut_left = jax.random.randint(key_left, (canvases, 1, 1), 1, blocks)
    cut_right = jax.random.randint(key_right, (canvases, 1, 1), 1, blocks)
    row_index = lax.broadcasted_iota(jnp.int32, (1, blocks, blocks), 1)
    column_index = lax.broadcasted_iota(jnp.int32, (1, blocks, blocks), 2)
    on_right = (column_index >= cut_column).astype(jnp.int32)
    cut_row = jnp.where(on_right == 1, cut_right, cut_left)
    below_cut = (row_index >= cut_row).astype(jnp.int32)
    labels = 2 * on_right + below_cut
    labels = jnp.repeat(jnp.repeat(labels, 4, axis=1), 4, axis=2)
    return labels.reshape(MICRO, CANVASES, GRID * GRID).astype(jnp.int32)


def draw_weight_narrow(key, part):
    key = jax.random.fold_in(key, 23)
    key_gain, key_shift = jax.random.split(key, 2)
    rising = 0.5 + lax.broadcasted_iota(jnp.float32, (1, D), 1) / D
    row_index = lax.broadcasted_iota(jnp.int32, (11, D), 0)
    is_gain = (row_index == 0) | (row_index == 5) | (row_index == 8)
    gains = rising * (1.0 + 0.1 * jnp.clip(jax.random.normal(key_gain, (11, D), jnp.float32), -4.0, 4.0))
    shifts = 0.3 * jnp.clip(jax.random.normal(key_shift, (11, D), jnp.float32), -4.0, 4.0)
    return jnp.where(is_gain, gains, shifts).astype(jnp.float32)


def draw_second_narrow(key, part):
    key = jax.random.fold_in(key, 31)
    row_index = lax.broadcasted_iota(jnp.int32, (11, D), 0)
    row_scale = jnp.full((11, D), 1.0, jnp.float32)
    row_scale = jnp.where(row_index <= 1, 8.4, row_scale)
    row_scale = jnp.where(row_index == 2, 3.6, row_scale)
    row_scale = jnp.where(row_index == 3, 1.6, row_scale)
    row_scale = jnp.where((row_index >= 4) & (row_index <= 6), 5.0, row_scale)
    row_scale = jnp.where(row_index == 7, 1.2, row_scale)
    row_scale = jnp.where((row_index == 8) | (row_index == 9), 0.4, row_scale)
    spread = jax.random.uniform(key, (11, D), jnp.float32, 0.0, 1.0)
    factor = 0.19 * jnp.exp(spread * jnp.log(4.0))
    return (ROWS_ALL * row_scale * factor).astype(jnp.float32)


def levels(stream_key, shape, cuts, smallest, high):
    def one(axis_at, blocks):
        draws = jax.random.uniform(jax.random.fold_in(jax.random.fold_in(stream_key, 6), axis_at), (blocks,), jnp.float32, smallest / len(cuts), high / len(cuts))
        return jnp.repeat(jnp.exp(draws), shape[axis_at] // blocks).reshape((-1,) + (1,) * (len(shape) - axis_at - 1))

    level = one(*cuts[0])
    for cut in cuts[1:]:
        level = level * one(*cut)
    return level


def scatter_about(own_key, shape, scale, bound, pieces=(), held_as=jnp.bfloat16):
    values = scale * jax.random.normal(own_key, shape, jnp.float32)
    if pieces:
        values = values * levels(own_key, shape, pieces, -0.22, 0.18)
    return jnp.clip(values, -bound, bound).astype(held_as)


def setup_inputs(seed: int = 0) -> dict:
    seeds = jax.random.split(jax.random.key(seed), 34)
    return {
        "tokens_in": scatter_about(seeds[0], (MICRO, CANVASES, GRID * GRID, D), 1.0, 6.0, ((1, 32),)),
        "cotangent": scatter_about(seeds[1], (MICRO, CANVASES, GRID * GRID, D), 1.0, 6.0, ((1, 32),)),
        "crop_ids": draw_crop_ids(jax.random.fold_in(seeds[33], 71), 0),
        "weight_query": scatter_about(seeds[3], (D, D), D ** -0.5, 0.5, ((0, 4), (1, 8)), jnp.float32),
        "moment_query": scatter_about(seeds[4], (D, D), 0.15, 0.9, ((0, 4), (1, 8)), jnp.float32),
        "rowvar_query": jnp.clip(jnp.exp(math.log(66901.0) - 1.3863093 * jax.random.uniform(seeds[5], (D,), jnp.float32) ** levels(seeds[5], (D,), ((0, 4),), -0.2, 0.2)), 16725.0, 66901.0),
        "colvar_query": jnp.clip(jnp.exp(math.log(66901.0) - 1.3863093 * jax.random.uniform(seeds[6], (D,), jnp.float32) ** levels(seeds[6], (D,), ((0, 8),), -0.2, 0.2)), 16725.0, 66901.0),
        "weight_pairs": scatter_about(seeds[7], (D, 2 * D), D ** -0.5, 0.5, ((0, 4), (1, 8)), jnp.float32),
        "moment_pairs": scatter_about(seeds[8], (D, 2 * D), 0.15, 0.9, ((0, 4), (1, 8)), jnp.float32),
        "rowvar_pairs": jnp.clip(jnp.exp(math.log(401408.0) - 1.3862944 * jax.random.uniform(seeds[9], (D,), jnp.float32) ** levels(seeds[9], (D,), ((0, 4),), -0.2, 0.2)), 100352.0, 401408.0),
        "colvar_pairs": jnp.clip(jnp.exp(math.log(401408.0) - 1.3862944 * jax.random.uniform(seeds[10], (2 * D,), jnp.float32) ** levels(seeds[10], (2 * D,), ((0, 8),), -0.2, 0.2)), 100352.0, 401408.0),
        "weight_reduce": scatter_about(seeds[11], (16 * D, D), (16 * D) ** -0.5, 0.125, ((0, 4), (1, 8)), jnp.float32),
        "moment_reduce": scatter_about(seeds[12], (16 * D, D), 0.15, 0.9, ((0, 4), (1, 8)), jnp.float32),
        "rowvar_reduce": jnp.clip(jnp.exp(math.log(267605.0) - 1.3862981 * jax.random.uniform(seeds[13], (16 * D,), jnp.float32) ** levels(seeds[13], (16 * D,), ((0, 4),), -0.2, 0.2)), 66901.0, 267605.0),
        "colvar_reduce": jnp.clip(jnp.exp(math.log(802816.0) - 1.3862944 * jax.random.uniform(seeds[14], (D,), jnp.float32) ** levels(seeds[14], (D,), ((0, 8),), -0.2, 0.2)), 200704.0, 802816.0),
        "weight_output": scatter_about(seeds[15], (D, D), (D // 8) ** -0.5, 1.5, ((0, 4), (1, 8)), jnp.float32),
        "moment_output": scatter_about(seeds[16], (D, D), 0.15, 0.9, ((0, 4), (1, 8)), jnp.float32),
        "rowvar_output": jnp.clip(jnp.exp(math.log(32112.0) - 1.3862944 * jax.random.uniform(seeds[17], (D,), jnp.float32) ** levels(seeds[17], (D,), ((0, 4),), -0.2, 0.2)), 8028.0, 32112.0),
        "colvar_output": jnp.clip(jnp.exp(math.log(32112.0) - 1.3862944 * jax.random.uniform(seeds[18], (D,), jnp.float32) ** levels(seeds[18], (D,), ((0, 8),), -0.2, 0.2)), 8028.0, 32112.0),
        "weight_expand": scatter_about(seeds[19], (D, FF), D ** -0.5, 0.5, ((0, 4), (1, 8)), jnp.float32),
        "moment_expand": scatter_about(seeds[20], (D, FF), 0.15, 0.9, ((0, 4), (1, 8)), jnp.float32),
        "rowvar_expand": jnp.clip(jnp.exp(math.log(8028.0) - 1.3862944 * jax.random.uniform(seeds[21], (D,), jnp.float32) ** levels(seeds[21], (D,), ((0, 4),), -0.2, 0.2)), 2007.0, 8028.0),
        "colvar_expand": jnp.clip(jnp.exp(math.log(8028.0) - 1.3862944 * jax.random.uniform(seeds[22], (FF,), jnp.float32) ** levels(seeds[22], (FF,), ((0, 8),), -0.2, 0.2)), 2007.0, 8028.0),
        "weight_shrink": scatter_about(seeds[23], (FF, D), FF ** -0.5, 0.1875, ((0, 4), (1, 8)), jnp.float32),
        "moment_shrink": scatter_about(seeds[24], (FF, D), 0.15, 0.9, ((0, 4), (1, 8)), jnp.float32),
        "rowvar_shrink": jnp.clip(jnp.exp(math.log(66901.0) - 1.3863093 * jax.random.uniform(seeds[25], (FF,), jnp.float32) ** levels(seeds[25], (FF,), ((0, 4),), -0.2, 0.2)), 16725.0, 66901.0),
        "colvar_shrink": jnp.clip(jnp.exp(math.log(66901.0) - 1.3863093 * jax.random.uniform(seeds[26], (D,), jnp.float32) ** levels(seeds[26], (D,), ((0, 8),), -0.2, 0.2)), 16725.0, 66901.0),
        "weight_narrow": draw_weight_narrow(jax.random.fold_in(seeds[33], 71), 0),
        "moment_narrow": scatter_about(seeds[28], (11, D), 0.15, 0.9, ((1, 8),), jnp.float32),
        "second_narrow": draw_second_narrow(jax.random.fold_in(seeds[33], 71), 0),
        "weight_wide": scatter_about(seeds[30], (11, FF), 9 ** -0.5, 2.0, ((1, 32),), jnp.float32),
        "moment_wide": scatter_about(seeds[31], (11, FF), 0.15, 0.9, ((1, 32),), jnp.float32),
        "second_wide": jnp.clip(jnp.exp(math.log(6690.0) - 1.3865934 * jax.random.uniform(seeds[32], (11, FF), jnp.float32) ** levels(seeds[32], (11, FF), ((1, 32),), -0.2, 0.2)), 1672.0, 6690.0),
    }


@jax.custom_vjp
def low(v):
    return lax.optimization_barrier(v.astype(jnp.bfloat16)).astype(jnp.float32)

@jax.custom_vjp
def low_back(v):
    return v

def low_keep(v):
    return (low(v), None)

def low_pass(kept, grad):
    return (grad,)

def back_keep(v):
    return (v, None)

def back_low(kept, grad):
    return (low(grad),)
low.defvjp(low_keep, low_pass)
low_back.defvjp(back_keep, back_low)
NORM_EPS = 1e-06
SQUARE_EPS = 1e-30
CLIP_RMS = 1.0
BETA_ONE = 0.9
RATE = 1.0
DECAY_RATE = 0.01
MASKED = -1e+30

def layer_norm(values, norm_gain, norm_shift):
    center = values - lax.optimization_barrier(jnp.mean(values, axis=-1, keepdims=True))
    spread = lax.optimization_barrier(jnp.mean(center * center, axis=-1, keepdims=True))
    return center * lax.rsqrt(spread + NORM_EPS) * norm_gain + norm_shift

def depthwise(grid_values, tap_weights, crop_grid):
    extent = grid_values.shape[1]
    padded = jnp.pad(grid_values, ((0, 0), (1, 1), (1, 1), (0, 0)))
    padded_crops = jnp.pad(crop_grid, ((0, 0), (1, 1), (1, 1)), constant_values=-1)
    result = jnp.zeros_like(grid_values)
    for row_step in range(3):
        for col_step in range(3):
            nearby = padded[:, row_step:row_step + extent, col_step:col_step + extent, :]
            same_crop = padded_crops[:, row_step:row_step + extent, col_step:col_step + extent] == crop_grid
            result = result + jnp.where(same_crop[..., None], nearby, 0.0) * tap_weights[3 * row_step + col_step]
    return result

def product_high(left, right):
    return jnp.dot(left, right, precision=lax.Precision.HIGHEST, preferred_element_type=jnp.float32)

def block_forward(params, images, crop_rows):
    w_query, w_pairs, w_reduce, w_output, w_expand, w_shrink, narrow, vectors_wide = params
    canvases = images.shape[0]
    width = images.shape[2]
    hidden = w_expand.shape[1]
    blocks = GRID // 4
    tokens = GRID * GRID
    key_count = blocks * blocks
    head_size = width // HEADS
    score_scale = head_size ** (-0.5)
    inputs = images.reshape(canvases * tokens, width)
    normed = layer_norm(inputs, narrow[0], narrow[1])
    normed_low = low(normed)
    queries = low(low_back(product_high(normed_low, w_query) + narrow[2]))
    patches = normed_low.reshape(canvases, blocks, 4, blocks, 4, width).transpose(0, 1, 3, 2, 4, 5).reshape(canvases * key_count, 16 * width)
    reduced = low_back(product_high(patches, w_reduce) + narrow[4])
    reduced_norm = layer_norm(reduced, narrow[5], narrow[6])
    pair_bias = jnp.concatenate([jnp.zeros_like(narrow[3]), narrow[3]])
    pairs = low(low_back(product_high(low(reduced_norm), w_pairs) + pair_bias))
    query_heads = queries.reshape(canvases, tokens, HEADS, head_size)
    key_heads = pairs[:, :width].reshape(canvases, key_count, HEADS, head_size)
    value_heads = pairs[:, width:].reshape(canvases, key_count, HEADS, head_size)
    scores = low_back(jnp.einsum('bqhe,bkhe->bhqk', query_heads, key_heads, precision=lax.Precision.HIGHEST) * score_scale)
    key_crops = crop_rows.reshape(canvases, blocks, 4, blocks, 4)[:, :, 0, :, 0].reshape(canvases, key_count)
    allowed = crop_rows[:, None, :, None] == key_crops[:, None, None, :]
    scores = jnp.where(allowed, scores, MASKED)
    exponent = jnp.exp(scores - lax.optimization_barrier(jnp.max(scores, axis=-1, keepdims=True)))
    attention = exponent / lax.optimization_barrier(jnp.sum(exponent, axis=-1, keepdims=True))
    mixed_heads = jnp.einsum('bhqk,bkhe->bqhe', low(attention), value_heads, precision=lax.Precision.HIGHEST).reshape(canvases * tokens, width)
    mixed_heads = low(low_back(mixed_heads))
    residual = inputs + low_back(product_high(mixed_heads, w_output) + narrow[7])
    second_norm = layer_norm(residual, narrow[8], narrow[9])
    expanded = low_back(product_high(low(second_norm), w_expand) + vectors_wide[9])
    convolved = depthwise(expanded.reshape(canvases, GRID, GRID, hidden), vectors_wide[:9], crop_rows.reshape(canvases, GRID, GRID)) + vectors_wide[10]
    activated = jax.nn.gelu(convolved, approximate=False).reshape(canvases * tokens, hidden)
    branch = low_back(product_high(low(activated), w_shrink) + narrow[10])
    return (residual + branch).reshape(canvases, tokens, width)

def factored_step(weight, gradient, moment, rowvar, colvar):
    decay_two = 1.0 - STEP ** (-0.8)
    square = gradient * gradient + SQUARE_EPS
    row_new = decay_two * rowvar + (1.0 - decay_two) * lax.optimization_barrier(jnp.mean(square, axis=1))
    col_new = decay_two * colvar + (1.0 - decay_two) * lax.optimization_barrier(jnp.mean(square, axis=0))
    update = gradient * lax.rsqrt(row_new / jnp.mean(row_new))[:, None] * lax.rsqrt(col_new)[None, :]
    whole_norm = jnp.sqrt(jnp.mean(update * update))
    update = update / jnp.maximum(1.0, whole_norm / CLIP_RMS)
    moment_new = BETA_ONE * moment + (1.0 - BETA_ONE) * update
    weight_new = weight * (1.0 - RATE * DECAY_RATE) - RATE * moment_new
    return (moment_new, row_new, col_new, weight_new)

def stacked_step(weight, gradient, moment, second):
    decay_two = 1.0 - STEP ** (-0.8)
    second_new = decay_two * second + (1.0 - decay_two) * (gradient * gradient + SQUARE_EPS)
    update = gradient * lax.rsqrt(second_new)
    row_norm = jnp.sqrt(lax.optimization_barrier(jnp.mean(update * update, axis=1, keepdims=True)))
    update = update / jnp.maximum(1.0, row_norm / CLIP_RMS)
    moment_new = BETA_ONE * moment + (1.0 - BETA_ONE) * update
    weight_new = weight * (1.0 - RATE * DECAY_RATE) - RATE * moment_new
    return (moment_new, second_new, weight_new)

def reference(tokens_in, cotangent, crop_ids, weight_query, moment_query, rowvar_query, colvar_query, weight_pairs, moment_pairs, rowvar_pairs, colvar_pairs, weight_reduce, moment_reduce, rowvar_reduce, colvar_reduce, weight_output, moment_output, rowvar_output, colvar_output, weight_expand, moment_expand, rowvar_expand, colvar_expand, weight_shrink, moment_shrink, rowvar_shrink, colvar_shrink, weight_narrow, moment_narrow, second_narrow, weight_wide, moment_wide, second_wide):
    masters = (weight_query, weight_pairs, weight_reduce, weight_output, weight_expand, weight_shrink, weight_narrow, weight_wide)
    canvases = MICRO * CANVASES
    tokens = GRID * GRID
    groups = canvases // 4
    images = tokens_in.astype(jnp.float32).reshape(groups, 4, tokens, D)
    crop_groups = crop_ids.reshape(groups, 4, tokens)

    def whole(params, image_groups):
        rounded = tuple((low(weight) for weight in params))

        def one_group(packed):
            return block_forward(rounded, packed[0], packed[1])
        return lax.map(jax.checkpoint(one_group), (image_groups, crop_groups))
    outputs, pullback = jax.vjp(whole, masters, images)
    grads, image_grads = pullback(cotangent.astype(jnp.float32).reshape(groups, 4, tokens, D))
    block_out = outputs.reshape(MICRO, CANVASES, tokens, D).astype(jnp.bfloat16)
    grad_input = image_grads.reshape(MICRO, CANVASES, tokens, D).astype(jnp.bfloat16)
    next_moment_query, next_rowvar_query, next_colvar_query, next_weight_query = factored_step(weight_query, grads[0], moment_query, rowvar_query, colvar_query)
    next_moment_pairs, next_rowvar_pairs, next_colvar_pairs, next_weight_pairs = factored_step(weight_pairs, grads[1], moment_pairs, rowvar_pairs, colvar_pairs)
    next_moment_reduce, next_rowvar_reduce, next_colvar_reduce, next_weight_reduce = factored_step(weight_reduce, grads[2], moment_reduce, rowvar_reduce, colvar_reduce)
    next_moment_output, next_rowvar_output, next_colvar_output, next_weight_output = factored_step(weight_output, grads[3], moment_output, rowvar_output, colvar_output)
    next_moment_expand, next_rowvar_expand, next_colvar_expand, next_weight_expand = factored_step(weight_expand, grads[4], moment_expand, rowvar_expand, colvar_expand)
    next_moment_shrink, next_rowvar_shrink, next_colvar_shrink, next_weight_shrink = factored_step(weight_shrink, grads[5], moment_shrink, rowvar_shrink, colvar_shrink)
    next_moment_narrow, next_second_narrow, next_weight_narrow = stacked_step(weight_narrow, grads[6], moment_narrow, second_narrow)
    next_moment_wide, next_second_wide, next_weight_wide = stacked_step(weight_wide, grads[7], moment_wide, second_wide)
    return (block_out, grad_input, next_moment_query, next_rowvar_query, next_colvar_query, next_weight_query, next_moment_pairs, next_rowvar_pairs, next_colvar_pairs, next_weight_pairs, next_moment_reduce, next_rowvar_reduce, next_colvar_reduce, next_weight_reduce, next_moment_output, next_rowvar_output, next_colvar_output, next_weight_output, next_moment_expand, next_rowvar_expand, next_colvar_expand, next_weight_expand, next_moment_shrink, next_rowvar_shrink, next_colvar_shrink, next_weight_shrink, next_moment_narrow, next_second_narrow, next_weight_narrow, next_moment_wide, next_second_wide, next_weight_wide)
```

```python
import functools
import numpy as np
import jax
import jax.numpy as jnp
from jax import lax
from jax.experimental import pallas as pl
from jax.experimental.pallas import tpu as pltpu
from jax.sharding import PartitionSpec as P

HEADS = 2
GRID = 28
STEP = 10
NORM_EPS = 1e-06
SQUARE_EPS = 1e-30
CLIP_RMS = 1.0
BETA_ONE = 0.9
RATE = 1.0
DECAY_RATE = 0.01
MASKED = -1e30

D = 128
FF = 1024
SIDE = 4
BLOCKS = GRID // SIDE
KEYS = BLOCKS * BLOCKS
PAD_KEYS = KEYS + 1
GROUPS = SIDE * SIDE
TAPS = 9
DEPTH = (TAPS + 1) * D
MARGIN = 64
CHUNK = 256

F32 = jnp.float32
BF16 = jnp.bfloat16

PIECES = (
    ("reduce", (D, GROUPS * D), "f", "d"),
    ("shrink", (D, FF), "f", "d"),
    ("expand", (D, FF), "d", "f"),
    ("query", (D, D), "f", "d"),
    ("output", (D, D), "f", "d"),
    ("pairs", (D, 2 * D), "d", "f"),
    ("wide", (11, FF), "", "df"),
    ("narrow", (11, D), "", "f"),
)


class Plan:
    def __init__(self, dp, fsdp):
        self.dp, self.fsdp = dp, fsdp
        cuts = {"": 1, "d": dp, "f": fsdp, "df": dp * fsdp}
        self.shard = {}
        self.chunks = []
        free = []
        for name, (rows, cols), by_rows, by_cols in PIECES:
            height, width = rows // cuts[by_rows], cols // cuts[by_cols]
            self.shard[name] = (height, width)
            for row in range(0, height, 16):
                for col in range(0, width, D):
                    tall, wide = min(16, height - row), min(D, width - col)
                    for tile, used in enumerate(free):
                        if used + wide <= D:
                            break
                    else:
                        tile = len(free)
                        free.append(0)
                    self.chunks.append((name, tile, free[tile], tall, wide, row, col))
                    free[tile] += wide
        self.tiles = len(free)
        self.rows = 16 * self.tiles

    def origin(self, name, d, f):
        _, _, by_rows, by_cols = next(piece for piece in PIECES if piece[0] == name)
        at = {"": 0, "d": d, "f": f, "df": d * self.fsdp + f}
        height, width = self.shard[name]
        return at[by_rows] * height, at[by_cols] * width


def nn(left, right):
    return lax.dot_general(left, right, (((1,), (0,)), ((), ())), preferred_element_type=F32)


def nt(left, right):
    return lax.dot_general(left, right, (((1,), (1,)), ((), ())), preferred_element_type=F32)


def tn(left, right):
    return lax.dot_general(left, right, (((0,), (0,)), ((), ())), preferred_element_type=F32)


def fold(values):
    rows, cols = values.shape
    return jnp.sum(values.reshape(rows // 8, 8, cols), axis=0)


def normalize(values):
    center = values - jnp.mean(values, axis=-1, keepdims=True)
    scale = lax.rsqrt(jnp.mean(center * center, axis=-1, keepdims=True) + NORM_EPS)
    return center * scale, scale


def normalize_back(unit, scale, incoming, gain):
    c = incoming * gain
    mean_c = jnp.mean(c, axis=-1, keepdims=True)
    mean_cz = jnp.mean(c * unit, axis=-1, keepdims=True)
    return (c - mean_c - unit * mean_cz) * scale


def gelu_parts(v):
    bell = jnp.exp(v * v * -0.5)
    size = jnp.abs(v)
    below = 1.0 + (0.3275911 * 0.5**0.5) * size
    t = pl.reciprocal(below, approx=True)
    t = t * (2.0 - below * t)
    poly = t * (
        0.5 * 0.254829592
        + t
        * (
            0.5 * -0.284496736
            + t * (0.5 * 1.421413741 + t * (0.5 * -1.453152027 + t * (0.5 * 1.061405429)))
        )
    )
    tail = poly * bell
    share = jnp.where(v >= 0.0, 1.0 - tail, tail)
    return v * share, share + v * bell * 0.3989422804014327


def direction(step_at):
    return -1 if step_at < 0 else (1 if step_at >= SIDE else 0)


def halo_list():
    found = {}
    for at in range(-1, SIDE + 1):
        for bt in range(-1, SIDE + 1):
            di, dj = direction(at), direction(bt)
            if di or dj:
                group = (at % SIDE) * SIDE + bt % SIDE
                found.setdefault((di, dj), []).append((at + 1, bt + 1, group))
    return [((di + 1) * 3 + dj + 1, di * BLOCKS + dj, places) for (di, dj), places in sorted(found.items())]


def selector():
    table = np.zeros((9, D, D), np.float32)
    for row_class in range(3):
        for col_class in range(3):
            for row_step in (-1, 0, 1):
                for col_step in (-1, 0, 1):
                    di = row_step if row_step == row_class - 1 else 0
                    dj = col_step if col_step == col_class - 1 else 0
                    tap = (row_step + 1) * 3 + col_step + 1
                    source = (di + 1) * 3 + dj + 1
                    table[row_class * 3 + col_class, source, tap] = 1.0
                    table[row_class * 3 + col_class, source, 16 + tap] = 1.0
            table[row_class * 3 + col_class, 9, 9] = 1.0
            table[row_class * 3 + col_class, 9, 25] = 1.0
    return table


def crop_tables(crop_rows):
    canvases = crop_rows.shape[0]
    grid = crop_rows.reshape(canvases, BLOCKS, SIDE, BLOCKS, SIDE)[:, :, 0, :, 0].astype(F32)
    padded = jnp.pad(grid, ((0, 0), (1, 1), (1, 1)), constant_values=-1.0)
    columns = []
    for di in (-1, 0, 1):
        for dj in (-1, 0, 1):
            near = padded[:, 1 + di : 1 + di + BLOCKS, 1 + dj : 1 + dj + BLOCKS]
            columns.append((near == grid).astype(F32))
    columns.append(jnp.ones_like(grid))
    masks = jnp.stack(columns, axis=-1).reshape(canvases, KEYS, 10).transpose(1, 0, 2)
    masks = jnp.pad(masks, ((0, 1), (0, 0), (0, D - 10))).reshape(PAD_KEYS * canvases, D)
    flat = grid.reshape(canvases, KEYS)
    rows = jnp.pad(flat.T, ((0, 1), (0, 0)), constant_values=-1.0).reshape(PAD_KEYS * canvases, 1)
    rows = jnp.broadcast_to(rows, (PAD_KEYS * canvases, D))
    half = jnp.pad(flat, ((0, 0), (0, D // 2 - KEYS)), constant_values=-2.0)
    keys = jnp.concatenate([half, half], axis=1).reshape(canvases, 1, D)
    return rows, masks, keys


def compute_kernel(
    plan,
    x_ref,
    dy_ref,
    crop_ref,
    mask_ref,
    keycrop_ref,
    sel_ref,
    blob_ref,
    out_ref,
    gin_ref,
    gblob_ref,
    stage,
    passing,
    arrived,
    held,
    mixed_s,
    inputs_s,
    dy_s,
    normed_s,
    query_s,
    attn_s,
    probs_s,
    key_s,
    value_s,
    dkey_s,
    dvalue_s,
    halo_s,
    window_s,
    dconv_s,
    big_s,
    pad_s,
    bias_s,
    taps_s,
    dtaps_s,
    w_reduce,
    w_shrink,
    w_expand,
    w_query,
    w_output,
    w_pairs,
    w_wide,
    w_narrow,
    lo_reduce,
    lo_shrink,
    lo_query,
    lo_output,
    lo_pairs,
    g_reduce,
    g_shrink,
    g_query,
    g_output,
    g_pairs,
    g_wide,
    g_narrow,
    sums,
):
    canvases = x_ref.shape[0]
    rows = PAD_KEYS * canvases
    lane = lax.broadcasted_iota(jnp.int32, (1, D), 1)
    low_half = lane < D // 2
    full = {
        "reduce": w_reduce,
        "shrink": w_shrink,
        "expand": w_expand,
        "query": w_query,
        "output": w_output,
        "pairs": w_pairs,
        "wide": w_wide,
        "narrow": w_narrow,
    }
    for d in range(plan.dp):
        for f in range(plan.fsdp):
            base = (d * plan.fsdp + f) * plan.rows
            for name, tile, at, tall, wide, row, col in plan.chunks:
                if name == "narrow" and d:
                    continue
                r0, c0 = plan.origin(name, d, f)
                tile_rows = blob_ref[base + 16 * tile : base + 16 * tile + 16, :].astype(F32)
                full[name][r0 + row : r0 + row + tall, c0 + col : c0 + col + wide] = tile_rows[
                    :tall, at : at + wide
                ]
    lo_reduce[...] = w_reduce[...].astype(BF16)
    lo_shrink[...] = w_shrink[...].astype(BF16)
    lo_query[...] = w_query[...].astype(BF16)
    lo_output[...] = w_output[...].astype(BF16)
    lo_pairs[...] = w_pairs[...].astype(BF16)
    for tap in range(TAPS):
        taps_s[tap * D : (tap + 1) * D, :] = (w_expand[...] * w_wide[tap : tap + 1, :]).astype(BF16)
    bias_rows = w_wide[9:10, :] * w_wide[0:9, :]
    bias_rows = jnp.concatenate([bias_rows, w_wide[10:11, :], jnp.zeros((6, FF), F32)], axis=0)
    bias_high = bias_rows.astype(BF16)
    bias_low = (bias_rows - bias_high.astype(F32)).astype(BF16)
    taps_s[TAPS * D : TAPS * D + 16, :] = bias_high
    taps_s[TAPS * D + 16 : TAPS * D + 32, :] = bias_low
    taps_s[TAPS * D + 32 :, :] = jnp.zeros((D - 32, FF), BF16)

    def narrow(row):
        return w_narrow[row : row + 1, :]

    sums[...] = jnp.zeros_like(sums)
    held[...] = jnp.zeros_like(held)
    pad_s[...] = jnp.zeros_like(pad_s)
    dtaps_s[...] = jnp.zeros_like(dtaps_s)
    for ref in (g_shrink, g_query, g_output, g_narrow, g_wide):
        ref[...] = jnp.zeros_like(ref)
    for ref in (key_s, value_s):
        ref[rows:, :] = jnp.zeros((ref.shape[0] - rows, D), F32)

    def add(row, values):
        sums[8 * row : 8 * row + 8, :] += fold(values)

    def group_rows(g):
        return pl.ds(pl.multiple_of(g * rows, 16), rows)

    def held_rows(g):
        return pl.ds(pl.multiple_of(MARGIN + g * rows, 16), rows)

    def group_lanes(g):
        return pl.ds(pl.multiple_of(g * D, D), D)

    def places():
        for g in range(GROUPS):
            for block_row in range(BLOCKS):
                token = block_row * SIDE * GRID + (g // SIDE) * GRID + g % SIDE
                yield token, MARGIN + g * rows + block_row * BLOCKS * canvases

    def scatter(source):
        def fetch(c):
            slot = lax.rem(c, 2)
            return pltpu.make_async_copy(source.at[c], passing.at[slot], arrived.at[slot])

        fetch(0).start()

        def one(c, _):
            @pl.when(c + 1 < canvases)
            def _():
                fetch(c + 1).start()

            fetch(c).wait()
            stage[...] = passing[lax.rem(c, 2)].astype(F32)
            for token, place in places():
                held[pl.ds(place + c, BLOCKS, stride=canvases), :] = stage[
                    pl.ds(token, BLOCKS, stride=SIDE), :
                ]
            return 0

        lax.fori_loop(0, canvases, one, 0)

    def collect(target):
        def leave(c):
            slot = lax.rem(c, 2)
            return pltpu.make_async_copy(passing.at[slot], target.at[c], arrived.at[slot])

        def one(c, _):
            for token, place in places():
                stage[pl.ds(token, BLOCKS, stride=SIDE), :] = held[
                    pl.ds(place + c, BLOCKS, stride=canvases), :
                ]

            @pl.when(c >= 2)
            def _():
                leave(c - 2).wait()

            passing[lax.rem(c, 2)] = stage[...].astype(BF16)
            leave(c).start()
            return 0

        lax.fori_loop(0, canvases, one, 0)
        for c in range(max(0, canvases - 2), canvases):
            leave(c).wait()

    scatter(dy_ref)

    def keep_dy(g, _):
        dy_s[group_rows(g), :] = held[held_rows(g), :].astype(BF16)
        return 0

    lax.fori_loop(0, GROUPS, keep_dy, 0)
    scatter(x_ref)

    def first(g, _):
        values = held[held_rows(g), :]
        mixed_s[group_rows(g), :] = values
        inputs_s[group_rows(g), :] = values.astype(BF16)
        unit, _ = normalize(values)
        low = (unit * narrow(0) + narrow(1)).astype(BF16)
        normed_s[:, group_lanes(g)] = low
        query_s[group_rows(g), :] = (nt(low, lo_query[...]) + narrow(2)).astype(BF16).astype(F32)
        big_s[group_rows(g), :] = crop_ref[...]
        return 0

    lax.fori_loop(0, GROUPS, first, 0)

    reduced = nt(normed_s[...], lo_reduce[...]) + narrow(4)
    reduced_unit, reduced_scale = normalize(reduced)
    reduced_low = (reduced_unit * narrow(5) + narrow(6)).astype(BF16)
    pairs = nn(reduced_low, lo_pairs[...])
    key_s[:rows, :] = pairs[:, :D].astype(BF16).astype(F32)
    value_s[:rows, :] = (pairs[:, D:] + narrow(3)).astype(BF16).astype(F32)

    def split_heads(values):
        return jnp.concatenate(
            [jnp.where(low_half, values, 0.0), jnp.where(low_half, 0.0, values)], axis=0
        ).astype(BF16)

    def join_heads(values):
        return jnp.where(low_half, values[: D // 2, :], values[D // 2 :, :])

    tokens = GROUPS * PAD_KEYS

    def canvas_rows(c):
        return pl.ds(c, tokens, stride=canvases)

    def held_canvas_rows(c):
        return pl.ds(MARGIN + c, tokens, stride=canvases)

    def key_rows(c):
        return pl.ds(c, D // 2, stride=canvases)

    def per_head(values, reduce, fill):
        first_half = reduce(jnp.where(low_half, values, fill), axis=-1, keepdims=True)
        second_half = reduce(jnp.where(low_half, fill, values), axis=-1, keepdims=True)
        return jnp.where(low_half, first_half, second_half)

    def attend(c, _):
        queries = query_s[canvas_rows(c), :].astype(BF16)
        keys = split_heads(key_s[key_rows(c), :])
        values = split_heads(value_s[key_rows(c), :])
        scores = nt(queries, keys) * (D // HEADS) ** (-0.5)
        allowed = big_s[canvas_rows(c), :] == keycrop_ref[c]
        scores = jnp.where(allowed, scores, MASKED)
        exponent = jnp.exp(scores - per_head(scores, jnp.max, -3e38))
        exponent = jnp.where(allowed, exponent, 0.0)
        total = jnp.maximum(per_head(exponent, jnp.sum, 0.0), 1.0)
        probs = (exponent / total).astype(BF16)
        probs_s[c] = probs
        held[held_canvas_rows(c), :] = nn(probs, values)
        return 0

    lax.fori_loop(0, canvases, attend, 0)

    def second(g, _):
        low = held[held_rows(g), :].astype(BF16)
        attn_s[group_rows(g), :] = low
        mixed = mixed_s[group_rows(g), :] + (nt(low, lo_output[...]) + narrow(7))
        mixed_s[group_rows(g), :] = mixed
        unit, _ = normalize(mixed)
        normed = unit * narrow(8) + narrow(9)
        held[held_rows(g), :] = normed
        halo_s[g // SIDE + 1, :, group_lanes(g % SIDE + 1)] = normed.astype(BF16)
        return 0

    lax.fori_loop(0, GROUPS, second, 0)
    for number, step, spots in halo_list():
        mask = mask_ref[:, number : number + 1] > 0.0
        for at, bt, g in spots:
            start = MARGIN + g * rows + step * canvases
            near = jnp.where(mask, held[start : start + rows, :], 0.0)
            halo_s[at, :, bt * D : (bt + 1) * D] = near.astype(BF16)
    mask_low = mask_ref[...].astype(BF16)
    for kind in range(9):
        bias_s[kind] = nn(mask_low, sel_ref[kind]).astype(BF16)

    big_s[...] = jnp.zeros_like(big_s)

    def feed(a, _):
        for b in range(SIDE):
            g = a * SIDE + b
            kind = jnp.where(a == 0, 0, jnp.where(a == SIDE - 1, 2, 1)) * 3 + (
                0 if b == 0 else (2 if b == SIDE - 1 else 1)
            )
            window = jnp.concatenate(
                [halo_s[a + step, :, b * D : (b + 3) * D] for step in range(3)] + [bias_s[kind]],
                axis=1,
            )
            window_s[b] = window
            cot = dy_s[group_rows(g), :]
            branch = None
            for n in range(0, FF, CHUNK):
                conv = nn(window, taps_s[:, n : n + CHUNK])
                act, slope = gelu_parts(conv)
                act = act.astype(BF16)
                weight = lo_shrink[:, n : n + CHUNK]
                part = nt(act, weight)
                branch = part if branch is None else branch + part
                g_shrink[:, n : n + CHUNK] += tn(cot, act)
                dconv_s[b, :, n : n + CHUNK] = (nn(cot, weight) * slope).astype(BF16)
            held[held_rows(g), :] = mixed_s[group_rows(g), :] + (branch + narrow(10))
            back = nt(dconv_s[b], taps_s[: TAPS * D, :])
            for tap in range(TAPS):
                place = (a + tap // 3) * (SIDE + 2) + b + tap % 3
                big_s[group_rows(place), :] += back[:, tap * D : (tap + 1) * D]
        dtaps_s[...] += tn(
            window_s[...].reshape(SIDE * rows, DEPTH), dconv_s[...].reshape(SIDE * rows, FF)
        )
        return 0

    lax.fori_loop(0, SIDE, feed, 0)
    collect(out_ref)

    for number, step, spots in halo_list():
        mask = mask_ref[:, number : number + 1] > 0.0
        for at, bt, g in spots:
            place = (at * (SIDE + 2) + bt) * rows
            inner = ((g // SIDE + 1) * (SIDE + 2) + g % SIDE + 1) * rows
            pad_s[MARGIN : MARGIN + rows, :] = jnp.where(mask, big_s[place : place + rows, :], 0.0)
            start = MARGIN - step * canvases
            big_s[inner : inner + rows, :] += pad_s[start : start + rows, :]

    def third(g, _):
        place = (g // SIDE + 1) * (SIDE + 2) + g % SIDE + 1
        cot = dy_s[group_rows(g), :]
        incoming = big_s[group_rows(place), :]
        unit, scale = normalize(mixed_s[group_rows(g), :])
        d_mixed = cot.astype(F32) + normalize_back(unit, scale, incoming, narrow(8))
        add(8, incoming * unit)
        add(9, incoming)
        add(10, cot.astype(F32))
        mixed_s[group_rows(g), :] = d_mixed
        low = d_mixed.astype(BF16)
        add(7, low.astype(F32))
        g_output[...] += tn(low, attn_s[group_rows(g), :])
        held[held_rows(g), :] = nn(low, lo_output[...])
        return 0

    lax.fori_loop(0, GROUPS, third, 0)

    def attend_back(c, _):
        queries = query_s[canvas_rows(c), :].astype(BF16)
        keys = split_heads(key_s[key_rows(c), :])
        values = split_heads(value_s[key_rows(c), :])
        probs_low = probs_s[c]
        probs = probs_low.astype(F32)
        d_attn = held[held_canvas_rows(c), :].astype(BF16)
        d_probs = nt(d_attn, values)
        d_scores = probs * (d_probs - per_head(d_probs * probs, jnp.sum, 0.0))
        d_scores = d_scores.astype(BF16)
        scale = (D // HEADS) ** (-0.5)
        held[held_canvas_rows(c), :] = nn(d_scores, keys) * scale
        dkey_s[key_rows(c), :] = join_heads(tn(d_scores, queries)) * scale
        dvalue_s[key_rows(c), :] = join_heads(tn(probs_low, d_attn))
        return 0

    lax.fori_loop(0, canvases, attend_back, 0)

    d_pairs = jnp.concatenate([dkey_s[:rows, :], dvalue_s[:rows, :]], axis=1).astype(BF16)
    g_pairs[...] = tn(reduced_low, d_pairs)
    add(3, d_pairs[:, D:].astype(F32))
    incoming = nt(d_pairs, lo_pairs[...])
    add(5, incoming * reduced_unit)
    add(6, incoming)
    d_reduced = normalize_back(reduced_unit, reduced_scale, incoming, narrow(5)).astype(BF16)
    add(4, d_reduced.astype(F32))
    g_reduce[...] = tn(d_reduced, normed_s[...])

    def fourth(g, _):
        low = held[held_rows(g), :].astype(BF16)
        add(2, low.astype(F32))
        g_query[...] += tn(low, normed_s[:, group_lanes(g)])
        incoming = nn(low, lo_query[...]) + nn(d_reduced, lo_reduce[:, group_lanes(g)])
        unit, scale = normalize(inputs_s[group_rows(g), :].astype(F32))
        add(0, incoming * unit)
        add(1, incoming)
        back = normalize_back(unit, scale, incoming, narrow(0))
        held[held_rows(g), :] = mixed_s[group_rows(g), :] + back
        return 0

    lax.fori_loop(0, GROUPS, fourth, 0)
    collect(gin_ref)

    for row in range(11):
        g_narrow[row : row + 1, :] = jnp.sum(sums[8 * row : 8 * row + 8, :], axis=0, keepdims=True)
    g_wide[10:11, :] = dtaps_s[TAPS * D + 9 : TAPS * D + 10, :]
    g_expand = w_reduce
    d_bias = jnp.zeros((1, FF), F32)
    for tap in range(TAPS):
        tap_row = w_wide[tap : tap + 1, :]
        through = dtaps_s[TAPS * D + tap : TAPS * D + tap + 1, :]
        block = dtaps_s[tap * D : (tap + 1) * D, :]
        d_bias += tap_row * through
        g_wide[tap : tap + 1, :] = jnp.sum(w_expand[...] * block, axis=0, keepdims=True) + (
            w_wide[9:10, :] * through
        )
        if tap:
            g_expand[:, :FF] += tap_row * block
        else:
            g_expand[:, :FF] = tap_row * block
    g_wide[9:10, :] = d_bias
    grads = {
        "reduce": g_reduce,
        "shrink": g_shrink,
        "expand": g_expand,
        "query": g_query,
        "output": g_output,
        "pairs": g_pairs,
        "wide": g_wide,
        "narrow": g_narrow,
    }
    blank = jnp.zeros((16, D), F32)
    for d in range(plan.dp):
        for f in range(plan.fsdp):
            base = (d * plan.fsdp + f) * plan.rows
            for tile in range(plan.tiles):
                held[0:16, :] = blank
                for name, where, at, tall, wide, row, col in plan.chunks:
                    if where == tile:
                        r0, c0 = plan.origin(name, d, f)
                        held[0:tall, at : at + wide] = grads[name][
                            r0 + row : r0 + row + tall, c0 + col : c0 + col + wide
                        ]
                gblob_ref[base + 16 * tile : base + 16 * tile + 16, :] = held[0:16, :].astype(BF16)


def compute(plan, tokens, cots, crops, blobs):
    canvases, length, width = tokens.shape
    rows = PAD_KEYS * canvases
    every = GROUPS * rows
    crop_rows, masks, keycrops = crop_tables(crops)
    sel = jnp.asarray(selector(), BF16)
    vm = pl.BlockSpec(memory_space=pltpu.VMEM)
    hbm = pl.BlockSpec(memory_space=pl.ANY)
    scratch = [
        pltpu.VMEM((length, D), F32),
        pltpu.VMEM((2, length, D), BF16),
        pltpu.SemaphoreType.DMA((2,)),
        pltpu.VMEM((every + 2 * MARGIN, D), F32),
        pltpu.VMEM((every, D), F32),
        pltpu.VMEM((every, D), BF16),
        pltpu.VMEM((every, D), BF16),
        pltpu.VMEM((rows, GROUPS * D), BF16),
        pltpu.VMEM((every, D), F32),
        pltpu.VMEM((every, D), BF16),
        pltpu.VMEM((canvases, GROUPS * PAD_KEYS, D), BF16),
        pltpu.VMEM((D // 2 * canvases, D), F32),
        pltpu.VMEM((D // 2 * canvases, D), F32),
        pltpu.VMEM((D // 2 * canvases, D), F32),
        pltpu.VMEM((D // 2 * canvases, D), F32),
        pltpu.VMEM((SIDE + 2, rows, (SIDE + 2) * D), BF16),
        pltpu.VMEM((SIDE, rows, DEPTH), BF16),
        pltpu.VMEM((SIDE, rows, FF), BF16),
        pltpu.VMEM(((SIDE + 2) ** 2 * rows, D), F32),
        pltpu.VMEM((rows + 2 * MARGIN, D), F32),
        pltpu.VMEM((9, rows, D), BF16),
        pltpu.VMEM((DEPTH, FF), BF16),
        pltpu.VMEM((DEPTH, FF), F32),
        pltpu.VMEM((D, GROUPS * D), F32),
        pltpu.VMEM((D, FF), F32),
        pltpu.VMEM((D, FF), F32),
        pltpu.VMEM((D, D), F32),
        pltpu.VMEM((D, D), F32),
        pltpu.VMEM((D, 2 * D), F32),
        pltpu.VMEM((16, FF), F32),
        pltpu.VMEM((16, D), F32),
        pltpu.VMEM((D, GROUPS * D), BF16),
        pltpu.VMEM((D, FF), BF16),
        pltpu.VMEM((D, D), BF16),
        pltpu.VMEM((D, D), BF16),
        pltpu.VMEM((D, 2 * D), BF16),
        pltpu.VMEM((D, GROUPS * D), F32),
        pltpu.VMEM((D, FF), F32),
        pltpu.VMEM((D, D), F32),
        pltpu.VMEM((D, D), F32),
        pltpu.VMEM((D, 2 * D), F32),
        pltpu.VMEM((16, FF), F32),
        pltpu.VMEM((16, D), F32),
        pltpu.VMEM((88, D), F32),
    ]
    return pl.pallas_call(
        functools.partial(compute_kernel, plan),
        out_shape=(
            jax.ShapeDtypeStruct(tokens.shape, BF16),
            jax.ShapeDtypeStruct(tokens.shape, BF16),
            jax.ShapeDtypeStruct(blobs.shape, BF16),
        ),
        in_specs=[hbm] * 2 + [vm] * 5,
        out_specs=(hbm, hbm, vm),
        scratch_shapes=scratch,
        compiler_params=pltpu.CompilerParams(vmem_limit_bytes=63 * 1024 * 1024),
    )(tokens, cots, crop_rows, masks, keycrops, sel, blobs)


def pack(plan, shards):
    tiles = [jnp.zeros((16, D), F32) for _ in range(plan.tiles)]
    for name, tile, at, tall, wide, row, col in plan.chunks:
        tiles[tile] = (
            tiles[tile]
            .at[:tall, at : at + wide]
            .set(shards[name][row : row + tall, col : col + wide])
        )
    return jnp.concatenate(tiles, axis=0)


def unpack(plan, blob):
    found = {name: jnp.zeros(shape, F32) for name, shape in plan.shard.items()}
    for name, tile, at, tall, wide, row, col in plan.chunks:
        part = blob[16 * tile : 16 * tile + tall, at : at + wide]
        found[name] = found[name].at[row : row + tall, col : col + wide].set(part)
    return found


NAMES = ("query", "pairs", "reduce", "output", "expand", "shrink")
TURNED = ("query", "reduce", "output", "shrink")


def body(plan, tokens_in, cotangent, crop_ids, *state):
    weights, moments, rowvars, colvars = {}, {}, {}, {}
    for number, name in enumerate(NAMES):
        weights[name], moments[name], rowvars[name], colvars[name] = state[4 * number : 4 * number + 4]
    for number, name in enumerate(("narrow", "wide")):
        weights[name], moments[name], rowvars[name] = state[24 + 3 * number : 27 + 3 * number]
    shards = {name: value.T if name in TURNED else value for name, value in weights.items()}
    micro, local, length, width = tokens_in.shape
    flat = (micro * local, length, width)
    axes = ("dp", "fsdp")
    blob = pack(plan, shards).astype(BF16)
    blobs = lax.all_gather(blob, axes, axis=0, tiled=True)
    result, input_grad, gblobs = compute(
        plan,
        tokens_in.reshape(flat),
        cotangent.reshape(flat),
        crop_ids.reshape(micro * local, length),
        blobs,
    )
    summed = lax.psum_scatter(gblobs, axes, scatter_dimension=0, tiled=True).astype(F32)
    grads = unpack(plan, summed)
    grads = {name: value.T if name in TURNED else value for name, value in grads.items()}
    decay_two = 1.0 - STEP ** (-0.8)
    dp_count, fsdp_count = plan.dp, plan.fsdp
    dp_first = (lax.axis_index("dp") == 0).astype(F32)
    squares = {name: grads[name] * grads[name] + SQUARE_EPS for name in NAMES}
    full_rows = {name: grads[name].shape[0] * dp_count for name in NAMES}
    full_cols = {name: grads[name].shape[1] * fsdp_count for name in NAMES}
    row_totals = lax.psum(tuple(jnp.sum(squares[name], axis=1) for name in NAMES), "fsdp")
    row_new = {
        name: decay_two * rowvars[name] + (1.0 - decay_two) * total / full_cols[name]
        for name, total in zip(NAMES, row_totals)
    }
    col_totals, row_sums, narrow_grad = lax.psum(
        (
            tuple(jnp.sum(squares[name], axis=0) for name in NAMES),
            tuple(jnp.sum(row_new[name]) for name in NAMES),
            grads["narrow"] * dp_first,
        ),
        "dp",
    )
    col_new = {
        name: decay_two * colvars[name] + (1.0 - decay_two) * total / full_rows[name]
        for name, total in zip(NAMES, col_totals)
    }
    updates = {}
    for name, row_sum in zip(NAMES, row_sums):
        mean = row_sum / full_rows[name]
        updates[name] = (
            grads[name]
            * lax.rsqrt(row_new[name] / mean)[:, None]
            * lax.rsqrt(col_new[name])[None, :]
        )
    grads["narrow"] = narrow_grad
    second = {}
    for name in ("narrow", "wide"):
        grad = grads[name]
        second[name] = decay_two * rowvars[name] + (1.0 - decay_two) * (grad * grad + SQUARE_EPS)
        updates[name] = grad * lax.rsqrt(second[name])
    norms = lax.psum(
        tuple(jnp.sum(updates[name] * updates[name]) for name in NAMES)
        + (
            jnp.sum(updates["narrow"] * updates["narrow"], axis=1) * dp_first,
            jnp.sum(updates["wide"] * updates["wide"], axis=1),
        ),
        axes,
    )
    sizes = [full_rows[name] * full_cols[name] for name in NAMES] + [D, FF]
    next_moment, next_weight = {}, {}
    for name, norm, size in zip(NAMES + ("narrow", "wide"), norms, sizes):
        clip = jnp.maximum(1.0, jnp.sqrt(norm / size) / CLIP_RMS)
        if norm.ndim:
            clip = clip[:, None]
        next_moment[name] = BETA_ONE * moments[name] + (1.0 - BETA_ONE) * (updates[name] / clip)
        next_weight[name] = weights[name] * (1.0 - RATE * DECAY_RATE) - RATE * next_moment[name]
    results = [result.reshape(tokens_in.shape), input_grad.reshape(tokens_in.shape)]
    for name in NAMES:
        results += [next_moment[name], row_new[name], col_new[name], next_weight[name]]
    for name in ("narrow", "wide"):
        results += [next_moment[name], second[name], next_weight[name]]
    return tuple(results)


def solution(mesh):
    plan = Plan(mesh.shape["dp"], mesh.shape["fsdp"])
    tokens = P(None, ("dp", "fsdp"), None, None)
    matrix = P("dp", "fsdp")
    by_rows, by_cols = P("dp"), P("fsdp")
    thin, broad = P(None, "fsdp"), P(None, ("dp", "fsdp"))
    state = (matrix, matrix, by_rows, by_cols) * 6 + (thin,) * 3 + (broad,) * 3
    in_specs = (tokens, tokens, P(None, ("dp", "fsdp"), None)) + state
    moved = (matrix, by_rows, by_cols, matrix) * 6 + (thin,) * 3 + (broad,) * 3
    return jax.shard_map(
        functools.partial(body, plan),
        mesh=mesh,
        in_specs=in_specs,
        out_specs=(tokens, tokens) + moved,
        check_vma=False,
    )
```

```python
import functools
import numpy as np
import jax
import jax.numpy as jnp
from jax import lax
from jax.experimental import pallas as pl
from jax.experimental.pallas import tpu as pltpu
from jax.sharding import PartitionSpec as P

HEADS = 2
GRID = 28
STEP = 10
NORM_EPS = 1e-06
SQUARE_EPS = 1e-30
CLIP_RMS = 1.0
BETA_ONE = 0.9
RATE = 1.0
DECAY_RATE = 0.01
MASKED = -1e30

D = 128
FF = 1024
SIDE = 4
BLOCKS = GRID // SIDE
KEYS = BLOCKS * BLOCKS
PAD_KEYS = KEYS + 1
GROUPS = SIDE * SIDE
TAPS = 9
DEPTH = (TAPS + 1) * D
MARGIN = 64
CHUNK = 256

F32 = jnp.float32
BF16 = jnp.bfloat16

PIECES = (
    ("reduce", (D, GROUPS * D), "f", "d"),
    ("shrink", (D, FF), "f", "d"),
    ("expand", (D, FF), "d", "f"),
    ("query", (D, D), "f", "d"),
    ("output", (D, D), "f", "d"),
    ("pairs", (D, 2 * D), "d", "f"),
    ("wide", (11, FF), "", "df"),
    ("narrow", (11, D), "", "f"),
)


class Plan:
    def __init__(self, dp, fsdp):
        self.dp, self.fsdp = dp, fsdp
        cuts = {"": 1, "d": dp, "f": fsdp, "df": dp * fsdp}
        self.shard = {}
        self.chunks = []
        free = []
        for name, (rows, cols), by_rows, by_cols in PIECES:
            height, width = rows // cuts[by_rows], cols // cuts[by_cols]
            self.shard[name] = (height, width)
            for row in range(0, height, 16):
                for col in range(0, width, D):
                    tall, wide = min(16, height - row), min(D, width - col)
                    for tile, used in enumerate(free):
                        if used + wide <= D:
                            break
                    else:
                        tile = len(free)
                        free.append(0)
                    self.chunks.append((name, tile, free[tile], tall, wide, row, col))
                    free[tile] += wide
        self.tiles = len(free)
        self.rows = 16 * self.tiles
        self.devices = dp * fsdp
        self.cores = 2 if dp % 2 == 0 else 1
        self.ys = dp // self.cores
        self.xs = 1
        while self.xs * self.xs * 4 <= fsdp and fsdp % (2 * self.xs) == 0:
            self.xs *= 2
        self.zs = fsdp // self.xs

    def base(self, d, f):
        y, core = divmod(d, self.cores)
        z, x = divmod(f, self.xs)
        return (((core * self.ys + y) * self.xs + x) * self.zs + z) * self.rows

    def origin(self, name, d, f):
        _, _, by_rows, by_cols = next(piece for piece in PIECES if piece[0] == name)
        at = {"": 0, "d": d, "f": f, "df": d * self.fsdp + f}
        height, width = self.shard[name]
        return at[by_rows] * height, at[by_cols] * width


def nn(left, right):
    return lax.dot_general(left, right, (((1,), (0,)), ((), ())), preferred_element_type=F32)


def nt(left, right):
    return lax.dot_general(left, right, (((1,), (1,)), ((), ())), preferred_element_type=F32)


def tn(left, right):
    return lax.dot_general(left, right, (((0,), (0,)), ((), ())), preferred_element_type=F32)


def fold(values):
    rows, cols = values.shape
    return jnp.sum(values.reshape(rows // 8, 8, cols), axis=0)


def normalize(values):
    center = values - jnp.mean(values, axis=-1, keepdims=True)
    scale = lax.rsqrt(jnp.mean(center * center, axis=-1, keepdims=True) + NORM_EPS)
    return center * scale, scale


def normalize_back(unit, scale, incoming, gain):
    c = incoming * gain
    mean_c = jnp.mean(c, axis=-1, keepdims=True)
    mean_cz = jnp.mean(c * unit, axis=-1, keepdims=True)
    return (c - mean_c - unit * mean_cz) * scale


def gelu_parts(v):
    bell = jnp.exp(v * v * -0.5)
    size = jnp.abs(v)
    below = 1.0 + (0.3275911 * 0.5**0.5) * size
    t = pl.reciprocal(below, approx=True)
    t = t * (2.0 - below * t)
    poly = t * (
        0.5 * 0.254829592
        + t
        * (
            0.5 * -0.284496736
            + t * (0.5 * 1.421413741 + t * (0.5 * -1.453152027 + t * (0.5 * 1.061405429)))
        )
    )
    tail = poly * bell
    share = jnp.where(v >= 0.0, 1.0 - tail, tail)
    return v * share, share + v * bell * 0.3989422804014327


def direction(step_at):
    return -1 if step_at < 0 else (1 if step_at >= SIDE else 0)


def halo_list():
    found = {}
    for at in range(-1, SIDE + 1):
        for bt in range(-1, SIDE + 1):
            di, dj = direction(at), direction(bt)
            if di or dj:
                group = (at % SIDE) * SIDE + bt % SIDE
                found.setdefault((di, dj), []).append((at + 1, bt + 1, group))
    return [((di + 1) * 3 + dj + 1, di * BLOCKS + dj, places) for (di, dj), places in sorted(found.items())]


def selector():
    table = np.zeros((9, D, D), np.float32)
    for row_class in range(3):
        for col_class in range(3):
            for row_step in (-1, 0, 1):
                for col_step in (-1, 0, 1):
                    di = row_step if row_step == row_class - 1 else 0
                    dj = col_step if col_step == col_class - 1 else 0
                    tap = (row_step + 1) * 3 + col_step + 1
                    source = (di + 1) * 3 + dj + 1
                    table[row_class * 3 + col_class, source, tap] = 1.0
                    table[row_class * 3 + col_class, source, 16 + tap] = 1.0
            table[row_class * 3 + col_class, 9, 9] = 1.0
            table[row_class * 3 + col_class, 9, 25] = 1.0
    return table


def compute_kernel(
    plan,
    x_ref,
    dy_ref,
    crop_ref,
    sel_ref,
    blob_ref,
    out_ref,
    gin_ref,
    gblob_ref,
    stage,
    passing,
    arrived,
    held,
    mixed_s,
    inputs_s,
    dy_s,
    normed_s,
    query_s,
    attn_s,
    probs_s,
    key_s,
    value_s,
    dkey_s,
    dvalue_s,
    halo_s,
    window_s,
    dconv_s,
    big_s,
    pad_s,
    bias_s,
    crop_s,
    mask_s,
    keycrop_s,
    taps_s,
    dtaps_s,
    w_reduce,
    w_shrink,
    w_expand,
    w_query,
    w_output,
    w_pairs,
    w_wide,
    w_narrow,
    lo_reduce,
    lo_shrink,
    lo_query,
    lo_output,
    lo_pairs,
    g_reduce,
    g_shrink,
    g_query,
    g_output,
    g_pairs,
    g_wide,
    g_narrow,
    sums,
):
    canvases = x_ref.shape[0]
    rows = PAD_KEYS * canvases
    lane = lax.broadcasted_iota(jnp.int32, (1, D), 1)
    low_half = lane < D // 2
    full = {
        "reduce": w_reduce,
        "shrink": w_shrink,
        "expand": w_expand,
        "query": w_query,
        "output": w_output,
        "pairs": w_pairs,
        "wide": w_wide,
        "narrow": w_narrow,
    }
    for d in range(plan.dp):
        for f in range(plan.fsdp):
            base = plan.base(d, f)
            for name, tile, at, tall, wide, row, col in plan.chunks:
                if name == "narrow" and d:
                    continue
                r0, c0 = plan.origin(name, d, f)
                tile_rows = blob_ref[base + 16 * tile : base + 16 * tile + 16, :].astype(F32)
                full[name][r0 + row : r0 + row + tall, c0 + col : c0 + col + wide] = tile_rows[
                    :tall, at : at + wide
                ]
    lo_reduce[...] = w_reduce[...].astype(BF16)
    lo_shrink[...] = w_shrink[...].astype(BF16)
    lo_query[...] = w_query[...].astype(BF16)
    lo_output[...] = w_output[...].astype(BF16)
    lo_pairs[...] = w_pairs[...].astype(BF16)
    for tap in range(TAPS):
        taps_s[tap * D : (tap + 1) * D, :] = (w_expand[...] * w_wide[tap : tap + 1, :]).astype(BF16)
    bias_rows = w_wide[9:10, :] * w_wide[0:9, :]
    bias_rows = jnp.concatenate([bias_rows, w_wide[10:11, :], jnp.zeros((6, FF), F32)], axis=0)
    bias_high = bias_rows.astype(BF16)
    bias_low = (bias_rows - bias_high.astype(F32)).astype(BF16)
    taps_s[TAPS * D : TAPS * D + 16, :] = bias_high
    taps_s[TAPS * D + 16 : TAPS * D + 32, :] = bias_low
    taps_s[TAPS * D + 32 :, :] = jnp.zeros((D - 32, FF), BF16)

    def narrow(row):
        return w_narrow[row : row + 1, :]

    sums[...] = jnp.zeros_like(sums)
    held[...] = jnp.zeros_like(held)
    pad_s[...] = jnp.zeros_like(pad_s)
    dtaps_s[...] = jnp.zeros_like(dtaps_s)
    for ref in (g_shrink, g_query, g_output, g_narrow, g_wide):
        ref[...] = jnp.zeros_like(ref)
    for ref in (key_s, value_s):
        ref[rows:, :] = jnp.zeros((ref.shape[0] - rows, D), F32)

    def add(row, values):
        sums[8 * row : 8 * row + 8, :] += fold(values)

    def group_rows(g):
        return pl.ds(pl.multiple_of(g * rows, 16), rows)

    def held_rows(g):
        return pl.ds(pl.multiple_of(MARGIN + g * rows, 16), rows)

    def group_lanes(g):
        return pl.ds(pl.multiple_of(g * D, D), D)

    def places():
        for g in range(GROUPS):
            for block_row in range(BLOCKS):
                token = block_row * SIDE * GRID + (g // SIDE) * GRID + g % SIDE
                yield token, MARGIN + g * rows + block_row * BLOCKS * canvases

    def scatter(source):
        def fetch(c):
            slot = lax.rem(c, 2)
            return pltpu.make_async_copy(source.at[c], passing.at[slot], arrived.at[slot])

        fetch(0).start()

        def one(c, _):
            @pl.when(c + 1 < canvases)
            def _():
                fetch(c + 1).start()

            fetch(c).wait()
            stage[...] = passing[lax.rem(c, 2)].astype(F32)
            for token, place in places():
                held[pl.ds(place + c, BLOCKS, stride=canvases), :] = stage[
                    pl.ds(token, BLOCKS, stride=SIDE), :
                ]
            return 0

        lax.fori_loop(0, canvases, one, 0)

    def collect(target):
        def leave(c):
            slot = lax.rem(c, 2)
            return pltpu.make_async_copy(passing.at[slot], target.at[c], arrived.at[slot])

        def one(c, _):
            for token, place in places():
                stage[pl.ds(token, BLOCKS, stride=SIDE), :] = held[
                    pl.ds(place + c, BLOCKS, stride=canvases), :
                ]

            @pl.when(c >= 2)
            def _():
                leave(c - 2).wait()

            passing[lax.rem(c, 2)] = stage[...].astype(BF16)
            leave(c).start()
            return 0

        lax.fori_loop(0, canvases, one, 0)
        for c in range(max(0, canvases - 2), canvases):
            leave(c).wait()

    key_lane = lax.rem(lax.broadcasted_iota(jnp.int32, (GRID * GRID, D), 1), D // 2)
    corner = lax.div(key_lane, BLOCKS) * (SIDE * GRID) + lax.rem(key_lane, BLOCKS) * SIDE
    token = lax.broadcasted_iota(jnp.int32, (GRID * GRID, D), 0)
    picked = jnp.where((corner == token) & (key_lane < KEYS), 1.0, 0.0).astype(BF16)
    crops = jnp.concatenate([crop_ref[m] for m in range(crop_ref.shape[0])], axis=0)
    keycrop = nn(crops.astype(F32).astype(BF16), picked)
    keycrop = jnp.where(lax.rem(lane, D // 2) < KEYS, keycrop, -2.0)
    keycrop_s[...] = keycrop.reshape(keycrop_s.shape)
    by_key = jnp.concatenate([keycrop, jnp.zeros((D - canvases, D), F32)], axis=0).T
    crop_s[...] = jnp.full(crop_s.shape, -1.0, F32)
    for c in range(canvases):
        crop_s[pl.ds(MARGIN + c, KEYS, stride=canvases), :] = jnp.broadcast_to(
            by_key[:KEYS, c : c + 1], (KEYS, D)
        )
    own_crop = crop_s[MARGIN : MARGIN + rows, :]
    block = lax.div(lax.broadcasted_iota(jnp.int32, (rows, D), 0), canvases)
    block_i, block_j = lax.div(block, BLOCKS), lax.rem(block, BLOCKS)
    columns = jnp.where(lax.broadcasted_iota(jnp.int32, (rows, D), 1) == 9, 1.0, 0.0)
    for di in (-1, 0, 1):
        for dj in (-1, 0, 1):
            number = (di + 1) * 3 + dj + 1
            start = MARGIN + (di * BLOCKS + dj) * canvases
            inside = (block < KEYS) & (block_i + di >= 0) & (block_i + di < BLOCKS)
            inside = inside & (block_j + dj >= 0) & (block_j + dj < BLOCKS)
            near = crop_s[start : start + rows, :] == own_crop
            mask = jnp.where(near & inside, 1.0, 0.0)
            mask_s[number] = mask.astype(BF16)
            columns = jnp.where(lane == number, mask, columns)
    mask_low = columns.astype(BF16)
    for kind in range(9):
        bias_s[kind] = nn(mask_low, sel_ref[kind]).astype(BF16)

    scatter(dy_ref)

    def keep_dy(g, _):
        dy_s[group_rows(g), :] = held[held_rows(g), :].astype(BF16)
        return 0

    lax.fori_loop(0, GROUPS, keep_dy, 0)
    scatter(x_ref)

    def first(g, _):
        values = held[held_rows(g), :]
        mixed_s[group_rows(g), :] = values
        inputs_s[group_rows(g), :] = values.astype(BF16)
        unit, _ = normalize(values)
        low = (unit * narrow(0) + narrow(1)).astype(BF16)
        normed_s[:, group_lanes(g)] = low
        query_s[group_rows(g), :] = (nt(low, lo_query[...]) + narrow(2)).astype(BF16).astype(F32)
        big_s[group_rows(g), :] = crop_s[MARGIN : MARGIN + rows, :]
        return 0

    lax.fori_loop(0, GROUPS, first, 0)

    reduced = nt(normed_s[...], lo_reduce[...]) + narrow(4)
    reduced_unit, reduced_scale = normalize(reduced)
    reduced_low = (reduced_unit * narrow(5) + narrow(6)).astype(BF16)
    pairs = nn(reduced_low, lo_pairs[...])
    key_s[:rows, :] = pairs[:, :D].astype(BF16).astype(F32)
    value_s[:rows, :] = (pairs[:, D:] + narrow(3)).astype(BF16).astype(F32)

    def split_heads(values):
        return jnp.concatenate(
            [jnp.where(low_half, values, 0.0), jnp.where(low_half, 0.0, values)], axis=0
        ).astype(BF16)

    def join_heads(values):
        return jnp.where(low_half, values[: D // 2, :], values[D // 2 :, :])

    tokens = GROUPS * PAD_KEYS

    def canvas_rows(c):
        return pl.ds(c, tokens, stride=canvases)

    def held_canvas_rows(c):
        return pl.ds(MARGIN + c, tokens, stride=canvases)

    def key_rows(c):
        return pl.ds(c, D // 2, stride=canvases)

    def per_head(values, reduce, fill):
        first_half = reduce(jnp.where(low_half, values, fill), axis=-1, keepdims=True)
        second_half = reduce(jnp.where(low_half, fill, values), axis=-1, keepdims=True)
        return jnp.where(low_half, first_half, second_half)

    def attend(c, _):
        queries = query_s[canvas_rows(c), :].astype(BF16)
        keys = split_heads(key_s[key_rows(c), :])
        values = split_heads(value_s[key_rows(c), :])
        scores = nt(queries, keys) * (D // HEADS) ** (-0.5)
        allowed = big_s[canvas_rows(c), :] == keycrop_s[c]
        scores = jnp.where(allowed, scores, MASKED)
        exponent = jnp.exp(scores - per_head(scores, jnp.max, -3e38))
        exponent = jnp.where(allowed, exponent, 0.0)
        total = jnp.maximum(per_head(exponent, jnp.sum, 0.0), 1.0)
        probs = (exponent / total).astype(BF16)
        probs_s[c] = probs
        held[held_canvas_rows(c), :] = nn(probs, values)
        return 0

    lax.fori_loop(0, canvases, attend, 0)

    def second(g, _):
        low = held[held_rows(g), :].astype(BF16)
        attn_s[group_rows(g), :] = low
        mixed = mixed_s[group_rows(g), :] + (nt(low, lo_output[...]) + narrow(7))
        mixed_s[group_rows(g), :] = mixed
        unit, _ = normalize(mixed)
        normed = unit * narrow(8) + narrow(9)
        held[held_rows(g), :] = normed
        halo_s[g // SIDE + 1, :, group_lanes(g % SIDE + 1)] = normed.astype(BF16)
        return 0

    lax.fori_loop(0, GROUPS, second, 0)
    for number, step, spots in halo_list():
        mask = mask_s[number].astype(F32) > 0.0
        for at, bt, g in spots:
            start = MARGIN + g * rows + step * canvases
            near = jnp.where(mask, held[start : start + rows, :], 0.0)
            halo_s[at, :, bt * D : (bt + 1) * D] = near.astype(BF16)

    big_s[...] = jnp.zeros_like(big_s)

    def feed(a, _):
        for b in range(SIDE):
            g = a * SIDE + b
            kind = jnp.where(a == 0, 0, jnp.where(a == SIDE - 1, 2, 1)) * 3 + (
                0 if b == 0 else (2 if b == SIDE - 1 else 1)
            )
            window = jnp.concatenate(
                [halo_s[a + step, :, b * D : (b + 3) * D] for step in range(3)] + [bias_s[kind]],
                axis=1,
            )
            window_s[b] = window
            cot = dy_s[group_rows(g), :]
            branch = None
            for n in range(0, FF, CHUNK):
                conv = nn(window, taps_s[:, n : n + CHUNK])
                act, slope = gelu_parts(conv)
                act = act.astype(BF16)
                weight = lo_shrink[:, n : n + CHUNK]
                part = nt(act, weight)
                branch = part if branch is None else branch + part
                g_shrink[:, n : n + CHUNK] += tn(cot, act)
                dconv_s[b, :, n : n + CHUNK] = (nn(cot, weight) * slope).astype(BF16)
            held[held_rows(g), :] = mixed_s[group_rows(g), :] + (branch + narrow(10))
            back = nt(dconv_s[b], taps_s[: TAPS * D, :])
            for tap in range(TAPS):
                place = (a + tap // 3) * (SIDE + 2) + b + tap % 3
                big_s[group_rows(place), :] += back[:, tap * D : (tap + 1) * D]
        dtaps_s[...] += tn(
            window_s[...].reshape(SIDE * rows, DEPTH), dconv_s[...].reshape(SIDE * rows, FF)
        )
        return 0

    lax.fori_loop(0, SIDE, feed, 0)
    collect(out_ref)

    for number, step, spots in halo_list():
        mask = mask_s[number].astype(F32) > 0.0
        for at, bt, g in spots:
            place = (at * (SIDE + 2) + bt) * rows
            inner = ((g // SIDE + 1) * (SIDE + 2) + g % SIDE + 1) * rows
            pad_s[MARGIN : MARGIN + rows, :] = jnp.where(mask, big_s[place : place + rows, :], 0.0)
            start = MARGIN - step * canvases
            big_s[inner : inner + rows, :] += pad_s[start : start + rows, :]

    def third(g, _):
        place = (g // SIDE + 1) * (SIDE + 2) + g % SIDE + 1
        cot = dy_s[group_rows(g), :]
        incoming = big_s[group_rows(place), :]
        unit, scale = normalize(mixed_s[group_rows(g), :])
        d_mixed = cot.astype(F32) + normalize_back(unit, scale, incoming, narrow(8))
        add(8, incoming * unit)
        add(9, incoming)
        add(10, cot.astype(F32))
        mixed_s[group_rows(g), :] = d_mixed
        low = d_mixed.astype(BF16)
        add(7, low.astype(F32))
        g_output[...] += tn(low, attn_s[group_rows(g), :])
        held[held_rows(g), :] = nn(low, lo_output[...])
        return 0

    lax.fori_loop(0, GROUPS, third, 0)

    def attend_back(c, _):
        queries = query_s[canvas_rows(c), :].astype(BF16)
        keys = split_heads(key_s[key_rows(c), :])
        values = split_heads(value_s[key_rows(c), :])
        probs_low = probs_s[c]
        probs = probs_low.astype(F32)
        d_attn = held[held_canvas_rows(c), :].astype(BF16)
        d_probs = nt(d_attn, values)
        d_scores = probs * (d_probs - per_head(d_probs * probs, jnp.sum, 0.0))
        d_scores = d_scores.astype(BF16)
        scale = (D // HEADS) ** (-0.5)
        held[held_canvas_rows(c), :] = nn(d_scores, keys) * scale
        dkey_s[key_rows(c), :] = join_heads(tn(d_scores, queries)) * scale
        dvalue_s[key_rows(c), :] = join_heads(tn(probs_low, d_attn))
        return 0

    lax.fori_loop(0, canvases, attend_back, 0)

    d_pairs = jnp.concatenate([dkey_s[:rows, :], dvalue_s[:rows, :]], axis=1).astype(BF16)
    g_pairs[...] = tn(reduced_low, d_pairs)
    add(3, d_pairs[:, D:].astype(F32))
    incoming = nt(d_pairs, lo_pairs[...])
    add(5, incoming * reduced_unit)
    add(6, incoming)
    d_reduced = normalize_back(reduced_unit, reduced_scale, incoming, narrow(5)).astype(BF16)
    add(4, d_reduced.astype(F32))
    g_reduce[...] = tn(d_reduced, normed_s[...])

    def fourth(g, _):
        low = held[held_rows(g), :].astype(BF16)
        add(2, low.astype(F32))
        g_query[...] += tn(low, normed_s[:, group_lanes(g)])
        incoming = nn(low, lo_query[...]) + nn(d_reduced, lo_reduce[:, group_lanes(g)])
        unit, scale = normalize(inputs_s[group_rows(g), :].astype(F32))
        add(0, incoming * unit)
        add(1, incoming)
        back = normalize_back(unit, scale, incoming, narrow(0))
        held[held_rows(g), :] = mixed_s[group_rows(g), :] + back
        return 0

    lax.fori_loop(0, GROUPS, fourth, 0)
    collect(gin_ref)

    for row in range(11):
        g_narrow[row : row + 1, :] = jnp.sum(sums[8 * row : 8 * row + 8, :], axis=0, keepdims=True)
    g_wide[10:11, :] = dtaps_s[TAPS * D + 9 : TAPS * D + 10, :]
    g_expand = w_reduce
    d_bias = jnp.zeros((1, FF), F32)
    for tap in range(TAPS):
        tap_row = w_wide[tap : tap + 1, :]
        through = dtaps_s[TAPS * D + tap : TAPS * D + tap + 1, :]
        block = dtaps_s[tap * D : (tap + 1) * D, :]
        d_bias += tap_row * through
        g_wide[tap : tap + 1, :] = jnp.sum(w_expand[...] * block, axis=0, keepdims=True) + (
            w_wide[9:10, :] * through
        )
        if tap:
            g_expand[:, :FF] += tap_row * block
        else:
            g_expand[:, :FF] = tap_row * block
    g_wide[9:10, :] = d_bias
    grads = {
        "reduce": g_reduce,
        "shrink": g_shrink,
        "expand": g_expand,
        "query": g_query,
        "output": g_output,
        "pairs": g_pairs,
        "wide": g_wide,
        "narrow": g_narrow,
    }
    blank = jnp.zeros((16, D), F32)
    for d in range(plan.dp):
        for f in range(plan.fsdp):
            base = plan.base(d, f)
            for tile in range(plan.tiles):
                held[0:16, :] = blank
                for name, where, at, tall, wide, row, col in plan.chunks:
                    if where == tile:
                        r0, c0 = plan.origin(name, d, f)
                        held[0:tall, at : at + wide] = grads[name][
                            r0 + row : r0 + row + tall, c0 + col : c0 + col + wide
                        ]
                gblob_ref[base + 16 * tile : base + 16 * tile + 16, :] = held[0:16, :].astype(BF16)


def compute(plan, tokens, cots, crops, blobs):
    canvases, length, width = tokens.shape
    rows = PAD_KEYS * canvases
    every = GROUPS * rows
    sel = jnp.asarray(selector(), BF16)
    vm = pl.BlockSpec(memory_space=pltpu.VMEM)
    hbm = pl.BlockSpec(memory_space=pl.ANY)
    scratch = [
        pltpu.VMEM((length, D), F32),
        pltpu.VMEM((2, length, D), BF16),
        pltpu.SemaphoreType.DMA((2,)),
        pltpu.VMEM((every + 2 * MARGIN, D), F32),
        pltpu.VMEM((every, D), F32),
        pltpu.VMEM((every, D), BF16),
        pltpu.VMEM((every, D), BF16),
        pltpu.VMEM((rows, GROUPS * D), BF16),
        pltpu.VMEM((every, D), F32),
        pltpu.VMEM((every, D), BF16),
        pltpu.VMEM((canvases, GROUPS * PAD_KEYS, D), BF16),
        pltpu.VMEM((D // 2 * canvases, D), F32),
        pltpu.VMEM((D // 2 * canvases, D), F32),
        pltpu.VMEM((D // 2 * canvases, D), F32),
        pltpu.VMEM((D // 2 * canvases, D), F32),
        pltpu.VMEM((SIDE + 2, rows, (SIDE + 2) * D), BF16),
        pltpu.VMEM((SIDE, rows, DEPTH), BF16),
        pltpu.VMEM((SIDE, rows, FF), BF16),
        pltpu.VMEM(((SIDE + 2) ** 2 * rows, D), F32),
        pltpu.VMEM((rows + 2 * MARGIN, D), F32),
        pltpu.VMEM((9, rows, D), BF16),
        pltpu.VMEM((rows + 2 * MARGIN, D), F32),
        pltpu.VMEM((9, rows, D), BF16),
        pltpu.VMEM((canvases, 1, D), F32),
        pltpu.VMEM((DEPTH, FF), BF16),
        pltpu.VMEM((DEPTH, FF), F32),
        pltpu.VMEM((D, GROUPS * D), F32),
        pltpu.VMEM((D, FF), F32),
        pltpu.VMEM((D, FF), F32),
        pltpu.VMEM((D, D), F32),
        pltpu.VMEM((D, D), F32),
        pltpu.VMEM((D, 2 * D), F32),
        pltpu.VMEM((16, FF), F32),
        pltpu.VMEM((16, D), F32),
        pltpu.VMEM((D, GROUPS * D), BF16),
        pltpu.VMEM((D, FF), BF16),
        pltpu.VMEM((D, D), BF16),
        pltpu.VMEM((D, D), BF16),
        pltpu.VMEM((D, 2 * D), BF16),
        pltpu.VMEM((D, GROUPS * D), F32),
        pltpu.VMEM((D, FF), F32),
        pltpu.VMEM((D, D), F32),
        pltpu.VMEM((D, D), F32),
        pltpu.VMEM((D, 2 * D), F32),
        pltpu.VMEM((16, FF), F32),
        pltpu.VMEM((16, D), F32),
        pltpu.VMEM((88, D), F32),
    ]
    return pl.pallas_call(
        functools.partial(compute_kernel, plan),
        out_shape=(
            jax.ShapeDtypeStruct(tokens.shape, BF16),
            jax.ShapeDtypeStruct(tokens.shape, BF16),
            jax.ShapeDtypeStruct(blobs.shape, BF16),
        ),
        in_specs=[hbm] * 2 + [vm] * 3,
        out_specs=(hbm, hbm, vm),
        scratch_shapes=scratch,
        compiler_params=pltpu.CompilerParams(vmem_limit_bytes=63 * 1024 * 1024),
    )(tokens, cots, crops, sel, blobs)


NAMES = ("query", "pairs", "reduce", "output", "expand", "shrink")
TURNED = ("query", "reduce", "output", "shrink")
MESH = pl.DeviceIdType.MESH


class Place:
    def __init__(self, plan):
        self.plan = plan
        dp, fsdp = lax.axis_index("dp"), lax.axis_index("fsdp")
        self.core, self.y = lax.rem(dp, plan.cores), lax.div(dp, plan.cores)
        self.x, self.z = lax.rem(fsdp, plan.xs), lax.div(fsdp, plan.xs)
        self.dp, self.fsdp = dp, fsdp

    def device(self, core=0, y=0, x=0, z=0):
        plan = self.plan
        core = lax.rem(self.core + core, plan.cores)
        y, x = lax.rem(self.y + y, plan.ys), lax.rem(self.x + x, plan.xs)
        z = lax.rem(self.z + z, plan.zs)
        return {"dp": y * plan.cores + core, "fsdp": z * plan.xs + x}

    def block(self, core=0, y=0, x=0):
        plan = self.plan
        core = lax.rem(self.core + core, plan.cores)
        return pl.multiple_of((core * plan.ys * plan.xs + self.within(y, x)) * plan.zs * plan.rows, 16)

    def within(self, y=0, x=0):
        plan = self.plan
        return lax.rem(self.y + y, plan.ys) * plan.xs + lax.rem(self.x + x, plan.xs)

    def blob(self, z=0):
        plan = self.plan
        return pl.multiple_of(lax.rem(self.z + z, plan.zs) * plan.rows, 16)

    def partners(self):
        plan = self.plan
        return (
            [self.device(z=k) for k in range(1, plan.zs)]
            + [self.device(x=k) for k in range(1, plan.xs)]
            + [self.device(y=k) for k in range(1, plan.ys)]
            + [self.device(core=k) for k in range(1, plan.cores)]
        )


def greet(devices):
    barrier = pltpu.get_barrier_semaphore()
    for device in devices:
        pl.semaphore_signal(barrier, inc=1, device_id=device, device_id_type=MESH)
    pl.semaphore_wait(barrier, len(devices))


class Copies:
    def __init__(self, send, receive):
        self.send, self.receive, self.all = send, receive, []

    def start(self, source, target, device):
        number = len(self.all)
        copy = pltpu.make_async_remote_copy(
            src_ref=source,
            dst_ref=target,
            send_sem=self.send.at[number],
            recv_sem=self.receive.at[number],
            device_id=device,
            device_id_type=MESH,
        )
        copy.start()
        self.all.append(copy)
        return copy

    def finish(self):
        for copy in self.all:
            copy.wait_send()


def gather_count(plan):
    xs, ys, cores = plan.xs - 1, plan.ys - 1, plan.cores - 1
    return plan.zs - 1 + xs + ys + 2 * xs * ys + cores * (1 + xs + ys + 2 * xs * ys)


def gather_kernel(plan, *refs):
    pieces, (out, tile_s, send, receive) = refs[: len(PIECES)], refs[len(PIECES) :]
    me = Place(plan)
    copies = Copies(send, receive)
    source = {piece[0]: ref for piece, ref in zip(PIECES, pieces)}
    tile_s[...] = jnp.zeros_like(tile_s)
    for name, tile, at, tall, wide, row, col in plan.chunks:
        tile_s[16 * tile : 16 * tile + tall, at : at + wide] = source[name][
            row : row + tall, col : col + wide
        ]
    own = out.at[pl.ds(pl.multiple_of(me.block() + me.blob(), 16), plan.rows)]
    own[...] = tile_s[...].astype(BF16)
    greet(me.partners())
    group = plan.zs * plan.rows
    half = group // 2

    def part(y=0, x=0, second=None):
        start = me.block(y=y, x=x)
        if second is None:
            return out.at[pl.ds(start, group)]
        return out.at[pl.ds(pl.multiple_of(start + (half if second else 0), 16), half)]

    def pass_on(ref, device):
        return copies.start(ref, ref, device)

    def to_cores(ref):
        return [pass_on(ref, me.device(core=k)) for k in range(1, plan.cores)]

    waits = []
    for copy in [pass_on(own, me.device(z=k)) for k in range(1, plan.zs)]:
        copy.wait_recv()
    along_x = {k: pass_on(part(), me.device(x=k)) for k in range(1, plan.xs)}
    along_y = {k: pass_on(part(), me.device(y=k)) for k in range(1, plan.ys)}
    waits += to_cores(part())
    first, second = {}, {}
    for kx, copy in along_x.items():
        copy.wait_recv()
        for ky in range(1, plan.ys):
            first[ky, kx] = pass_on(part(x=plan.xs - kx, second=False), me.device(y=ky))
        waits += to_cores(part(x=plan.xs - kx))
    for ky, copy in along_y.items():
        copy.wait_recv()
        for kx in range(1, plan.xs):
            second[ky, kx] = pass_on(part(y=plan.ys - ky, second=True), me.device(x=kx))
        waits += to_cores(part(y=plan.ys - ky))
    for number, table in enumerate((first, second)):
        for (ky, kx), copy in table.items():
            copy.wait_recv()
            waits += to_cores(part(y=plan.ys - ky, x=plan.xs - kx, second=bool(number)))
    for copy in waits:
        copy.wait_recv()
    copies.finish()


def gather(plan, shards):
    vm = pl.BlockSpec(memory_space=pltpu.VMEM)
    count = gather_count(plan)
    return pl.pallas_call(
        functools.partial(gather_kernel, plan),
        out_shape=jax.ShapeDtypeStruct((plan.devices * plan.rows, D), BF16),
        in_specs=[vm] * len(PIECES),
        out_specs=vm,
        scratch_shapes=[
            pltpu.VMEM((plan.rows, D), F32),
            pltpu.SemaphoreType.DMA((count,)),
            pltpu.SemaphoreType.DMA((count,)),
        ],
        compiler_params=pltpu.CompilerParams(
            collective_id=1, has_side_effects=True, vmem_limit_bytes=40 * 1024 * 1024
        ),
    )(*(shards[piece[0]] for piece in PIECES))


class Vectors:
    def __init__(self, plan, rows):
        self.chunks, used = [], []
        for name in NAMES:
            height, width = plan.shard[name]
            length = width if (name in TURNED) == rows else height
            for start in range(0, length, D):
                size = min(D, length - start)
                for row, taken in enumerate(used):
                    if taken + size <= D:
                        break
                else:
                    row = len(used)
                    used.append(0)
                self.chunks.append((name, row, used[row], size, start))
                used[row] += size
        self.rows = -(-len(used) // 8) * 8

    def of(self, name):
        return [chunk[1:] for chunk in self.chunks if chunk[0] == name]

    def put(self, ref, name, vector, offset=0):
        lanes = vector.shape[0] == 1
        for row, at, size, start in self.of(name):
            if lanes:
                line = vector[:, start : start + size]
            else:
                here = turn_spot(vector.shape[0], at)
                line = jnp.sum(jnp.where(here, vector, 0.0), axis=0, keepdims=True)
                line = line[:, at : at + size]
            ref[offset + row : offset + row + 1, at : at + size] = line

    def get_lanes(self, value, name):
        parts = [value[row : row + 1, at : at + size] for row, at, size, _ in self.of(name)]
        return parts[0] if len(parts) == 1 else jnp.concatenate(parts, axis=1)

    def get_column(self, value, name):
        ((row, at, size, _),) = self.of(name)
        here = turn_spot(size, at)
        return jnp.sum(jnp.where(here, value[row : row + 1, :], 0.0), axis=1, keepdims=True)


def turn_spot(size, at):
    lanes = lax.broadcasted_iota(jnp.int32, (size, D), 1)
    return lanes == lax.broadcasted_iota(jnp.int32, (size, D), 0) + at


def reduce_count(plan):
    xs, ys = plan.xs - 1, plan.ys - 1
    swap = plan.ys * plan.xs * (plan.cores - 1)
    return swap + 2 * xs * ys + xs + ys + plan.zs - 1 + 2 * (plan.dp - 1) + 2 * (plan.fsdp - 1)


def reduce_kernel(plan, *refs):
    gblob = refs[0]
    rowvars, colvars = refs[1:7], refs[7:13]
    second_wide, second_narrow = refs[13:15]
    outs = dict(zip([piece[0] for piece in PIECES], refs[15:23]))
    row_out, col_out, wide_out, narrow_out = refs[23:27]
    (
        swap_s,
        sum_s,
        first_s,
        second_s,
        along_x_s,
        along_y_s,
        own_s,
        away_s,
        along_z_s,
        grad_s,
        rows_s,
        cols_s,
        part_s,
        norm_s,
        old_s,
        send,
        receive,
    ) = refs[27:]
    me = Place(plan)
    copies = Copies(send, receive)
    group = plan.zs * plan.rows
    half = group // 2
    by_row, by_col = Vectors(plan, True), Vectors(plan, False)
    dp_peers = [{"dp": lax.rem(me.dp + k, plan.dp), "fsdp": me.fsdp} for k in range(1, plan.dp)]
    fsdp_peers = [{"dp": me.dp, "fsdp": lax.rem(me.fsdp + k, plan.fsdp)} for k in range(1, plan.fsdp)]
    greet(dp_peers + fsdp_peers)

    def spot(y, x):
        return pl.ds(pl.multiple_of(me.within(y, x) * group, 16), group)

    spots = sorted(((y, x) for y in range(plan.ys) for x in range(plan.xs)), key=lambda s: -(s[0] > 0) - (s[1] > 0))
    swaps = {}
    for y, x in spots:
        for k in range(1, plan.cores):
            source = gblob.at[pl.ds(me.block(core=k, y=y, x=x), group)]
            swaps[y, x] = copies.start(source, swap_s.at[spot(y, x)], me.device(core=k))

    def chip_sum(y, x):
        total = gblob[pl.ds(me.block(y=y, x=x), group), :].astype(F32)
        if (y, x) in swaps:
            swaps[y, x].wait_recv()
            total = total + swap_s[spot(y, x), :].astype(F32)
        return total

    pairs = [(y, x) for y in range(1, plan.ys) for x in range(1, plan.xs)]
    first, second = {}, {}
    for number, (y, x) in enumerate(pairs):
        here = spot(y, x)
        sum_s[here, :] = chip_sum(y, x).astype(BF16)
        base = me.within(y, x) * group
        low = sum_s.at[pl.ds(pl.multiple_of(base, 16), half)]
        high = sum_s.at[pl.ds(pl.multiple_of(base + half, 16), half)]
        first[y, x] = copies.start(low, first_s.at[number], me.device(y=y))
        second[y, x] = copies.start(high, second_s.at[number], me.device(x=x))
    along_x, along_y = {}, {}
    for x in range(1, plan.xs):
        own_s[...] = chip_sum(0, x)
        for number, (py, px) in enumerate(pairs):
            if px == x:
                first[py, px].wait_recv()
                own_s[:half, :] += first_s[number].astype(F32)
        sum_s[spot(0, x), :] = own_s[...].astype(BF16)
        along_x[x] = copies.start(sum_s.at[spot(0, x)], along_x_s.at[x - 1], me.device(x=x))
    for y in range(1, plan.ys):
        own_s[...] = chip_sum(y, 0)
        for number, (py, px) in enumerate(pairs):
            if py == y:
                second[py, px].wait_recv()
                own_s[half:, :] += second_s[number].astype(F32)
        sum_s[spot(y, 0), :] = own_s[...].astype(BF16)
        along_y[y] = copies.start(sum_s.at[spot(y, 0)], along_y_s.at[y - 1], me.device(y=y))
    own_s[...] = chip_sum(0, 0)
    for x, copy in along_x.items():
        copy.wait_recv()
        own_s[...] += along_x_s[x - 1].astype(F32)
    for y, copy in along_y.items():
        copy.wait_recv()
        own_s[...] += along_y_s[y - 1].astype(F32)

    away_s[...] = own_s[...].astype(BF16)
    along_z = [
        copies.start(away_s.at[pl.ds(me.blob(k), plan.rows)], along_z_s.at[k - 1], me.device(z=k))
        for k in range(1, plan.zs)
    ]
    total = own_s[pl.ds(me.blob(), plan.rows), :]
    for k, copy in enumerate(along_z):
        copy.wait_recv()
        total = total + along_z_s[k].astype(F32)
    grad_s[...] = total
    grads = {}
    for name, (height, width) in plan.shard.items():
        lines = {}
        for owner, tile, at, tall, wide, row, col in plan.chunks:
            if owner == name:
                lines.setdefault(row, []).append(
                    grad_s[16 * tile : 16 * tile + tall, at : at + wide]
                )
        lines = [parts[0] if len(parts) == 1 else jnp.concatenate(parts, axis=1) for parts in lines.values()]
        grads[name] = lines[0] if len(lines) == 1 else jnp.concatenate(lines, axis=0)

    decay_two = 1.0 - STEP ** (-0.8)

    def exchange(buffer, mine, peers):
        started = [copies.start(buffer.at[mine], buffer.at[mine], peer) for peer in peers]
        return started

    def gathered(buffer, started):
        for copy in started:
            copy.wait_recv()
        total = buffer[0]
        for number in range(1, buffer.shape[0]):
            total = total + buffer[number]
        return total

    full = {}
    own_rows, own_cols = rows_s.at[me.fsdp], cols_s.at[me.dp]
    own_rows[...] = jnp.zeros(own_rows.shape, F32)
    own_cols[...] = jnp.zeros(own_cols.shape, F32)
    for name in NAMES:
        height, width = plan.shard[name]
        square = grads[name] * grads[name] + SQUARE_EPS
        over_rows = jnp.sum(square, axis=0, keepdims=True)
        over_cols = jnp.sum(square, axis=1, keepdims=True)
        if name in TURNED:
            full[name] = (width * plan.dp, height * plan.fsdp)
            row_part, col_part = over_rows, over_cols
        else:
            full[name] = (height * plan.dp, width * plan.fsdp)
            row_part, col_part = over_cols, over_rows
        by_row.put(own_rows, name, row_part * ((1.0 - decay_two) / full[name][1]))
        by_col.put(own_cols, name, col_part * ((1.0 - decay_two) / full[name][0]))
    height, width = plan.shard["narrow"]
    own_cols[by_col.rows : by_col.rows + height, 0:width] = grads["narrow"]
    row_copies = exchange(rows_s, me.fsdp, fsdp_peers)
    col_copies = exchange(cols_s, me.dp, dp_peers)
    old_s[...] = jnp.zeros_like(old_s)
    for name, ref in zip(NAMES, rowvars):
        by_row.put(old_s, name, ref[...].reshape(1, ref.shape[0]))
    for name, ref in zip(NAMES, colvars):
        by_col.put(old_s, name, ref[...].reshape(1, ref.shape[0]), by_row.rows)
    wide = grads["wide"]
    wide_second = decay_two * second_wide[...] + (1.0 - decay_two) * (wide * wide + SQUARE_EPS)
    wide_out[...] = wide_second
    wide_update = wide * lax.rsqrt(wide_second)
    row_new = decay_two * old_s[: by_row.rows, :] + gathered(rows_s, row_copies)
    row_out[...] = row_new
    all_cols = gathered(cols_s, col_copies)[: by_col.rows, :]
    col_new = decay_two * old_s[by_row.rows :, :] + all_cols
    col_out[...] = col_new
    narrow = cols_s[0, by_col.rows : by_col.rows + height, 0:width]
    narrow_second = decay_two * second_narrow[...] + (1.0 - decay_two) * (narrow * narrow + SQUARE_EPS)
    narrow_out[...] = narrow_second
    narrow_update = narrow * lax.rsqrt(narrow_second)

    lane = lax.broadcasted_iota(jnp.int32, (16, D), 1)
    count = len(NAMES)

    def whole_sum(values):
        return jnp.sum(jnp.sum(values, axis=1, keepdims=True), axis=0, keepdims=True)

    def row_norm(values):
        norm = jnp.sum(values * values, axis=1, keepdims=True)
        return jnp.concatenate([norm, jnp.zeros((16 - norm.shape[0], 1), F32)], axis=0)

    updates = {}
    part = jnp.where(lane == 2 * count, row_norm(wide_update), 0.0)
    for number, name in enumerate(NAMES):
        lanes = by_row.get_lanes(row_new, name)
        if name in TURNED:
            row_scale = lax.rsqrt(lanes)
            col_scale = lax.rsqrt(by_col.get_column(col_new, name))
        else:
            row_scale = lax.rsqrt(by_row.get_column(row_new, name))
            col_scale = lax.rsqrt(by_col.get_lanes(col_new, name))
        update = grads[name] * row_scale * col_scale
        updates[name] = update
        part = jnp.where(lane == number, whole_sum(update * update), part)
        part = jnp.where(lane == count + number, whole_sum(lanes), part)
    part_s[me.dp] = part
    sums = gathered(part_s, exchange(part_s, me.dp, dp_peers))
    norm_s[me.fsdp] = jnp.where(lane == 2 * count + 1, row_norm(narrow_update), sums)
    norms = gathered(norm_s, exchange(norm_s, me.fsdp, fsdp_peers))
    for number, name in enumerate(NAMES):
        mean = sums[0:1, count + number : count + number + 1] / full[name][0]
        norm = norms[0:1, number : number + 1] / (full[name][0] * full[name][1])
        clip = jnp.maximum(1.0, jnp.sqrt(mean * norm) / CLIP_RMS)
        outs[name][...] = updates[name] * (jnp.sqrt(mean) / clip)
    for number, name, update in ((0, "wide", wide_update), (1, "narrow", narrow_update)):
        size = FF if name == "wide" else D
        norm = norms[: update.shape[0], 2 * count + number : 2 * count + number + 1] / size
        outs[name][...] = update / jnp.maximum(1.0, jnp.sqrt(norm) / CLIP_RMS)
    copies.finish()


def reduce_all(plan, gblobs, rowvars, colvars, second_wide, second_narrow):
    vm = pl.BlockSpec(memory_space=pltpu.VMEM)
    count = reduce_count(plan)
    by_row, by_col = Vectors(plan, True), Vectors(plan, False)
    group = plan.zs * plan.rows
    mine = plan.ys * plan.xs * group
    pairs = max(1, (plan.ys - 1) * (plan.xs - 1))
    thin = by_col.rows + 16
    out_shape = [jax.ShapeDtypeStruct(plan.shard[piece[0]], F32) for piece in PIECES]
    out_shape += [jax.ShapeDtypeStruct((by_row.rows, D), F32), jax.ShapeDtypeStruct((by_col.rows, D), F32)]
    out_shape += [jax.ShapeDtypeStruct(plan.shard[name], F32) for name in ("wide", "narrow")]
    return pl.pallas_call(
        functools.partial(reduce_kernel, plan),
        out_shape=out_shape,
        in_specs=[vm] * 15,
        out_specs=[vm] * 12,
        scratch_shapes=[
            pltpu.VMEM((mine, D), BF16),
            pltpu.VMEM((mine, D), BF16),
            pltpu.VMEM((pairs, group // 2, D), BF16),
            pltpu.VMEM((pairs, group // 2, D), BF16),
            pltpu.VMEM((max(1, plan.xs - 1), group, D), BF16),
            pltpu.VMEM((max(1, plan.ys - 1), group, D), BF16),
            pltpu.VMEM((group, D), F32),
            pltpu.VMEM((group, D), BF16),
            pltpu.VMEM((max(1, plan.zs - 1), plan.rows, D), BF16),
            pltpu.VMEM((plan.rows, D), F32),
            pltpu.VMEM((plan.fsdp, by_row.rows, D), F32),
            pltpu.VMEM((plan.dp, thin, D), F32),
            pltpu.VMEM((plan.dp, 16, D), F32),
            pltpu.VMEM((plan.fsdp, 16, D), F32),
            pltpu.VMEM((by_row.rows + by_col.rows, D), F32),
            pltpu.SemaphoreType.DMA((count,)),
            pltpu.SemaphoreType.DMA((count,)),
        ],
        compiler_params=pltpu.CompilerParams(
            collective_id=2, has_side_effects=True, vmem_limit_bytes=60 * 1024 * 1024
        ),
    )(gblobs, *rowvars, *colvars, second_wide, second_narrow)


def update_kernel(plan, *refs):
    order = [piece[0] for piece in PIECES]
    updates, moments, weights = (dict(zip(order, refs[8 * n : 8 * n + 8])) for n in range(3))
    row_new, col_new, second_wide, second_narrow = refs[24:28]
    new_moments, new_weights = (dict(zip(order, refs[8 * n + 28 : 8 * n + 36])) for n in range(2))
    row_outs, col_outs, wide_out, narrow_out = refs[44:50], refs[50:56], refs[56], refs[57]
    for name in order:
        moment = BETA_ONE * moments[name][...] + (1.0 - BETA_ONE) * updates[name][...]
        new_moments[name][...] = moment
        new_weights[name][...] = weights[name][...] * (1.0 - RATE * DECAY_RATE) - RATE * moment
    by_row, by_col = Vectors(plan, True), Vectors(plan, False)
    for vectors, source, targets in ((by_row, row_new, row_outs), (by_col, col_new, col_outs)):
        for name, ref in zip(NAMES, targets):
            for row, at, size, start in vectors.of(name):
                ref[start : start + size] = source[row : row + 1, at : at + size].reshape(size)
    wide_out[...] = second_wide[...]
    narrow_out[...] = second_narrow[...]


def update_all(plan, reduced, moments, weights):
    vm = pl.BlockSpec(memory_space=pltpu.VMEM)
    order = [piece[0] for piece in PIECES]
    pieces = [jax.ShapeDtypeStruct(plan.shard[name], F32) for name in order]
    row_shapes, col_shapes = [], []
    for name in NAMES:
        height, width = plan.shard[name]
        if name in TURNED:
            height, width = width, height
        row_shapes.append(jax.ShapeDtypeStruct((height,), F32))
        col_shapes.append(jax.ShapeDtypeStruct((width,), F32))
    seconds = [jax.ShapeDtypeStruct(plan.shard[name], F32) for name in ("wide", "narrow")]
    out_shape = pieces + pieces + row_shapes + col_shapes + seconds
    found = pl.pallas_call(
        functools.partial(update_kernel, plan),
        out_shape=out_shape,
        in_specs=[vm] * 28,
        out_specs=[vm] * len(out_shape),
    )(*reduced[:8], *(moments[name] for name in order), *(weights[name] for name in order), *reduced[8:])
    next_moment, next_weight = dict(zip(order, found[:8])), dict(zip(order, found[8:16]))
    return next_moment, next_weight, found[16:22], found[22:28], found[28], found[29]


def body(plan, tokens_in, cotangent, crop_ids, *state):
    weights, moments, rowvars, colvars = {}, {}, [], []
    for number, name in enumerate(NAMES):
        weights[name], moments[name], row, col = state[4 * number : 4 * number + 4]
        rowvars.append(row)
        colvars.append(col)
    weights["narrow"], moments["narrow"], second_narrow = state[24:27]
    weights["wide"], moments["wide"], second_wide = state[27:30]

    def turned(values):
        return {name: value.T if name in TURNED else value for name, value in values.items()}

    weights, moments = turned(weights), turned(moments)
    micro, local, length, width = tokens_in.shape
    flat = (micro * local, length, width)
    blobs = gather(plan, weights)
    result, input_grad, gblobs = compute(
        plan, tokens_in.reshape(flat), cotangent.reshape(flat), crop_ids, blobs
    )
    reduced = reduce_all(plan, gblobs, rowvars, colvars, second_wide, second_narrow)
    next_moment, next_weight, row_new, col_new, wide_new, narrow_new = update_all(
        plan, reduced, moments, weights
    )
    next_moment, next_weight = turned(next_moment), turned(next_weight)
    results = [result.reshape(tokens_in.shape), input_grad.reshape(tokens_in.shape)]
    for number, name in enumerate(NAMES):
        results += [next_moment[name], row_new[number], col_new[number], next_weight[name]]
    for name, second in (("narrow", narrow_new), ("wide", wide_new)):
        results += [next_moment[name], second, next_weight[name]]
    return tuple(results)


def solution(mesh):
    plan = Plan(mesh.shape["dp"], mesh.shape["fsdp"])
    tokens = P(None, ("dp", "fsdp"), None, None)
    matrix = P("dp", "fsdp")
    by_rows, by_cols = P("dp"), P("fsdp")
    thin, broad = P(None, "fsdp"), P(None, ("dp", "fsdp"))
    state = (matrix, matrix, by_rows, by_cols) * 6 + (thin,) * 3 + (broad,) * 3
    in_specs = (tokens, tokens, P(None, ("dp", "fsdp"), None)) + state
    moved = (matrix, by_rows, by_cols, matrix) * 6 + (thin,) * 3 + (broad,) * 3
    return jax.shard_map(
        functools.partial(body, plan),
        mesh=mesh,
        in_specs=in_specs,
        out_specs=(tokens, tokens) + moved,
        check_vma=False,
    )
```

```python
import functools
import numpy as np
import jax
import jax.numpy as jnp
from jax import lax
from jax.experimental import pallas as pl
from jax.experimental.pallas import tpu as pltpu
from jax.sharding import PartitionSpec as P

HEADS = 2
GRID = 28
STEP = 10
NORM_EPS = 1e-06
SQUARE_EPS = 1e-30
CLIP_RMS = 1.0
BETA_ONE = 0.9
RATE = 1.0
DECAY_RATE = 0.01
MASKED = -1e30

D = 128
FF = 1024
SIDE = 4
BLOCKS = GRID // SIDE
KEYS = BLOCKS * BLOCKS
PAD_KEYS = KEYS + 1
GROUPS = SIDE * SIDE
TAPS = 9
MARGIN = 64
CHUNK = 256
PARTS = FF // CHUNK
HALF = PAD_KEYS // 2
REACH = BLOCKS + 1
RUN = 5

F32 = jnp.float32
BF16 = jnp.bfloat16

PIECES = (
    ("reduce", (D, GROUPS * D), "f", "d"),
    ("shrink", (D, FF), "f", "d"),
    ("expand", (D, FF), "d", "f"),
    ("query", (D, D), "f", "d"),
    ("output", (D, D), "f", "d"),
    ("pairs", (D, 2 * D), "d", "f"),
    ("wide", (11, FF), "", "df"),
    ("narrow", (11, D), "", "f"),
)


class Plan:
    def __init__(self, dp, fsdp):
        self.dp, self.fsdp = dp, fsdp
        cuts = {"": 1, "d": dp, "f": fsdp, "df": dp * fsdp}
        self.shard = {}
        self.chunks = []
        free = []
        for name, (rows, cols), by_rows, by_cols in PIECES:
            height, width = rows // cuts[by_rows], cols // cuts[by_cols]
            self.shard[name] = (height, width)
            for row in range(0, height, 16):
                for col in range(0, width, D):
                    tall, wide = min(16, height - row), min(D, width - col)
                    for tile, used in enumerate(free):
                        if used + wide <= D:
                            break
                    else:
                        tile = len(free)
                        free.append(0)
                    self.chunks.append((name, tile, free[tile], tall, wide, row, col))
                    free[tile] += wide
        self.tiles = len(free)
        self.rows = 16 * self.tiles
        self.devices = dp * fsdp
        self.cores = 2 if dp % 2 == 0 else 1
        self.ys = dp // self.cores
        self.xs = 1
        while self.xs * self.xs * 4 <= fsdp and fsdp % (2 * self.xs) == 0:
            self.xs *= 2
        self.zs = fsdp // self.xs

    def base(self, d, f):
        y, core = divmod(d, self.cores)
        z, x = divmod(f, self.xs)
        return (((core * self.ys + y) * self.xs + x) * self.zs + z) * self.rows

    def origin(self, name, d, f):
        _, _, by_rows, by_cols = next(piece for piece in PIECES if piece[0] == name)
        at = {"": 0, "d": d, "f": f, "df": d * self.fsdp + f}
        height, width = self.shard[name]
        return at[by_rows] * height, at[by_cols] * width


def nn(left, right):
    return lax.dot_general(left, right, (((1,), (0,)), ((), ())), preferred_element_type=F32)


def nt(left, right):
    return lax.dot_general(left, right, (((1,), (1,)), ((), ())), preferred_element_type=F32)


def tn(left, right):
    return lax.dot_general(left, right, (((0,), (0,)), ((), ())), preferred_element_type=F32)


def fold(values):
    rows, cols = values.shape
    return jnp.sum(values.reshape(rows // 8, 8, cols), axis=0)


def normalize(values):
    center = values - jnp.mean(values, axis=-1, keepdims=True)
    scale = lax.rsqrt(jnp.mean(center * center, axis=-1, keepdims=True) + NORM_EPS)
    return center * scale, scale


def normalize_back(unit, scale, incoming, gain):
    c = incoming * gain
    mean_c = jnp.mean(c, axis=-1, keepdims=True)
    mean_cz = jnp.mean(c * unit, axis=-1, keepdims=True)
    return (c - mean_c - unit * mean_cz) * scale


def gelu_parts(v):
    share = 0.5 + 0.5 * lax.erf(v * 0.5**0.5)
    bell = jnp.exp2(v * v * (-0.5 * 1.4426950408889634))
    return v * share, share + (v * 0.3989422804014327) * bell


def direction(step_at):
    return -1 if step_at < 0 else (1 if step_at >= SIDE else 0)


def at_position(position):
    return position // 2 + HALF * (position % 2)


def compute_kernel(
    plan,
    x_ref,
    dy_ref,
    crop_ref,
    blob_ref,
    out_ref,
    gin_ref,
    gblob_ref,
    stage,
    passing,
    arrived,
    held,
    mixed_s,
    inputs_s,
    dy_s,
    normed_s,
    query_s,
    attn_s,
    probs_s,
    key_s,
    value_s,
    dkey_s,
    dvalue_s,
    dred_s,
    second_s,
    back_s,
    crop_s,
    mask_s,
    keycrop_s,
    taps_s,
    dtaps_s,
    w_reduce,
    w_shrink,
    w_expand,
    w_query,
    w_output,
    w_pairs,
    w_wide,
    w_narrow,
    lo_reduce,
    lo_shrink,
    lo_expand,
    lo_query,
    lo_output,
    lo_pairs,
    g_reduce,
    g_shrink,
    g_expand,
    g_query,
    g_output,
    g_pairs,
    g_wide,
    g_narrow,
    sums,
):
    canvases = x_ref.shape[0]
    pair = 2 * canvases
    rows = PAD_KEYS * canvases
    slab = GROUPS * pair
    run = RUN * slab
    lane = lax.broadcasted_iota(jnp.int32, (1, D), 1)
    low_half = lane < D // 2
    full = {
        "reduce": w_reduce,
        "shrink": w_shrink,
        "expand": w_expand,
        "query": w_query,
        "output": w_output,
        "pairs": w_pairs,
        "wide": w_wide,
        "narrow": w_narrow,
    }
    def assemble(blobs, landed):
        copy = pltpu.make_async_copy(blob_ref, blobs, landed)
        copy.start()
        copy.wait()
        for d in range(plan.dp):
            for f in range(plan.fsdp):
                base = plan.base(d, f)
                for name, tile, at, tall, wide, row, col in plan.chunks:
                    if name == "narrow" and d:
                        continue
                    r0, c0 = plan.origin(name, d, f)
                    tile_rows = blobs[base + 16 * tile : base + 16 * tile + 16, :].astype(F32)
                    full[name][r0 + row : r0 + row + tall, c0 + col : c0 + col + wide] = tile_rows[
                        :tall, at : at + wide
                    ]

    pl.run_scoped(assemble, pltpu.VMEM(blob_ref.shape, BF16), pltpu.SemaphoreType.DMA)
    lo_reduce[...] = w_reduce[...].astype(BF16)
    lo_query[...] = w_query[...].astype(BF16)
    lo_output[...] = w_output[...].astype(BF16)
    lo_pairs[...] = w_pairs[...].astype(BF16)
    for part in range(PARTS):
        cols = slice(part * CHUNK, (part + 1) * CHUNK)
        lo_shrink[part] = w_shrink[:, cols].astype(BF16)
        lo_expand[part] = w_expand[:, cols].astype(BF16)
        for tap in range(TAPS + 2):
            taps_s[part, tap] = jnp.broadcast_to(w_wide[tap : tap + 1, cols], (pair, CHUNK)).astype(BF16)

    def narrow(row):
        return w_narrow[row : row + 1, :]

    sums[...] = jnp.zeros_like(sums)
    held[...] = jnp.zeros_like(held)
    back_s[...] = jnp.zeros_like(back_s)
    dtaps_s[...] = jnp.zeros_like(dtaps_s)
    for ref in (g_shrink, g_expand, g_query, g_output, g_narrow, g_wide):
        ref[...] = jnp.zeros_like(ref)
    for ref in (key_s, value_s):
        ref[rows:, :] = jnp.zeros((ref.shape[0] - rows, D), F32)

    def add(row, values):
        sums[8 * row : 8 * row + 8, :] += fold(values)

    def run_rows(m):
        return pl.ds(pl.multiple_of(m * run, 16), run)

    def places():
        for g in range(GROUPS):
            for block_row in range(BLOCKS):
                first = block_row * BLOCKS
                for half in range(2):
                    start, stop = max(first, HALF * half), min(first + BLOCKS, HALF * (half + 1))
                    if start < stop:
                        column = start - first
                        token = (block_row * SIDE + g // SIDE) * GRID + column * SIDE + g % SIDE
                        place = (start - HALF * half) * slab + g * pair + half * canvases
                        yield token, place, stop - start

    def scatter(source):
        def fetch(c):
            slot = lax.rem(c, 2)
            return pltpu.make_async_copy(source.at[c], passing.at[slot], arrived.at[slot])

        fetch(0).start()

        def one(c, _):
            @pl.when(c + 1 < canvases)
            def _():
                fetch(c + 1).start()

            fetch(c).wait()
            stage[...] = passing[lax.rem(c, 2)].astype(F32)
            for token, place, count in places():
                held[pl.ds(place + c, count, stride=slab), :] = stage[
                    pl.ds(token, count, stride=SIDE), :
                ]
            return 0

        lax.fori_loop(0, canvases, one, 0)

    def collect(target):
        def leave(c):
            slot = lax.rem(c, 2)
            return pltpu.make_async_copy(passing.at[slot], target.at[c], arrived.at[slot])

        def one(c, _):
            for token, place, count in places():
                stage[pl.ds(token, count, stride=SIDE), :] = held[
                    pl.ds(place + c, count, stride=slab), :
                ]

            @pl.when(c >= 2)
            def _():
                leave(c - 2).wait()

            passing[lax.rem(c, 2)] = stage[...].astype(BF16)
            leave(c).start()
            return 0

        lax.fori_loop(0, canvases, one, 0)
        for c in range(max(0, canvases - 2), canvases):
            leave(c).wait()

    token = lax.broadcasted_iota(jnp.int32, (GRID * GRID, D), 0)
    key_lane = lax.rem(lax.broadcasted_iota(jnp.int32, (GRID * GRID, D), 1), D // 2)
    crops = jnp.concatenate([crop_ref[m] for m in range(crop_ref.shape[0])], axis=0)
    crops = crops.astype(F32).astype(BF16)

    def crops_of(block):
        corner = lax.div(block, BLOCKS) * (SIDE * GRID) + lax.rem(block, BLOCKS) * SIDE
        return nn(crops, jnp.where((corner == token) & (block < KEYS), 1.0, 0.0).astype(BF16))

    position = lax.rem(lane, D // 2)
    keycrop = crops_of(lax.div(key_lane, 2) + HALF * lax.rem(key_lane, 2))
    keycrop = jnp.where((position < PAD_KEYS) & (position != 2 * HALF - 1), keycrop, -2.0)
    keycrop_s[...] = keycrop.reshape(keycrop_s.shape)
    by_block = jnp.concatenate([crops_of(key_lane), jnp.zeros((D - canvases, D), F32)], axis=0).T
    crop_s[...] = jnp.full(crop_s.shape, -1.0, F32)
    for c in range(canvases):
        crop_s[pl.ds(MARGIN + c, KEYS, stride=canvases), :] = jnp.broadcast_to(
            by_block[:KEYS, c : c + 1], (KEYS, D)
        )

    def by_position(values):
        order = [at_position(number) * canvases for number in range(PAD_KEYS)]
        return jnp.concatenate([values[start : start + canvases, :] for start in order], axis=0)

    own_crop = crop_s[MARGIN : MARGIN + rows, :]
    block = lax.div(lax.broadcasted_iota(jnp.int32, (rows, D), 0), canvases)
    block_i, block_j = lax.div(block, BLOCKS), lax.rem(block, BLOCKS)
    for di in (-1, 0, 1):
        for dj in (-1, 0, 1):
            start = MARGIN + (di * BLOCKS + dj) * canvases
            inside = (block < KEYS) & (block_i + di >= 0) & (block_i + di < BLOCKS)
            inside = inside & (block_j + dj >= 0) & (block_j + dj < BLOCKS)
            near = crop_s[start : start + rows, :] == own_crop
            mask = by_position(jnp.where(near & inside, 1.0, 0.0)).astype(BF16)
            for at in range(0, CHUNK, D):
                mask_s[(di + 1) * 3 + dj + 1, :, at : at + D] = mask
    row_crops = by_position(own_crop)
    for k in range(HALF):
        piece = row_crops[k * pair : (k + 1) * pair, :]
        back_s[k * slab : (k + 1) * slab, :] = jnp.concatenate([piece] * GROUPS, axis=0)

    scatter(dy_ref)

    def keep_dy(m, _):
        dy_s[run_rows(m), :] = held[run_rows(m), :].astype(BF16)
        return 0

    lax.fori_loop(0, HALF // RUN, keep_dy, 0)
    scatter(x_ref)

    def pair_rows(m, k):
        return pl.ds(pl.multiple_of((m * RUN + k) * pair, 16), pair)

    def first(m, _):
        values = held[run_rows(m), :]
        mixed_s[run_rows(m), :] = values
        inputs_s[run_rows(m), :] = values.astype(BF16)
        unit, _ = normalize(values)
        low = (unit * narrow(0) + narrow(1)).astype(BF16)
        for k in range(RUN):
            for g in range(GROUPS):
                start = k * slab + g * pair
                normed_s[pair_rows(m, k), g * D : (g + 1) * D] = low[start : start + pair, :]
        query_s[run_rows(m), :] = (nt(low, lo_query[...]) + narrow(2)).astype(BF16).astype(F32)
        return 0

    lax.fori_loop(0, HALF // RUN, first, 0)

    reduced = nt(normed_s[...], lo_reduce[...]) + narrow(4)
    reduced_unit, reduced_scale = normalize(reduced)
    reduced_low = (reduced_unit * narrow(5) + narrow(6)).astype(BF16)
    pairs = nn(reduced_low, lo_pairs[...])
    key_s[:rows, :] = pairs[:, :D].astype(BF16).astype(F32)
    value_s[:rows, :] = (pairs[:, D:] + narrow(3)).astype(BF16).astype(F32)

    def split_heads(values):
        return jnp.concatenate(
            [jnp.where(low_half, values, 0.0), jnp.where(low_half, 0.0, values)], axis=0
        ).astype(BF16)

    def join_heads(values):
        return jnp.where(low_half, values[: D // 2, :], values[D // 2 :, :])

    def canvas_rows(c):
        return pl.ds(c, GROUPS * PAD_KEYS, stride=canvases)

    def key_rows(c):
        return pl.ds(c, D // 2, stride=canvases)

    def per_head(values, reduce, fill):
        first_half = reduce(jnp.where(low_half, values, fill), axis=-1, keepdims=True)
        second_half = reduce(jnp.where(low_half, fill, values), axis=-1, keepdims=True)
        return jnp.where(low_half, first_half, second_half)

    def attend(c, _):
        queries = query_s[canvas_rows(c), :].astype(BF16)
        keys = split_heads(key_s[key_rows(c), :])
        values = split_heads(value_s[key_rows(c), :])
        scores = nt(queries, keys) * (D // HEADS) ** (-0.5)
        allowed = back_s[canvas_rows(c), :] == keycrop_s[c]
        scores = jnp.where(allowed, scores, MASKED)
        exponent = jnp.exp(scores - per_head(scores, jnp.max, -3e38))
        exponent = jnp.where(allowed, exponent, 0.0)
        total = jnp.maximum(per_head(exponent, jnp.sum, 0.0), 1.0)
        probs = (exponent / total).astype(BF16)
        probs_s[c] = probs
        held[canvas_rows(c), :] = nn(probs, values)
        return 0

    lax.fori_loop(0, canvases, attend, 0)

    def feed_forward(up_even, up_odd, dconv_s, act_s, dup_s):
        def slab_rows(k):
            return pl.ds(pl.multiple_of(k * slab, 16), slab)

        def keep(ref, k, values):
            ref[REACH + k] = values.astype(BF16)
            pieces = []
            for start in range(0, slab, canvases):
                other = start ^ canvases
                pieces.append(values[other : other + canvases, :])
            spare = ref.shape[0] - 1
            beyond = jnp.where(k < REACH, REACH + HALF + k, jnp.where(k >= HALF - REACH, k - (HALF - REACH), spare))
            ref[beyond] = jnp.concatenate(pieces, axis=0).astype(BF16)

        ups = [up_odd if part % 2 else up_even for part in range(PARTS)]

        def spread(part, k, values):
            up = nn(values, lo_expand[part])
            up = up.reshape(slab // pair, pair, CHUNK) + taps_s[part, TAPS].astype(F32)
            keep(ups[part], k, up.reshape(slab, CHUNK))

        def second(m, _):
            low = held[run_rows(m), :].astype(BF16)
            attn_s[run_rows(m), :] = low
            mixed = mixed_s[run_rows(m), :] + (nt(low, lo_output[...]) + narrow(7))
            mixed_s[run_rows(m), :] = mixed
            held[run_rows(m), :] = mixed + narrow(10)
            unit, _ = normalize(mixed)
            low = (unit * narrow(8) + narrow(9)).astype(BF16)
            second_s[run_rows(m), :] = low
            for k in range(RUN):
                spread(0, m * RUN + k, low[k * slab : (k + 1) * slab, :])
            back_s[run_rows(m), :] = jnp.zeros((run, D), F32)
            return 0

        lax.fori_loop(0, HALF // RUN, second, 0)

        def around(ref, k, at):
            found = []
            for bt in range(-1, SIDE + 1):
                di, dj = direction(at), direction(bt)
                group = (at % SIDE) * SIDE + bt % SIDE
                values = ref[REACH + k + di * BLOCKS + dj, group * pair : (group + 1) * pair, :]
                if di or dj:
                    values = values * mask_s[
                        (di + 1) * 3 + dj + 1, pl.ds(pl.multiple_of(k * pair, 16), pair), :
                    ]
                found.append(values)
            return found

        def contract(part, k):
            act = act_s[k]
            here = slab_rows(k)
            held[here, :] += nt(act, lo_shrink[part])
            g_shrink[part] += tn(dy_s[here, :], act)

        def contract_back(part, k):
            d_up = dup_s[k]
            here = slab_rows(k)
            back_s[here, :] += nt(d_up, lo_expand[part])
            g_expand[part] += tn(second_s[here, :], d_up)

        def convolve(ref, k, taps, finish):
            sums_of = {}
            for at in range(-1, SIDE + 1):
                near = around(ref, k, at)
                for a in range(max(0, at - 1), min(SIDE - 1, at + 1) + 1):
                    for b in range(SIDE):
                        for step in range(3):
                            term = near[b + step] * taps[(at - a + 1) * 3 + step]
                            sums_of[a, b] = sums_of[a, b] + term if (a, b) in sums_of else term
                    if at == a + 1:
                        for b in range(SIDE):
                            finish(a * SIDE + b, sums_of.pop((a, b)))

        def feed(part):
            def forward(k, _):
                if part + 1 < PARTS:
                    spread(part + 1, k, second_s[slab_rows(k), :])
                if part:
                    contract_back(part - 1, k)
                d_act = nn(dy_s[slab_rows(k), :], lo_shrink[part])
                taps = [taps_s[part, tap] for tap in range(TAPS)]
                shift = taps_s[part, TAPS + 1]
                kept = {}

                def finish(g, conv):
                    act, slope = gelu_parts((conv + shift).astype(F32))
                    act_s[k, g * pair : (g + 1) * pair, :] = act.astype(BF16)
                    kept[g] = d_act[g * pair : (g + 1) * pair, :] * slope

                convolve(ups[part], k, taps, finish)
                keep(dconv_s, k, jnp.concatenate([kept[g] for g in range(GROUPS)], axis=0))
                return 0

            lax.fori_loop(0, HALF, forward, 0)

            def backward(k, _):
                contract(part, k)
                taps = [taps_s[part, TAPS - 1 - tap] for tap in range(TAPS)]
                through = []

                def finish(g, d_up):
                    dup_s[k, g * pair : (g + 1) * pair, :] = d_up
                    through.append(d_up)

                convolve(dconv_s, k, taps, finish)
                here = {}
                products = [None] * TAPS
                for at in range(-1, SIDE + 1):
                    near = around(ups[part], k, at)
                    if at + 1 < SIDE:
                        for b in range(SIDE):
                            g = (at + 1) * SIDE + b
                            here[at + 1, b] = dconv_s[REACH + k, g * pair : (g + 1) * pair, :]
                    for a in range(max(0, at - 1), min(SIDE - 1, at + 1) + 1):
                        for b in range(SIDE):
                            for step in range(3):
                                tap = (at - a + 1) * 3 + step
                                term = near[b + step] * here[a, b]
                                products[tap] = term if products[tap] is None else products[tap] + term

                def total(terms):
                    while len(terms) > 1:
                        terms = [sum(terms[n : n + 2][1:], terms[n]) for n in range(0, len(terms), 2)]
                    return terms[0]

                for row, value in enumerate(products + [total(through), total(list(here.values()))]):
                    value = value.astype(F32)
                    dtaps_s[part, 8 * row : 8 * row + 8, :] += fold(value)
                return 0

            lax.fori_loop(0, HALF, backward, 0)

        for part in range(PARTS):
            feed(part)
        collect(out_ref)

        def third(m, _):
            cot = dy_s[run_rows(m), :]
            d_up = dup_s[pl.ds(m * RUN, RUN)].reshape(run, CHUNK)
            g_expand[PARTS - 1] += tn(second_s[run_rows(m), :], d_up)
            incoming = back_s[run_rows(m), :] + nt(d_up, lo_expand[PARTS - 1])
            unit, scale = normalize(mixed_s[run_rows(m), :])
            d_mixed = cot.astype(F32) + normalize_back(unit, scale, incoming, narrow(8))
            add(8, incoming * unit)
            add(9, incoming)
            add(10, cot.astype(F32))
            mixed_s[run_rows(m), :] = d_mixed
            low = d_mixed.astype(BF16)
            add(7, low.astype(F32))
            g_output[...] += tn(low, attn_s[run_rows(m), :])
            held[run_rows(m), :] = nn(low, lo_output[...])
            return 0

        lax.fori_loop(0, HALF // RUN, third, 0)

    far = pltpu.VMEM((HALF + 2 * REACH + 1, slab, CHUNK), BF16)
    near = pltpu.VMEM((HALF, slab, CHUNK), BF16)
    pl.run_scoped(feed_forward, far, far, far, near, near)

    def attend_back(c, _):
        queries = query_s[canvas_rows(c), :].astype(BF16)
        keys = split_heads(key_s[key_rows(c), :])
        values = split_heads(value_s[key_rows(c), :])
        probs_low = probs_s[c]
        probs = probs_low.astype(F32)
        d_attn = held[canvas_rows(c), :].astype(BF16)
        d_probs = nt(d_attn, values)
        d_scores = probs * (d_probs - per_head(d_probs * probs, jnp.sum, 0.0))
        d_scores = d_scores.astype(BF16)
        scale = (D // HEADS) ** (-0.5)
        held[canvas_rows(c), :] = nn(d_scores, keys) * scale
        dkey_s[key_rows(c), :] = join_heads(tn(d_scores, queries)) * scale
        dvalue_s[key_rows(c), :] = join_heads(tn(probs_low, d_attn))
        return 0

    lax.fori_loop(0, canvases, attend_back, 0)

    d_pairs = jnp.concatenate([dkey_s[:rows, :], dvalue_s[:rows, :]], axis=1).astype(BF16)
    g_pairs[...] = tn(reduced_low, d_pairs)
    add(3, d_pairs[:, D:].astype(F32))
    incoming = nt(d_pairs, lo_pairs[...])
    add(5, incoming * reduced_unit)
    add(6, incoming)
    d_reduced = normalize_back(reduced_unit, reduced_scale, incoming, narrow(5)).astype(BF16)
    add(4, d_reduced.astype(F32))
    dred_s[...] = d_reduced
    g_reduce[...] = tn(d_reduced, normed_s[...])

    def fourth(m, _):
        low = held[run_rows(m), :].astype(BF16)
        add(2, low.astype(F32))
        here = pl.ds(pl.multiple_of(m * RUN * pair, 16), RUN * pair)
        normed, patches = normed_s[here, :], nn(dred_s[here, :], lo_reduce[...])

        def by_token(values):
            return jnp.concatenate(
                [
                    values[k * pair : (k + 1) * pair, g * D : (g + 1) * D]
                    for k in range(RUN)
                    for g in range(GROUPS)
                ],
                axis=0,
            )

        g_query[...] += tn(low, by_token(normed))
        incoming = nn(low, lo_query[...]) + by_token(patches)
        unit, scale = normalize(inputs_s[run_rows(m), :].astype(F32))
        add(0, incoming * unit)
        add(1, incoming)
        back = normalize_back(unit, scale, incoming, narrow(0))
        held[run_rows(m), :] = mixed_s[run_rows(m), :] + back
        return 0

    lax.fori_loop(0, HALF // RUN, fourth, 0)
    collect(gin_ref)

    for row in range(11):
        g_narrow[row : row + 1, :] = jnp.sum(sums[8 * row : 8 * row + 8, :], axis=0, keepdims=True)
        for part in range(PARTS):
            g_wide[row : row + 1, part * CHUNK : (part + 1) * CHUNK] = jnp.sum(
                dtaps_s[part, 8 * row : 8 * row + 8, :], axis=0, keepdims=True
            )
    whole_shrink, whole_expand = w_shrink, w_expand
    for part in range(PARTS):
        whole_shrink[:, part * CHUNK : (part + 1) * CHUNK] = g_shrink[part]
        whole_expand[:, part * CHUNK : (part + 1) * CHUNK] = g_expand[part]
    grads = {
        "reduce": g_reduce,
        "shrink": whole_shrink,
        "expand": whole_expand,
        "query": g_query,
        "output": g_output,
        "pairs": g_pairs,
        "wide": g_wide,
        "narrow": g_narrow,
    }
    blank = jnp.zeros((16, D), F32)

    def part_out(blobs, left):
        for d in range(plan.dp):
            for f in range(plan.fsdp):
                base = plan.base(d, f)
                for tile in range(plan.tiles):
                    held[0:16, :] = blank
                    for name, where, at, tall, wide, row, col in plan.chunks:
                        if where == tile:
                            r0, c0 = plan.origin(name, d, f)
                            held[0:tall, at : at + wide] = grads[name][
                                r0 + row : r0 + row + tall, c0 + col : c0 + col + wide
                            ]
                    blobs[base + 16 * tile : base + 16 * tile + 16, :] = held[0:16, :].astype(BF16)
        copy = pltpu.make_async_copy(blobs, gblob_ref, left)
        copy.start()
        copy.wait()

    pl.run_scoped(part_out, pltpu.VMEM(blob_ref.shape, BF16), pltpu.SemaphoreType.DMA)


def compute(plan, tokens, cots, crops, blobs):
    canvases, length, width = tokens.shape
    rows = PAD_KEYS * canvases
    every = GROUPS * rows
    pair = 2 * canvases
    slab = GROUPS * pair
    vm = pl.BlockSpec(memory_space=pltpu.VMEM)
    hbm = pl.BlockSpec(memory_space=pl.ANY)

    def whole(dtype):
        return [
            pltpu.VMEM((D, GROUPS * D), dtype),
            pltpu.VMEM((PARTS, D, CHUNK), dtype),
            pltpu.VMEM((PARTS, D, CHUNK), dtype),
            pltpu.VMEM((D, D), dtype),
            pltpu.VMEM((D, D), dtype),
            pltpu.VMEM((D, 2 * D), dtype),
        ]

    scratch = [
        pltpu.VMEM((length, D), F32),
        pltpu.VMEM((2, length, D), BF16),
        pltpu.SemaphoreType.DMA((2,)),
        pltpu.VMEM((every, D), F32),
        pltpu.VMEM((every, D), F32),
        pltpu.VMEM((every, D), BF16),
        pltpu.VMEM((every, D), BF16),
        pltpu.VMEM((rows, GROUPS * D), BF16),
        pltpu.VMEM((every, D), F32),
        pltpu.VMEM((every, D), BF16),
        pltpu.VMEM((canvases, GROUPS * PAD_KEYS, D), BF16),
        pltpu.VMEM((D // 2 * canvases, D), F32),
        pltpu.VMEM((D // 2 * canvases, D), F32),
        pltpu.VMEM((D // 2 * canvases, D), F32),
        pltpu.VMEM((D // 2 * canvases, D), F32),
        pltpu.VMEM((rows, D), BF16),
        pltpu.VMEM((every, D), BF16),
        pltpu.VMEM((every, D), F32),
        pltpu.VMEM((rows + 2 * MARGIN, D), F32),
        pltpu.VMEM((9, rows, CHUNK), BF16),
        pltpu.VMEM((canvases, 1, D), F32),
        pltpu.VMEM((PARTS, TAPS + 2, pair, CHUNK), BF16),
        pltpu.VMEM((PARTS, 8 * (TAPS + 2), CHUNK), F32),
        pltpu.VMEM((D, GROUPS * D), F32),
        pltpu.VMEM((D, FF), F32),
        pltpu.VMEM((D, FF), F32),
        pltpu.VMEM((D, D), F32),
        pltpu.VMEM((D, D), F32),
        pltpu.VMEM((D, 2 * D), F32),
        pltpu.VMEM((16, FF), F32),
        pltpu.VMEM((16, D), F32),
        *whole(BF16),
        *whole(F32),
        pltpu.VMEM((16, FF), F32),
        pltpu.VMEM((16, D), F32),
        pltpu.VMEM((88, D), F32),
    ]
    return pl.pallas_call(
        functools.partial(compute_kernel, plan),
        out_shape=(
            jax.ShapeDtypeStruct(tokens.shape, BF16),
            jax.ShapeDtypeStruct(tokens.shape, BF16),
            jax.ShapeDtypeStruct(blobs.shape, BF16),
        ),
        in_specs=[hbm, hbm, vm, hbm],
        out_specs=(hbm, hbm, hbm),
        scratch_shapes=scratch,
        compiler_params=pltpu.CompilerParams(vmem_limit_bytes=63 * 1024 * 1024),
    )(tokens, cots, crops, blobs)


NAMES = ("query", "pairs", "reduce", "output", "expand", "shrink")
TURNED = ("query", "reduce", "output", "shrink")
MESH = pl.DeviceIdType.MESH


class Place:
    def __init__(self, plan):
        self.plan = plan
        dp, fsdp = lax.axis_index("dp"), lax.axis_index("fsdp")
        self.core, self.y = lax.rem(dp, plan.cores), lax.div(dp, plan.cores)
        self.x, self.z = lax.rem(fsdp, plan.xs), lax.div(fsdp, plan.xs)
        self.dp, self.fsdp = dp, fsdp

    def device(self, core=0, y=0, x=0, z=0):
        plan = self.plan
        core = lax.rem(self.core + core, plan.cores)
        y, x = lax.rem(self.y + y, plan.ys), lax.rem(self.x + x, plan.xs)
        z = lax.rem(self.z + z, plan.zs)
        return {"dp": y * plan.cores + core, "fsdp": z * plan.xs + x}

    def block(self, core=0, y=0, x=0):
        plan = self.plan
        core = lax.rem(self.core + core, plan.cores)
        return pl.multiple_of((core * plan.ys * plan.xs + self.within(y, x)) * plan.zs * plan.rows, 16)

    def within(self, y=0, x=0):
        plan = self.plan
        return lax.rem(self.y + y, plan.ys) * plan.xs + lax.rem(self.x + x, plan.xs)

    def blob(self, z=0):
        plan = self.plan
        return pl.multiple_of(lax.rem(self.z + z, plan.zs) * plan.rows, 16)

    def partners(self):
        plan = self.plan
        return (
            [self.device(z=k) for k in range(1, plan.zs)]
            + [self.device(x=k) for k in range(1, plan.xs)]
            + [self.device(y=k) for k in range(1, plan.ys)]
            + [self.device(core=k) for k in range(1, plan.cores)]
        )


def greet(devices):
    barrier = pltpu.get_barrier_semaphore()
    for device in devices:
        pl.semaphore_signal(barrier, inc=1, device_id=device, device_id_type=MESH)
    pl.semaphore_wait(barrier, len(devices))


class Copies:
    def __init__(self, send, receive):
        self.send, self.receive, self.all = send, receive, []

    def start(self, source, target, device):
        number = len(self.all)
        copy = pltpu.make_async_remote_copy(
            src_ref=source,
            dst_ref=target,
            send_sem=self.send.at[number],
            recv_sem=self.receive.at[number],
            device_id=device,
            device_id_type=MESH,
        )
        copy.start()
        self.all.append(copy)
        return copy

    def finish(self):
        for copy in self.all:
            copy.wait_send()


def gather_count(plan):
    xs, ys, cores = plan.xs - 1, plan.ys - 1, plan.cores - 1
    return plan.zs - 1 + xs + ys + 2 * xs * ys + cores * (1 + xs + ys + 2 * xs * ys)


def gather_kernel(plan, *refs):
    pieces, (out, tile_s, send, receive) = refs[: len(PIECES)], refs[len(PIECES) :]
    me = Place(plan)
    copies = Copies(send, receive)
    source = {piece[0]: ref for piece, ref in zip(PIECES, pieces)}
    tile_s[...] = jnp.zeros_like(tile_s)
    for name, tile, at, tall, wide, row, col in plan.chunks:
        tile_s[16 * tile : 16 * tile + tall, at : at + wide] = source[name][
            row : row + tall, col : col + wide
        ]
    own = out.at[pl.ds(pl.multiple_of(me.block() + me.blob(), 16), plan.rows)]
    own[...] = tile_s[...].astype(BF16)
    greet(me.partners())
    group = plan.zs * plan.rows
    half = group // 2

    def part(y=0, x=0, second=None):
        start = me.block(y=y, x=x)
        if second is None:
            return out.at[pl.ds(start, group)]
        return out.at[pl.ds(pl.multiple_of(start + (half if second else 0), 16), half)]

    def pass_on(ref, device):
        return copies.start(ref, ref, device)

    def to_cores(ref):
        return [pass_on(ref, me.device(core=k)) for k in range(1, plan.cores)]

    waits = []
    for copy in [pass_on(own, me.device(z=k)) for k in range(1, plan.zs)]:
        copy.wait_recv()
    along_x = {k: pass_on(part(), me.device(x=k)) for k in range(1, plan.xs)}
    along_y = {k: pass_on(part(), me.device(y=k)) for k in range(1, plan.ys)}
    waits += to_cores(part())
    first, second = {}, {}
    for kx, copy in along_x.items():
        copy.wait_recv()
        for ky in range(1, plan.ys):
            first[ky, kx] = pass_on(part(x=plan.xs - kx, second=False), me.device(y=ky))
        waits += to_cores(part(x=plan.xs - kx))
    for ky, copy in along_y.items():
        copy.wait_recv()
        for kx in range(1, plan.xs):
            second[ky, kx] = pass_on(part(y=plan.ys - ky, second=True), me.device(x=kx))
        waits += to_cores(part(y=plan.ys - ky))
    for number, table in enumerate((first, second)):
        for (ky, kx), copy in table.items():
            copy.wait_recv()
            waits += to_cores(part(y=plan.ys - ky, x=plan.xs - kx, second=bool(number)))
    for copy in waits:
        copy.wait_recv()
    copies.finish()


def gather(plan, shards):
    vm = pl.BlockSpec(memory_space=pltpu.VMEM)
    count = gather_count(plan)
    return pl.pallas_call(
        functools.partial(gather_kernel, plan),
        out_shape=jax.ShapeDtypeStruct((plan.devices * plan.rows, D), BF16),
        in_specs=[vm] * len(PIECES),
        out_specs=vm,
        scratch_shapes=[
            pltpu.VMEM((plan.rows, D), F32),
            pltpu.SemaphoreType.DMA((count,)),
            pltpu.SemaphoreType.DMA((count,)),
        ],
        compiler_params=pltpu.CompilerParams(
            collective_id=1, has_side_effects=True, vmem_limit_bytes=40 * 1024 * 1024
        ),
    )(*(shards[piece[0]] for piece in PIECES))


class Vectors:
    def __init__(self, plan, rows):
        self.chunks, used = [], []
        for name in NAMES:
            height, width = plan.shard[name]
            length = width if (name in TURNED) == rows else height
            for start in range(0, length, D):
                size = min(D, length - start)
                for row, taken in enumerate(used):
                    if taken + size <= D:
                        break
                else:
                    row = len(used)
                    used.append(0)
                self.chunks.append((name, row, used[row], size, start))
                used[row] += size
        self.rows = -(-len(used) // 8) * 8

    def of(self, name):
        return [chunk[1:] for chunk in self.chunks if chunk[0] == name]

    def put(self, ref, name, vector, offset=0):
        lanes = vector.shape[0] == 1
        for row, at, size, start in self.of(name):
            if lanes:
                line = vector[:, start : start + size]
            else:
                here = turn_spot(vector.shape[0], at)
                line = jnp.sum(jnp.where(here, vector, 0.0), axis=0, keepdims=True)
                line = line[:, at : at + size]
            ref[offset + row : offset + row + 1, at : at + size] = line

    def get_lanes(self, value, name):
        parts = [value[row : row + 1, at : at + size] for row, at, size, _ in self.of(name)]
        return parts[0] if len(parts) == 1 else jnp.concatenate(parts, axis=1)

    def get_column(self, value, name):
        ((row, at, size, _),) = self.of(name)
        here = turn_spot(size, at)
        return jnp.sum(jnp.where(here, value[row : row + 1, :], 0.0), axis=1, keepdims=True)


def turn_spot(size, at):
    lanes = lax.broadcasted_iota(jnp.int32, (size, D), 1)
    return lanes == lax.broadcasted_iota(jnp.int32, (size, D), 0) + at


def reduce_count(plan):
    xs, ys = plan.xs - 1, plan.ys - 1
    swap = plan.ys * plan.xs * (plan.cores - 1)
    return swap + 2 * xs * ys + xs + ys + plan.zs - 1 + 2 * (plan.dp - 1) + 2 * (plan.fsdp - 1)


def reduce_kernel(plan, *refs):
    gblob = refs[0]
    rowvars, colvars = refs[1:7], refs[7:13]
    second_wide, second_narrow = refs[13:15]
    outs = dict(zip([piece[0] for piece in PIECES], refs[15:23]))
    row_out, col_out, wide_out, narrow_out = refs[23:27]
    (
        swap_s,
        sum_s,
        first_s,
        second_s,
        along_x_s,
        along_y_s,
        own_s,
        away_s,
        along_z_s,
        grad_s,
        rows_s,
        cols_s,
        part_s,
        norm_s,
        old_s,
        send,
        receive,
    ) = refs[27:]
    me = Place(plan)
    copies = Copies(send, receive)
    group = plan.zs * plan.rows
    half = group // 2
    by_row, by_col = Vectors(plan, True), Vectors(plan, False)
    dp_peers = [{"dp": lax.rem(me.dp + k, plan.dp), "fsdp": me.fsdp} for k in range(1, plan.dp)]
    fsdp_peers = [{"dp": me.dp, "fsdp": lax.rem(me.fsdp + k, plan.fsdp)} for k in range(1, plan.fsdp)]
    greet(dp_peers + fsdp_peers)

    def spot(y, x):
        return pl.ds(pl.multiple_of(me.within(y, x) * group, 16), group)

    spots = sorted(((y, x) for y in range(plan.ys) for x in range(plan.xs)), key=lambda s: -(s[0] > 0) - (s[1] > 0))
    swaps = {}
    for y, x in spots:
        for k in range(1, plan.cores):
            source = gblob.at[pl.ds(me.block(core=k, y=y, x=x), group)]
            swaps[y, x] = copies.start(source, swap_s.at[spot(y, x)], me.device(core=k))

    def chip_sum(y, x):
        total = gblob[pl.ds(me.block(y=y, x=x), group), :].astype(F32)
        if (y, x) in swaps:
            swaps[y, x].wait_recv()
            total = total + swap_s[spot(y, x), :].astype(F32)
        return total

    pairs = [(y, x) for y in range(1, plan.ys) for x in range(1, plan.xs)]
    first, second = {}, {}
    for number, (y, x) in enumerate(pairs):
        here = spot(y, x)
        sum_s[here, :] = chip_sum(y, x).astype(BF16)
        base = me.within(y, x) * group
        low = sum_s.at[pl.ds(pl.multiple_of(base, 16), half)]
        high = sum_s.at[pl.ds(pl.multiple_of(base + half, 16), half)]
        first[y, x] = copies.start(low, first_s.at[number], me.device(y=y))
        second[y, x] = copies.start(high, second_s.at[number], me.device(x=x))
    along_x, along_y = {}, {}
    for x in range(1, plan.xs):
        own_s[...] = chip_sum(0, x)
        for number, (py, px) in enumerate(pairs):
            if px == x:
                first[py, px].wait_recv()
                own_s[:half, :] += first_s[number].astype(F32)
        sum_s[spot(0, x), :] = own_s[...].astype(BF16)
        along_x[x] = copies.start(sum_s.at[spot(0, x)], along_x_s.at[x - 1], me.device(x=x))
    for y in range(1, plan.ys):
        own_s[...] = chip_sum(y, 0)
        for number, (py, px) in enumerate(pairs):
            if py == y:
                second[py, px].wait_recv()
                own_s[half:, :] += second_s[number].astype(F32)
        sum_s[spot(y, 0), :] = own_s[...].astype(BF16)
        along_y[y] = copies.start(sum_s.at[spot(y, 0)], along_y_s.at[y - 1], me.device(y=y))
    own_s[...] = chip_sum(0, 0)
    for x, copy in along_x.items():
        copy.wait_recv()
        own_s[...] += along_x_s[x - 1].astype(F32)
    for y, copy in along_y.items():
        copy.wait_recv()
        own_s[...] += along_y_s[y - 1].astype(F32)

    away_s[...] = own_s[...].astype(BF16)
    along_z = [
        copies.start(away_s.at[pl.ds(me.blob(k), plan.rows)], along_z_s.at[k - 1], me.device(z=k))
        for k in range(1, plan.zs)
    ]
    total = own_s[pl.ds(me.blob(), plan.rows), :]
    for k, copy in enumerate(along_z):
        copy.wait_recv()
        total = total + along_z_s[k].astype(F32)
    grad_s[...] = total
    grads = {}
    for name, (height, width) in plan.shard.items():
        lines = {}
        for owner, tile, at, tall, wide, row, col in plan.chunks:
            if owner == name:
                lines.setdefault(row, []).append(
                    grad_s[16 * tile : 16 * tile + tall, at : at + wide]
                )
        lines = [parts[0] if len(parts) == 1 else jnp.concatenate(parts, axis=1) for parts in lines.values()]
        grads[name] = lines[0] if len(lines) == 1 else jnp.concatenate(lines, axis=0)

    decay_two = 1.0 - STEP ** (-0.8)

    def exchange(buffer, mine, peers):
        started = [copies.start(buffer.at[mine], buffer.at[mine], peer) for peer in peers]
        return started

    def gathered(buffer, started):
        for copy in started:
            copy.wait_recv()
        total = buffer[0]
        for number in range(1, buffer.shape[0]):
            total = total + buffer[number]
        return total

    full = {}
    own_rows, own_cols = rows_s.at[me.fsdp], cols_s.at[me.dp]
    own_rows[...] = jnp.zeros(own_rows.shape, F32)
    own_cols[...] = jnp.zeros(own_cols.shape, F32)
    for name in NAMES:
        height, width = plan.shard[name]
        square = grads[name] * grads[name] + SQUARE_EPS
        over_rows = jnp.sum(square, axis=0, keepdims=True)
        over_cols = jnp.sum(square, axis=1, keepdims=True)
        if name in TURNED:
            full[name] = (width * plan.dp, height * plan.fsdp)
            row_part, col_part = over_rows, over_cols
        else:
            full[name] = (height * plan.dp, width * plan.fsdp)
            row_part, col_part = over_cols, over_rows
        by_row.put(own_rows, name, row_part * ((1.0 - decay_two) / full[name][1]))
        by_col.put(own_cols, name, col_part * ((1.0 - decay_two) / full[name][0]))
    height, width = plan.shard["narrow"]
    own_cols[by_col.rows : by_col.rows + height, 0:width] = grads["narrow"]
    row_copies = exchange(rows_s, me.fsdp, fsdp_peers)
    col_copies = exchange(cols_s, me.dp, dp_peers)
    old_s[...] = jnp.zeros_like(old_s)
    for name, ref in zip(NAMES, rowvars):
        by_row.put(old_s, name, ref[...].reshape(1, ref.shape[0]))
    for name, ref in zip(NAMES, colvars):
        by_col.put(old_s, name, ref[...].reshape(1, ref.shape[0]), by_row.rows)
    wide = grads["wide"]
    wide_second = decay_two * second_wide[...] + (1.0 - decay_two) * (wide * wide + SQUARE_EPS)
    wide_out[...] = wide_second
    wide_update = wide * lax.rsqrt(wide_second)
    row_new = decay_two * old_s[: by_row.rows, :] + gathered(rows_s, row_copies)
    row_out[...] = row_new
    all_cols = gathered(cols_s, col_copies)[: by_col.rows, :]
    col_new = decay_two * old_s[by_row.rows :, :] + all_cols
    col_out[...] = col_new
    narrow = cols_s[0, by_col.rows : by_col.rows + height, 0:width]
    narrow_second = decay_two * second_narrow[...] + (1.0 - decay_two) * (narrow * narrow + SQUARE_EPS)
    narrow_out[...] = narrow_second
    narrow_update = narrow * lax.rsqrt(narrow_second)

    lane = lax.broadcasted_iota(jnp.int32, (16, D), 1)
    count = len(NAMES)

    def whole_sum(values):
        return jnp.sum(jnp.sum(values, axis=1, keepdims=True), axis=0, keepdims=True)

    def row_norm(values):
        norm = jnp.sum(values * values, axis=1, keepdims=True)
        return jnp.concatenate([norm, jnp.zeros((16 - norm.shape[0], 1), F32)], axis=0)

    updates = {}
    part = jnp.where(lane == 2 * count, row_norm(wide_update), 0.0)
    for number, name in enumerate(NAMES):
        lanes = by_row.get_lanes(row_new, name)
        if name in TURNED:
            row_scale = lax.rsqrt(lanes)
            col_scale = lax.rsqrt(by_col.get_column(col_new, name))
        else:
            row_scale = lax.rsqrt(by_row.get_column(row_new, name))
            col_scale = lax.rsqrt(by_col.get_lanes(col_new, name))
        update = grads[name] * row_scale * col_scale
        updates[name] = update
        part = jnp.where(lane == number, whole_sum(update * update), part)
        part = jnp.where(lane == count + number, whole_sum(lanes), part)
    part_s[me.dp] = part
    sums = gathered(part_s, exchange(part_s, me.dp, dp_peers))
    norm_s[me.fsdp] = jnp.where(lane == 2 * count + 1, row_norm(narrow_update), sums)
    norms = gathered(norm_s, exchange(norm_s, me.fsdp, fsdp_peers))
    for number, name in enumerate(NAMES):
        mean = sums[0:1, count + number : count + number + 1] / full[name][0]
        norm = norms[0:1, number : number + 1] / (full[name][0] * full[name][1])
        clip = jnp.maximum(1.0, jnp.sqrt(mean * norm) / CLIP_RMS)
        outs[name][...] = updates[name] * (jnp.sqrt(mean) / clip)
    for number, name, update in ((0, "wide", wide_update), (1, "narrow", narrow_update)):
        size = FF if name == "wide" else D
        norm = norms[: update.shape[0], 2 * count + number : 2 * count + number + 1] / size
        outs[name][...] = update / jnp.maximum(1.0, jnp.sqrt(norm) / CLIP_RMS)
    copies.finish()


def reduce_all(plan, gblobs, rowvars, colvars, second_wide, second_narrow):
    vm = pl.BlockSpec(memory_space=pltpu.VMEM)
    count = reduce_count(plan)
    by_row, by_col = Vectors(plan, True), Vectors(plan, False)
    group = plan.zs * plan.rows
    mine = plan.ys * plan.xs * group
    pairs = max(1, (plan.ys - 1) * (plan.xs - 1))
    thin = by_col.rows + 16
    out_shape = [jax.ShapeDtypeStruct(plan.shard[piece[0]], F32) for piece in PIECES]
    out_shape += [jax.ShapeDtypeStruct((by_row.rows, D), F32), jax.ShapeDtypeStruct((by_col.rows, D), F32)]
    out_shape += [jax.ShapeDtypeStruct(plan.shard[name], F32) for name in ("wide", "narrow")]
    return pl.pallas_call(
        functools.partial(reduce_kernel, plan),
        out_shape=out_shape,
        in_specs=[vm] * 15,
        out_specs=[vm] * 12,
        scratch_shapes=[
            pltpu.VMEM((mine, D), BF16),
            pltpu.VMEM((mine, D), BF16),
            pltpu.VMEM((pairs, group // 2, D), BF16),
            pltpu.VMEM((pairs, group // 2, D), BF16),
            pltpu.VMEM((max(1, plan.xs - 1), group, D), BF16),
            pltpu.VMEM((max(1, plan.ys - 1), group, D), BF16),
            pltpu.VMEM((group, D), F32),
            pltpu.VMEM((group, D), BF16),
            pltpu.VMEM((max(1, plan.zs - 1), plan.rows, D), BF16),
            pltpu.VMEM((plan.rows, D), F32),
            pltpu.VMEM((plan.fsdp, by_row.rows, D), F32),
            pltpu.VMEM((plan.dp, thin, D), F32),
            pltpu.VMEM((plan.dp, 16, D), F32),
            pltpu.VMEM((plan.fsdp, 16, D), F32),
            pltpu.VMEM((by_row.rows + by_col.rows, D), F32),
            pltpu.SemaphoreType.DMA((count,)),
            pltpu.SemaphoreType.DMA((count,)),
        ],
        compiler_params=pltpu.CompilerParams(
            collective_id=2, has_side_effects=True, vmem_limit_bytes=60 * 1024 * 1024
        ),
    )(gblobs, *rowvars, *colvars, second_wide, second_narrow)


def update_kernel(plan, *refs):
    order = [piece[0] for piece in PIECES]
    updates, moments, weights = (dict(zip(order, refs[8 * n : 8 * n + 8])) for n in range(3))
    row_new, col_new, second_wide, second_narrow = refs[24:28]
    new_moments, new_weights = (dict(zip(order, refs[8 * n + 28 : 8 * n + 36])) for n in range(2))
    row_outs, col_outs, wide_out, narrow_out = refs[44:50], refs[50:56], refs[56], refs[57]
    for name in order:
        moment = BETA_ONE * moments[name][...] + (1.0 - BETA_ONE) * updates[name][...]
        new_moments[name][...] = moment
        new_weights[name][...] = weights[name][...] * (1.0 - RATE * DECAY_RATE) - RATE * moment
    by_row, by_col = Vectors(plan, True), Vectors(plan, False)
    for vectors, source, targets in ((by_row, row_new, row_outs), (by_col, col_new, col_outs)):
        for name, ref in zip(NAMES, targets):
            for row, at, size, start in vectors.of(name):
                ref[start : start + size] = source[row : row + 1, at : at + size].reshape(size)
    wide_out[...] = second_wide[...]
    narrow_out[...] = second_narrow[...]


def update_all(plan, reduced, moments, weights):
    vm = pl.BlockSpec(memory_space=pltpu.VMEM)
    order = [piece[0] for piece in PIECES]
    pieces = [jax.ShapeDtypeStruct(plan.shard[name], F32) for name in order]
    row_shapes, col_shapes = [], []
    for name in NAMES:
        height, width = plan.shard[name]
        if name in TURNED:
            height, width = width, height
        row_shapes.append(jax.ShapeDtypeStruct((height,), F32))
        col_shapes.append(jax.ShapeDtypeStruct((width,), F32))
    seconds = [jax.ShapeDtypeStruct(plan.shard[name], F32) for name in ("wide", "narrow")]
    out_shape = pieces + pieces + row_shapes + col_shapes + seconds
    found = pl.pallas_call(
        functools.partial(update_kernel, plan),
        out_shape=out_shape,
        in_specs=[vm] * 28,
        out_specs=[vm] * len(out_shape),
    )(*reduced[:8], *(moments[name] for name in order), *(weights[name] for name in order), *reduced[8:])
    next_moment, next_weight = dict(zip(order, found[:8])), dict(zip(order, found[8:16]))
    return next_moment, next_weight, found[16:22], found[22:28], found[28], found[29]


def body(plan, tokens_in, cotangent, crop_ids, *state):
    weights, moments, rowvars, colvars = {}, {}, [], []
    for number, name in enumerate(NAMES):
        weights[name], moments[name], row, col = state[4 * number : 4 * number + 4]
        rowvars.append(row)
        colvars.append(col)
    weights["narrow"], moments["narrow"], second_narrow = state[24:27]
    weights["wide"], moments["wide"], second_wide = state[27:30]

    def turned(values):
        return {name: value.T if name in TURNED else value for name, value in values.items()}

    weights, moments = turned(weights), turned(moments)
    micro, local, length, width = tokens_in.shape
    flat = (micro * local, length, width)
    blobs = gather(plan, weights)
    result, input_grad, gblobs = compute(
        plan, tokens_in.reshape(flat), cotangent.reshape(flat), crop_ids, blobs
    )
    reduced = reduce_all(plan, gblobs, rowvars, colvars, second_wide, second_narrow)
    next_moment, next_weight, row_new, col_new, wide_new, narrow_new = update_all(
        plan, reduced, moments, weights
    )
    next_moment, next_weight = turned(next_moment), turned(next_weight)
    results = [result.reshape(tokens_in.shape), input_grad.reshape(tokens_in.shape)]
    for number, name in enumerate(NAMES):
        results += [next_moment[name], row_new[number], col_new[number], next_weight[name]]
    for name, second in (("narrow", narrow_new), ("wide", wide_new)):
        results += [next_moment[name], second, next_weight[name]]
    return tuple(results)


def solution(mesh):
    plan = Plan(mesh.shape["dp"], mesh.shape["fsdp"])
    tokens = P(None, ("dp", "fsdp"), None, None)
    matrix = P("dp", "fsdp")
    by_rows, by_cols = P("dp"), P("fsdp")
    thin, broad = P(None, "fsdp"), P(None, ("dp", "fsdp"))
    state = (matrix, matrix, by_rows, by_cols) * 6 + (thin,) * 3 + (broad,) * 3
    in_specs = (tokens, tokens, P(None, ("dp", "fsdp"), None)) + state
    moved = (matrix, by_rows, by_cols, matrix) * 6 + (thin,) * 3 + (broad,) * 3
    return jax.shard_map(
        functools.partial(body, plan),
        mesh=mesh,
        in_specs=in_specs,
        out_specs=(tokens, tokens) + moved,
        check_vma=False,
    )
```

```python
import functools
import numpy as np
import jax
import jax.numpy as jnp
from jax import lax
from jax.experimental import pallas as pl
from jax.experimental.pallas import tpu as pltpu
from jax.sharding import PartitionSpec as P

HEADS = 2
GRID = 28
STEP = 10
NORM_EPS = 1e-06
SQUARE_EPS = 1e-30
CLIP_RMS = 1.0
BETA_ONE = 0.9
RATE = 1.0
DECAY_RATE = 0.01
MASKED = -1e30

D = 128
FF = 1024
SIDE = 4
BLOCKS = GRID // SIDE
KEYS = BLOCKS * BLOCKS
PAD_KEYS = KEYS + 1
GROUPS = SIDE * SIDE
TAPS = 9
MARGIN = 64
CHUNK = 256
PARTS = FF // CHUNK
HALF = PAD_KEYS // 2
REACH = BLOCKS + 1
RUN = 5

F32 = jnp.float32
BF16 = jnp.bfloat16

PIECES = (
    ("reduce", (D, GROUPS * D), "f", "d"),
    ("shrink", (D, FF), "f", "d"),
    ("expand", (D, FF), "d", "f"),
    ("query", (D, D), "f", "d"),
    ("output", (D, D), "f", "d"),
    ("pairs", (D, 2 * D), "d", "f"),
    ("wide", (11, FF), "", "df"),
    ("narrow", (11, D), "", "f"),
)


class Plan:
    def __init__(self, dp, fsdp):
        self.dp, self.fsdp = dp, fsdp
        cuts = {"": 1, "d": dp, "f": fsdp, "df": dp * fsdp}
        self.shard = {}
        self.chunks = []
        free = []
        for name, (rows, cols), by_rows, by_cols in PIECES:
            height, width = rows // cuts[by_rows], cols // cuts[by_cols]
            self.shard[name] = (height, width)
            for row in range(0, height, 16):
                for col in range(0, width, D):
                    tall, wide = min(16, height - row), min(D, width - col)
                    for tile, used in enumerate(free):
                        if used + wide <= D:
                            break
                    else:
                        tile = len(free)
                        free.append(0)
                    self.chunks.append((name, tile, free[tile], tall, wide, row, col))
                    free[tile] += wide
        self.tiles = len(free)
        self.rows = 16 * self.tiles
        self.devices = dp * fsdp
        self.cores = 2 if dp % 2 == 0 else 1
        self.ys = dp // self.cores
        self.xs = 1
        while self.xs * self.xs * 4 <= fsdp and fsdp % (2 * self.xs) == 0:
            self.xs *= 2
        self.zs = fsdp // self.xs

    def base(self, d, f):
        y, core = divmod(d, self.cores)
        z, x = divmod(f, self.xs)
        return (((core * self.ys + y) * self.xs + x) * self.zs + z) * self.rows

    def origin(self, name, d, f):
        _, _, by_rows, by_cols = next(piece for piece in PIECES if piece[0] == name)
        at = {"": 0, "d": d, "f": f, "df": d * self.fsdp + f}
        height, width = self.shard[name]
        return at[by_rows] * height, at[by_cols] * width


def nn(left, right):
    return lax.dot_general(left, right, (((1,), (0,)), ((), ())), preferred_element_type=F32)


def nt(left, right):
    return lax.dot_general(left, right, (((1,), (1,)), ((), ())), preferred_element_type=F32)


def tn(left, right):
    return lax.dot_general(left, right, (((0,), (0,)), ((), ())), preferred_element_type=F32)


def fold(values):
    rows, cols = values.shape
    return jnp.sum(values.reshape(rows // 8, 8, cols), axis=0)


def normalize(values):
    center = values - jnp.mean(values, axis=-1, keepdims=True)
    scale = lax.rsqrt(jnp.mean(center * center, axis=-1, keepdims=True) + NORM_EPS)
    return center * scale, scale


def normalize_back(unit, scale, incoming, gain):
    c = incoming * gain
    mean_c = jnp.mean(c, axis=-1, keepdims=True)
    mean_cz = jnp.mean(c * unit, axis=-1, keepdims=True)
    return (c - mean_c - unit * mean_cz) * scale


def gelu_parts(v):
    share = 0.5 + 0.5 * lax.erf(v * 0.5**0.5)
    bell = jnp.exp2(v * v * (-0.5 * 1.4426950408889634))
    return v * share, share + (v * 0.3989422804014327) * bell


def direction(step_at):
    return -1 if step_at < 0 else (1 if step_at >= SIDE else 0)


def at_position(position):
    return position // 2 + HALF * (position % 2)


def places(slab, pair, canvases):
    for g in range(GROUPS):
        for block_row in range(BLOCKS):
            first = block_row * BLOCKS
            for half in range(2):
                start, stop = max(first, HALF * half), min(first + BLOCKS, HALF * (half + 1))
                if start < stop:
                    column = start - first
                    token = (block_row * SIDE + g // SIDE) * GRID + column * SIDE + g % SIDE
                    place = (start - HALF * half) * slab + g * pair + half * canvases
                    yield token, place, stop - start


def compute_kernel(
    plan,
    tokens_ref,
    cots_ref,
    crop_ref,
    blob_ref,
    out_ref,
    gin_ref,
    gblob_ref,
    stage,
    passing,
    arrived,
    landed,
    held,
    mixed_s,
    inputs_s,
    dy_s,
    normed_s,
    query_s,
    attn_s,
    probs_s,
    key_s,
    value_s,
    dkey_s,
    dvalue_s,
    dred_s,
    second_s,
    back_s,
    crop_s,
    mask_s,
    keycrop_s,
    taps_s,
    dtaps_s,
    w_reduce,
    w_shrink,
    w_expand,
    w_query,
    w_output,
    w_pairs,
    w_wide,
    w_narrow,
    lo_reduce,
    lo_shrink,
    lo_expand,
    lo_query,
    lo_output,
    lo_pairs,
    g_reduce,
    g_shrink,
    g_expand,
    g_query,
    g_output,
    g_pairs,
    g_wide,
    g_narrow,
    sums,
):
    canvases = out_ref.shape[0]
    pair = 2 * canvases
    rows = PAD_KEYS * canvases
    slab = GROUPS * pair
    run = RUN * slab
    lane = lax.broadcasted_iota(jnp.int32, (1, D), 1)
    low_half = lane < D // 2
    full = {
        "reduce": w_reduce,
        "shrink": w_shrink,
        "expand": w_expand,
        "query": w_query,
        "output": w_output,
        "pairs": w_pairs,
        "wide": w_wide,
        "narrow": w_narrow,
    }
    fetched = [
        pltpu.make_async_copy(source, target, landed.at[number])
        for number, (source, target) in enumerate(((cots_ref, dy_s), (tokens_ref, inputs_s)))
    ]
    for copy in fetched:
        copy.start()

    def assemble(blobs, landed):
        copy = pltpu.make_async_copy(blob_ref, blobs, landed)
        copy.start()
        copy.wait()
        for d in range(plan.dp):
            for f in range(plan.fsdp):
                base = plan.base(d, f)
                for name, tile, at, tall, wide, row, col in plan.chunks:
                    if name == "narrow" and d:
                        continue
                    r0, c0 = plan.origin(name, d, f)
                    tile_rows = blobs[base + 16 * tile : base + 16 * tile + 16, :].astype(F32)
                    full[name][r0 + row : r0 + row + tall, c0 + col : c0 + col + wide] = tile_rows[
                        :tall, at : at + wide
                    ]

    pl.run_scoped(assemble, pltpu.VMEM(blob_ref.shape, BF16), pltpu.SemaphoreType.DMA)
    lo_reduce[...] = w_reduce[...].astype(BF16)
    lo_query[...] = w_query[...].astype(BF16)
    lo_output[...] = w_output[...].astype(BF16)
    lo_pairs[...] = w_pairs[...].astype(BF16)
    for part in range(PARTS):
        cols = slice(part * CHUNK, (part + 1) * CHUNK)
        lo_shrink[part] = w_shrink[:, cols].astype(BF16)
        lo_expand[part] = w_expand[:, cols].astype(BF16)
        for tap in range(TAPS + 2):
            taps_s[part, tap] = jnp.broadcast_to(w_wide[tap : tap + 1, cols], (pair, CHUNK)).astype(BF16)

    def narrow(row):
        return w_narrow[row : row + 1, :]

    sums[...] = jnp.zeros_like(sums)
    dtaps_s[...] = jnp.zeros_like(dtaps_s)
    for ref in (g_shrink, g_expand, g_query, g_output, g_narrow, g_wide):
        ref[...] = jnp.zeros_like(ref)
    for ref in (key_s, value_s):
        ref[rows:, :] = jnp.zeros((ref.shape[0] - rows, D), F32)

    def add(row, values):
        sums[8 * row : 8 * row + 8, :] += fold(values)

    def run_rows(m):
        return pl.ds(pl.multiple_of(m * run, 16), run)

    def collect(target):
        def leave(c):
            slot = lax.rem(c, 2)
            return pltpu.make_async_copy(passing.at[slot], target.at[c], arrived.at[slot])

        def one(c, _):
            for token, place, count in places(slab, pair, canvases):
                stage[pl.ds(token, count, stride=SIDE), :] = held[
                    pl.ds(place + c, count, stride=slab), :
                ]

            @pl.when(c >= 2)
            def _():
                leave(c - 2).wait()

            passing[lax.rem(c, 2)] = stage[...].astype(BF16)
            leave(c).start()
            return 0

        lax.fori_loop(0, canvases, one, 0)
        for c in range(max(0, canvases - 2), canvases):
            leave(c).wait()

    token = lax.broadcasted_iota(jnp.int32, (GRID * GRID, D), 0)
    key_lane = lax.rem(lax.broadcasted_iota(jnp.int32, (GRID * GRID, D), 1), D // 2)
    crops = jnp.concatenate([crop_ref[m] for m in range(crop_ref.shape[0])], axis=0)
    crops = crops.astype(F32).astype(BF16)

    def crops_of(block):
        corner = lax.div(block, BLOCKS) * (SIDE * GRID) + lax.rem(block, BLOCKS) * SIDE
        return nn(crops, jnp.where((corner == token) & (block < KEYS), 1.0, 0.0).astype(BF16))

    position = lax.rem(lane, D // 2)
    keycrop = crops_of(lax.div(key_lane, 2) + HALF * lax.rem(key_lane, 2))
    keycrop = jnp.where((position < PAD_KEYS) & (position != 2 * HALF - 1), keycrop, -2.0)
    keycrop_s[...] = keycrop.reshape(keycrop_s.shape)
    by_block = jnp.concatenate([crops_of(key_lane), jnp.zeros((D - canvases, D), F32)], axis=0).T
    crop_s[...] = jnp.full(crop_s.shape, -1.0, F32)
    for c in range(canvases):
        crop_s[pl.ds(MARGIN + c, KEYS, stride=canvases), :] = jnp.broadcast_to(
            by_block[:KEYS, c : c + 1], (KEYS, D)
        )

    def by_position(values):
        order = [at_position(number) * canvases for number in range(PAD_KEYS)]
        return jnp.concatenate([values[start : start + canvases, :] for start in order], axis=0)

    own_crop = crop_s[MARGIN : MARGIN + rows, :]
    block = lax.div(lax.broadcasted_iota(jnp.int32, (rows, D), 0), canvases)
    block_i, block_j = lax.div(block, BLOCKS), lax.rem(block, BLOCKS)
    for di in (-1, 0, 1):
        for dj in (-1, 0, 1):
            start = MARGIN + (di * BLOCKS + dj) * canvases
            inside = (block < KEYS) & (block_i + di >= 0) & (block_i + di < BLOCKS)
            inside = inside & (block_j + dj >= 0) & (block_j + dj < BLOCKS)
            near = crop_s[start : start + rows, :] == own_crop
            mask = by_position(jnp.where(near & inside, 1.0, 0.0)).astype(BF16)
            mask_s[(di + 1) * 3 + dj + 1] = mask
    row_crops = by_position(own_crop)
    for k in range(HALF):
        piece = row_crops[k * pair : (k + 1) * pair, :]
        back_s[k * slab : (k + 1) * slab, :] = jnp.concatenate([piece] * GROUPS, axis=0)

    for copy in fetched:
        copy.wait()

    def pair_rows(m, k):
        return pl.ds(pl.multiple_of((m * RUN + k) * pair, 16), pair)

    def first(m, _):
        unit, _ = normalize(inputs_s[run_rows(m), :].astype(F32))
        low = (unit * narrow(0) + narrow(1)).astype(BF16)
        for k in range(RUN):
            for g in range(GROUPS):
                start = k * slab + g * pair
                normed_s[pair_rows(m, k), g * D : (g + 1) * D] = low[start : start + pair, :]
        query_s[run_rows(m), :] = (nt(low, lo_query[...]) + narrow(2)).astype(BF16).astype(F32)
        return 0

    lax.fori_loop(0, HALF // RUN, first, 0)

    reduced = nt(normed_s[...], lo_reduce[...]) + narrow(4)
    reduced_unit, reduced_scale = normalize(reduced)
    reduced_low = (reduced_unit * narrow(5) + narrow(6)).astype(BF16)
    pairs = nn(reduced_low, lo_pairs[...])
    key_s[:rows, :] = pairs[:, :D].astype(BF16).astype(F32)
    value_s[:rows, :] = (pairs[:, D:] + narrow(3)).astype(BF16).astype(F32)

    def split_heads(values):
        return jnp.concatenate(
            [jnp.where(low_half, values, 0.0), jnp.where(low_half, 0.0, values)], axis=0
        ).astype(BF16)

    def join_heads(values):
        return jnp.where(low_half, values[: D // 2, :], values[D // 2 :, :])

    def canvas_rows(c):
        return pl.ds(c, GROUPS * PAD_KEYS, stride=canvases)

    def key_rows(c):
        return pl.ds(c, D // 2, stride=canvases)

    def per_head(values, reduce, fill):
        first_half = reduce(jnp.where(low_half, values, fill), axis=-1, keepdims=True)
        second_half = reduce(jnp.where(low_half, fill, values), axis=-1, keepdims=True)
        return jnp.where(low_half, first_half, second_half)

    def attend(c, _):
        queries = query_s[canvas_rows(c), :].astype(BF16)
        keys = split_heads(key_s[key_rows(c), :])
        values = split_heads(value_s[key_rows(c), :])
        scores = nt(queries, keys) * (D // HEADS) ** (-0.5)
        allowed = back_s[canvas_rows(c), :] == keycrop_s[c]
        scores = jnp.where(allowed, scores, MASKED)
        exponent = jnp.exp(scores - per_head(scores, jnp.max, -3e38))
        exponent = jnp.where(allowed, exponent, 0.0)
        total = jnp.maximum(per_head(exponent, jnp.sum, 0.0), 1.0)
        probs = (exponent / total).astype(BF16)
        probs_s[c] = probs
        held[canvas_rows(c), :] = nn(probs, values)
        return 0

    lax.fori_loop(0, canvases, attend, 0)

    def feed_forward(up_even, up_odd, dconv_s, act_s, dup_s):
        def keep(ref, k):
            spare = ref.shape[0] - 1
            beyond = jnp.where(k < REACH, REACH + HALF + k, jnp.where(k >= HALF - REACH, k - (HALF - REACH), spare))

            def store(group, values):
                here = slice(group * pair, (group + 1) * pair)
                ref[REACH + k, here, :] = values.astype(BF16)
                swapped = jnp.concatenate([values[canvases:, :], values[:canvases, :]], axis=0)
                ref[beyond, here, :] = swapped.astype(BF16)

            return store

        ups = [up_odd if part % 2 else up_even for part in range(PARTS)]

        def spread(part, m, values):
            up = nn(values, lo_expand[part])
            shift = taps_s[part, TAPS].astype(F32)
            for k in range(RUN):
                store = keep(ups[part], m * RUN + k)
                for g in range(GROUPS):
                    start = k * slab + g * pair
                    store(g, up[start : start + pair, :] + shift)

        def second(m, _):
            low = held[run_rows(m), :].astype(BF16)
            attn_s[run_rows(m), :] = low
            mixed = inputs_s[run_rows(m), :].astype(F32) + (nt(low, lo_output[...]) + narrow(7))
            mixed_s[run_rows(m), :] = mixed
            held[run_rows(m), :] = mixed + narrow(10)
            unit, _ = normalize(mixed)
            low = (unit * narrow(8) + narrow(9)).astype(BF16)
            second_s[run_rows(m), :] = low
            spread(0, m, low)
            back_s[run_rows(m), :] = jnp.zeros((run, D), F32)
            return 0

        lax.fori_loop(0, HALF // RUN, second, 0)

        def around(ref, k, at):
            found = []
            for bt in range(-1, SIDE + 1):
                di, dj = direction(at), direction(bt)
                group = (at % SIDE) * SIDE + bt % SIDE
                values = ref[REACH + k + di * BLOCKS + dj, group * pair : (group + 1) * pair, :]
                if di or dj:
                    mask = mask_s[(di + 1) * 3 + dj + 1, pl.ds(pl.multiple_of(k * pair, 16), pair), :]
                    values = values * jnp.concatenate([mask] * (CHUNK // D), axis=1)
                found.append(values)
            return found

        def slabs(ref, m):
            return ref[pl.ds(m * RUN, RUN)].reshape(run, CHUNK)

        def contract(part, m):
            act = slabs(act_s, m)
            held[run_rows(m), :] += nt(act, lo_shrink[part])
            g_shrink[part] += tn(dy_s[run_rows(m), :], act)

        def contract_back(part, m):
            d_up = slabs(dup_s, m)
            back_s[run_rows(m), :] += nt(d_up, lo_expand[part])
            g_expand[part] += tn(second_s[run_rows(m), :], d_up)

        def convolve(ref, k, taps, finish):
            sums_of = {}
            for at in range(-1, SIDE + 1):
                near = around(ref, k, at)
                for a in range(max(0, at - 1), min(SIDE - 1, at + 1) + 1):
                    for b in range(SIDE):
                        for step in range(3):
                            term = near[b + step] * taps[(at - a + 1) * 3 + step]
                            sums_of[a, b] = sums_of[a, b] + term if (a, b) in sums_of else term
                    if at == a + 1:
                        for b in range(SIDE):
                            finish(a * SIDE + b, sums_of.pop((a, b)))

        def feed(part):
            def forward(m, _):
                if part + 1 < PARTS:
                    spread(part + 1, m, second_s[run_rows(m), :])
                if part:
                    contract_back(part - 1, m)
                d_act = nn(dy_s[run_rows(m), :], lo_shrink[part])
                for k in range(RUN):
                    activate(m * RUN + k, d_act[k * slab : (k + 1) * slab, :])
                return 0

            def activate(k, d_act):
                taps = [taps_s[part, tap] for tap in range(TAPS)]
                shift = taps_s[part, TAPS + 1]
                store = keep(dconv_s, k)

                def finish(g, conv):
                    act, slope = gelu_parts((conv + shift).astype(F32))
                    act_s[k, g * pair : (g + 1) * pair, :] = act.astype(BF16)
                    store(g, d_act[g * pair : (g + 1) * pair, :] * slope)

                convolve(ups[part], k, taps, finish)

            lax.fori_loop(0, HALF // RUN, forward, 0)

            def backward(m, _):
                contract(part, m)
                for k in range(RUN):
                    turn(m * RUN + k)
                return 0

            def turn(k):
                taps = [taps_s[part, TAPS - 1 - tap] for tap in range(TAPS)]
                through = {}

                def finish(g, d_up):
                    dup_s[k, g * pair : (g + 1) * pair, :] = d_up
                    through[0] = through[0] + d_up if through else d_up

                convolve(dconv_s, k, taps, finish)
                here, own = {}, None
                products = [None] * TAPS
                for at in range(-1, SIDE + 1):
                    near = around(ups[part], k, at)
                    if at + 1 < SIDE:
                        for b in range(SIDE):
                            g = (at + 1) * SIDE + b
                            here[at + 1, b] = dconv_s[REACH + k, g * pair : (g + 1) * pair, :]
                            own = here[at + 1, b] if own is None else own + here[at + 1, b]
                    for a in range(max(0, at - 1), min(SIDE - 1, at + 1) + 1):
                        for b in range(SIDE):
                            for step in range(3):
                                tap = (at - a + 1) * 3 + step
                                term = near[b + step] * here[a, b]
                                products[tap] = term if products[tap] is None else products[tap] + term

                for row, value in enumerate(products + [through[0], own]):
                    value = value.astype(F32)
                    dtaps_s[part, 8 * row : 8 * row + 8, :] += fold(value)

            lax.fori_loop(0, HALF // RUN, backward, 0)

        for part in range(PARTS):
            feed(part)
        collect(out_ref)

        def third(m, _):
            cot = dy_s[run_rows(m), :]
            d_up = slabs(dup_s, m)
            g_expand[PARTS - 1] += tn(second_s[run_rows(m), :], d_up)
            incoming = back_s[run_rows(m), :] + nt(d_up, lo_expand[PARTS - 1])
            unit, scale = normalize(mixed_s[run_rows(m), :])
            d_mixed = cot.astype(F32) + normalize_back(unit, scale, incoming, narrow(8))
            add(8, incoming * unit)
            add(9, incoming)
            add(10, cot.astype(F32))
            mixed_s[run_rows(m), :] = d_mixed
            low = d_mixed.astype(BF16)
            add(7, low.astype(F32))
            g_output[...] += tn(low, attn_s[run_rows(m), :])
            held[run_rows(m), :] = nn(low, lo_output[...])
            return 0

        lax.fori_loop(0, HALF // RUN, third, 0)

    far = pltpu.VMEM((HALF + 2 * REACH + 1, slab, CHUNK), BF16)
    near = pltpu.VMEM((HALF, slab, CHUNK), BF16)
    pl.run_scoped(feed_forward, far, far, far, near, near)

    def attend_back(c, _):
        queries = query_s[canvas_rows(c), :].astype(BF16)
        keys = split_heads(key_s[key_rows(c), :])
        values = split_heads(value_s[key_rows(c), :])
        probs_low = probs_s[c]
        probs = probs_low.astype(F32)
        d_attn = held[canvas_rows(c), :].astype(BF16)
        d_probs = nt(d_attn, values)
        d_scores = probs * (d_probs - per_head(d_probs * probs, jnp.sum, 0.0))
        d_scores = d_scores.astype(BF16)
        scale = (D // HEADS) ** (-0.5)
        held[canvas_rows(c), :] = nn(d_scores, keys) * scale
        dkey_s[key_rows(c), :] = join_heads(tn(d_scores, queries)) * scale
        dvalue_s[key_rows(c), :] = join_heads(tn(probs_low, d_attn))
        return 0

    lax.fori_loop(0, canvases, attend_back, 0)

    d_pairs = jnp.concatenate([dkey_s[:rows, :], dvalue_s[:rows, :]], axis=1).astype(BF16)
    g_pairs[...] = tn(reduced_low, d_pairs)
    add(3, d_pairs[:, D:].astype(F32))
    incoming = nt(d_pairs, lo_pairs[...])
    add(5, incoming * reduced_unit)
    add(6, incoming)
    d_reduced = normalize_back(reduced_unit, reduced_scale, incoming, narrow(5)).astype(BF16)
    add(4, d_reduced.astype(F32))
    dred_s[...] = d_reduced
    g_reduce[...] = tn(d_reduced, normed_s[...])

    def fourth(m, _):
        low = held[run_rows(m), :].astype(BF16)
        add(2, low.astype(F32))
        here = pl.ds(pl.multiple_of(m * RUN * pair, 16), RUN * pair)
        normed, patches = normed_s[here, :], nn(dred_s[here, :], lo_reduce[...])

        def by_token(values):
            return jnp.concatenate(
                [
                    values[k * pair : (k + 1) * pair, g * D : (g + 1) * D]
                    for k in range(RUN)
                    for g in range(GROUPS)
                ],
                axis=0,
            )

        g_query[...] += tn(low, by_token(normed))
        incoming = nn(low, lo_query[...]) + by_token(patches)
        unit, scale = normalize(inputs_s[run_rows(m), :].astype(F32))
        add(0, incoming * unit)
        add(1, incoming)
        back = normalize_back(unit, scale, incoming, narrow(0))
        held[run_rows(m), :] = mixed_s[run_rows(m), :] + back
        return 0

    lax.fori_loop(0, HALF // RUN, fourth, 0)
    collect(gin_ref)

    for row in range(11):
        g_narrow[row : row + 1, :] = jnp.sum(sums[8 * row : 8 * row + 8, :], axis=0, keepdims=True)
        for part in range(PARTS):
            g_wide[row : row + 1, part * CHUNK : (part + 1) * CHUNK] = jnp.sum(
                dtaps_s[part, 8 * row : 8 * row + 8, :], axis=0, keepdims=True
            )
    whole_shrink, whole_expand = w_shrink, w_expand
    for part in range(PARTS):
        whole_shrink[:, part * CHUNK : (part + 1) * CHUNK] = g_shrink[part]
        whole_expand[:, part * CHUNK : (part + 1) * CHUNK] = g_expand[part]
    grads = {
        "reduce": g_reduce,
        "shrink": whole_shrink,
        "expand": whole_expand,
        "query": g_query,
        "output": g_output,
        "pairs": g_pairs,
        "wide": g_wide,
        "narrow": g_narrow,
    }
    blank = jnp.zeros((16, D), F32)

    def part_out(blobs, left):
        for d in range(plan.dp):
            for f in range(plan.fsdp):
                base = plan.base(d, f)
                for tile in range(plan.tiles):
                    held[0:16, :] = blank
                    for name, where, at, tall, wide, row, col in plan.chunks:
                        if where == tile:
                            r0, c0 = plan.origin(name, d, f)
                            held[0:tall, at : at + wide] = grads[name][
                                r0 + row : r0 + row + tall, c0 + col : c0 + col + wide
                            ]
                    blobs[base + 16 * tile : base + 16 * tile + 16, :] = held[0:16, :].astype(BF16)
        copy = pltpu.make_async_copy(blobs, gblob_ref, left)
        copy.start()
        copy.wait()

    pl.run_scoped(part_out, pltpu.VMEM(blob_ref.shape, BF16), pltpu.SemaphoreType.DMA)


def compute(plan, shape, tokens, cots, crops, blobs):
    canvases, length, width = shape
    rows = PAD_KEYS * canvases
    every = GROUPS * rows
    pair = 2 * canvases
    slab = GROUPS * pair
    vm = pl.BlockSpec(memory_space=pltpu.VMEM)
    hbm = pl.BlockSpec(memory_space=pl.ANY)

    def whole(dtype):
        return [
            pltpu.VMEM((D, GROUPS * D), dtype),
            pltpu.VMEM((PARTS, D, CHUNK), dtype),
            pltpu.VMEM((PARTS, D, CHUNK), dtype),
            pltpu.VMEM((D, D), dtype),
            pltpu.VMEM((D, D), dtype),
            pltpu.VMEM((D, 2 * D), dtype),
        ]

    scratch = [
        pltpu.VMEM((length, D), F32),
        pltpu.VMEM((2, length, D), BF16),
        pltpu.SemaphoreType.DMA((2,)),
        pltpu.SemaphoreType.DMA((2,)),
        pltpu.VMEM((every, D), F32),
        pltpu.VMEM((every, D), F32),
        pltpu.VMEM((every, D), BF16),
        pltpu.VMEM((every, D), BF16),
        pltpu.VMEM((rows, GROUPS * D), BF16),
        pltpu.VMEM((every, D), F32),
        pltpu.VMEM((every, D), BF16),
        pltpu.VMEM((canvases, GROUPS * PAD_KEYS, D), BF16),
        pltpu.VMEM((D // 2 * canvases, D), F32),
        pltpu.VMEM((D // 2 * canvases, D), F32),
        pltpu.VMEM((D // 2 * canvases, D), F32),
        pltpu.VMEM((D // 2 * canvases, D), F32),
        pltpu.VMEM((rows, D), BF16),
        pltpu.VMEM((every, D), BF16),
        pltpu.VMEM((every, D), F32),
        pltpu.VMEM((rows + 2 * MARGIN, D), F32),
        pltpu.VMEM((9, rows, D), BF16),
        pltpu.VMEM((canvases, 1, D), F32),
        pltpu.VMEM((PARTS, TAPS + 2, pair, CHUNK), BF16),
        pltpu.VMEM((PARTS, 8 * (TAPS + 2), CHUNK), F32),
        pltpu.VMEM((D, GROUPS * D), F32),
        pltpu.VMEM((D, FF), F32),
        pltpu.VMEM((D, FF), F32),
        pltpu.VMEM((D, D), F32),
        pltpu.VMEM((D, D), F32),
        pltpu.VMEM((D, 2 * D), F32),
        pltpu.VMEM((16, FF), F32),
        pltpu.VMEM((16, D), F32),
        *whole(BF16),
        *whole(F32),
        pltpu.VMEM((16, FF), F32),
        pltpu.VMEM((16, D), F32),
        pltpu.VMEM((88, D), F32),
    ]
    return pl.pallas_call(
        functools.partial(compute_kernel, plan),
        out_shape=(
            jax.ShapeDtypeStruct(shape, BF16),
            jax.ShapeDtypeStruct(shape, BF16),
            jax.ShapeDtypeStruct(blobs.shape, BF16),
        ),
        in_specs=[hbm, hbm, vm, hbm],
        out_specs=(hbm, hbm, hbm),
        scratch_shapes=scratch,
        compiler_params=pltpu.CompilerParams(vmem_limit_bytes=63 * 1024 * 1024),
    )(tokens, cots, crops, blobs)


NAMES = ("query", "pairs", "reduce", "output", "expand", "shrink")
TURNED = ("query", "reduce", "output", "shrink")
MESH = pl.DeviceIdType.MESH


class Place:
    def __init__(self, plan):
        self.plan = plan
        dp, fsdp = lax.axis_index("dp"), lax.axis_index("fsdp")
        self.core, self.y = lax.rem(dp, plan.cores), lax.div(dp, plan.cores)
        self.x, self.z = lax.rem(fsdp, plan.xs), lax.div(fsdp, plan.xs)
        self.dp, self.fsdp = dp, fsdp

    def device(self, core=0, y=0, x=0, z=0):
        plan = self.plan
        core = lax.rem(self.core + core, plan.cores)
        y, x = lax.rem(self.y + y, plan.ys), lax.rem(self.x + x, plan.xs)
        z = lax.rem(self.z + z, plan.zs)
        return {"dp": y * plan.cores + core, "fsdp": z * plan.xs + x}

    def block(self, core=0, y=0, x=0):
        plan = self.plan
        core = lax.rem(self.core + core, plan.cores)
        return pl.multiple_of((core * plan.ys * plan.xs + self.within(y, x)) * plan.zs * plan.rows, 16)

    def within(self, y=0, x=0):
        plan = self.plan
        return lax.rem(self.y + y, plan.ys) * plan.xs + lax.rem(self.x + x, plan.xs)

    def blob(self, z=0):
        plan = self.plan
        return pl.multiple_of(lax.rem(self.z + z, plan.zs) * plan.rows, 16)

    def partners(self):
        plan = self.plan
        return (
            [self.device(z=k) for k in range(1, plan.zs)]
            + [self.device(x=k) for k in range(1, plan.xs)]
            + [self.device(y=k) for k in range(1, plan.ys)]
            + [self.device(core=k) for k in range(1, plan.cores)]
        )


def greet(devices):
    barrier = pltpu.get_barrier_semaphore()
    for device in devices:
        pl.semaphore_signal(barrier, inc=1, device_id=device, device_id_type=MESH)
    pl.semaphore_wait(barrier, len(devices))


class Copies:
    def __init__(self, send, receive):
        self.send, self.receive, self.all = send, receive, []

    def start(self, source, target, device):
        number = len(self.all)
        copy = pltpu.make_async_remote_copy(
            src_ref=source,
            dst_ref=target,
            send_sem=self.send.at[number],
            recv_sem=self.receive.at[number],
            device_id=device,
            device_id_type=MESH,
        )
        copy.start()
        self.all.append(copy)
        return copy

    def finish(self):
        for copy in self.all:
            copy.wait_send()


def gather_count(plan):
    xs, ys, cores = plan.xs - 1, plan.ys - 1, plan.cores - 1
    return plan.zs - 1 + xs + ys + 2 * xs * ys + cores * (1 + xs + ys + 2 * xs * ys)


def gather_kernel(plan, *refs):
    count = len(PIECES)
    tokens_ref, cots_ref, pieces = refs[0], refs[1], refs[2 : 2 + count]
    out, grouped_tokens, grouped_cots = refs[2 + count : 5 + count]
    own_pieces = refs[5 + count : 5 + 2 * count]
    tile_s, stage, passing, held, low_tokens, low_cots = refs[5 + 2 * count : 11 + 2 * count]
    fetched, arrived, left, send, receive = refs[11 + 2 * count :]
    me = Place(plan)
    copies = Copies(send, receive)
    canvases = tokens_ref.shape[0]
    pair = 2 * canvases
    slab = GROUPS * pair

    def fetch(number, source, c):
        slot = 2 * number + lax.rem(c, 2)
        return pltpu.make_async_copy(source.at[c], passing.at[slot], arrived.at[slot])

    pulls = [
        pltpu.make_async_copy(ref, own, fetched.at[number])
        for number, (ref, own) in enumerate(zip(pieces, own_pieces))
    ]
    for copy in pulls:
        copy.start()
    fetch(0, cots_ref, 0).start()
    fetch(1, tokens_ref, 0).start()

    def regroup(number, source, low, target, start, stop):
        def one(c, _):
            @pl.when(c + 1 < canvases)
            def _():
                fetch(number, source, c + 1).start()

            fetch(number, source, c).wait()
            stage[...] = passing[2 * number + lax.rem(c, 2)].astype(F32)
            for token, place, size in places(slab, pair, canvases):
                held[pl.ds(place + c, size, stride=slab), :] = stage[pl.ds(token, size, stride=SIDE), :]
            return 0

        lax.fori_loop(start, stop, one, 0)
        if stop == canvases:
            low[...] = held[...].astype(BF16)
            leave = pltpu.make_async_copy(low, target, left.at[number])
            leave.start()
            return leave

    def regroup_cots(start, stop):
        return regroup(0, cots_ref, low_cots, grouped_cots, start, stop)

    def regroup_tokens(start, stop):
        return regroup(1, tokens_ref, low_tokens, grouped_tokens, start, stop)

    barrier = pltpu.get_barrier_semaphore()
    partners = me.partners()
    for device in partners:
        pl.semaphore_signal(barrier, inc=1, device_id=device, device_id_type=MESH)
    for g in range(GROUPS):
        start = (HALF - 1) * slab + g * pair + canvases
        held[start : start + canvases, :] = jnp.zeros((canvases, D), F32)
    source = {piece[0]: ref for piece, ref in zip(PIECES, own_pieces)}
    tile_s[...] = jnp.zeros_like(tile_s)
    for copy in pulls:
        copy.wait()
    for name, tile, at, tall, wide, row, col in plan.chunks:
        tile_s[16 * tile : 16 * tile + tall, at : at + wide] = source[name][
            row : row + tall, col : col + wide
        ]
    own = out.at[pl.ds(pl.multiple_of(me.block() + me.blob(), 16), plan.rows)]
    own[...] = tile_s[...].astype(BF16)
    pl.semaphore_wait(barrier, len(partners))
    group = plan.zs * plan.rows
    half = group // 2

    def part(y=0, x=0, second=None):
        start = me.block(y=y, x=x)
        if second is None:
            return out.at[pl.ds(start, group)]
        return out.at[pl.ds(pl.multiple_of(start + (half if second else 0), 16), half)]

    def pass_on(ref, device):
        return copies.start(ref, ref, device)

    def to_cores(ref):
        return [pass_on(ref, me.device(core=k)) for k in range(1, plan.cores)]

    waits = []
    along_z = [pass_on(own, me.device(z=k)) for k in range(1, plan.zs)]
    early, late = canvases // 2, canvases // 4
    regroup_cots(0, early)
    for copy in along_z:
        copy.wait_recv()
    along_x = {k: pass_on(part(), me.device(x=k)) for k in range(1, plan.xs)}
    along_y = {k: pass_on(part(), me.device(y=k)) for k in range(1, plan.ys)}
    waits += to_cores(part())
    cots_left = regroup_cots(early, canvases)
    regroup_tokens(0, late)
    first, second = {}, {}
    for kx, copy in along_x.items():
        copy.wait_recv()
        for ky in range(1, plan.ys):
            first[ky, kx] = pass_on(part(x=plan.xs - kx, second=False), me.device(y=ky))
        waits += to_cores(part(x=plan.xs - kx))
    for ky, copy in along_y.items():
        copy.wait_recv()
        for kx in range(1, plan.xs):
            second[ky, kx] = pass_on(part(y=plan.ys - ky, second=True), me.device(x=kx))
        waits += to_cores(part(y=plan.ys - ky))
    regroup_tokens(late, early)
    for number, table in enumerate((first, second)):
        for (ky, kx), copy in table.items():
            copy.wait_recv()
            waits += to_cores(part(y=plan.ys - ky, x=plan.xs - kx, second=bool(number)))
    tokens_left = regroup_tokens(early, canvases)
    for copy in waits:
        copy.wait_recv()
    copies.finish()
    cots_left.wait()
    tokens_left.wait()


def gather(plan, tokens, cots, shards):
    vm = pl.BlockSpec(memory_space=pltpu.VMEM)
    hbm = pl.BlockSpec(memory_space=pl.ANY)
    canvases, length, width = tokens.shape
    every = GROUPS * PAD_KEYS * canvases
    count = gather_count(plan)
    names = [piece[0] for piece in PIECES]
    return pl.pallas_call(
        functools.partial(gather_kernel, plan),
        out_shape=(
            jax.ShapeDtypeStruct((plan.devices * plan.rows, D), BF16),
            jax.ShapeDtypeStruct((every, D), BF16),
            jax.ShapeDtypeStruct((every, D), BF16),
        ),
        in_specs=[hbm] * (2 + len(PIECES)),
        out_specs=(vm, hbm, hbm),
        scratch_shapes=[
            *(pltpu.VMEM(plan.shard[name], F32) for name in names),
            pltpu.VMEM((plan.rows, D), F32),
            pltpu.VMEM((length, D), F32),
            pltpu.VMEM((4, length, D), BF16),
            pltpu.VMEM((every, D), F32),
            pltpu.VMEM((every, D), BF16),
            pltpu.VMEM((every, D), BF16),
            pltpu.SemaphoreType.DMA((len(PIECES),)),
            pltpu.SemaphoreType.DMA((4,)),
            pltpu.SemaphoreType.DMA((2,)),
            pltpu.SemaphoreType.DMA((count,)),
            pltpu.SemaphoreType.DMA((count,)),
        ],
        compiler_params=pltpu.CompilerParams(
            collective_id=1, has_side_effects=True, vmem_limit_bytes=62 * 1024 * 1024
        ),
    )(tokens, cots, *(shards[name] for name in names))


class Vectors:
    def __init__(self, plan, rows):
        self.chunks, used = [], []
        for name in NAMES:
            height, width = plan.shard[name]
            length = width if (name in TURNED) == rows else height
            for start in range(0, length, D):
                size = min(D, length - start)
                for row, taken in enumerate(used):
                    if taken + size <= D:
                        break
                else:
                    row = len(used)
                    used.append(0)
                self.chunks.append((name, row, used[row], size, start))
                used[row] += size
        self.rows = -(-len(used) // 8) * 8

    def of(self, name):
        return [chunk[1:] for chunk in self.chunks if chunk[0] == name]

    def put(self, ref, name, vector, offset=0):
        lanes = vector.shape[0] == 1
        for row, at, size, start in self.of(name):
            if lanes:
                line = vector[:, start : start + size]
            else:
                here = turn_spot(vector.shape[0], at)
                line = jnp.sum(jnp.where(here, vector, 0.0), axis=0, keepdims=True)
                line = line[:, at : at + size]
            ref[offset + row : offset + row + 1, at : at + size] = line

    def get_lanes(self, value, name):
        parts = [value[row : row + 1, at : at + size] for row, at, size, _ in self.of(name)]
        return parts[0] if len(parts) == 1 else jnp.concatenate(parts, axis=1)

    def get_column(self, value, name):
        ((row, at, size, _),) = self.of(name)
        here = turn_spot(size, at)
        return jnp.sum(jnp.where(here, value[row : row + 1, :], 0.0), axis=1, keepdims=True)


def turn_spot(size, at):
    lanes = lax.broadcasted_iota(jnp.int32, (size, D), 1)
    return lanes == lax.broadcasted_iota(jnp.int32, (size, D), 0) + at


def reduce_count(plan):
    xs, ys = plan.xs - 1, plan.ys - 1
    swap = plan.ys * plan.xs * (plan.cores - 1)
    return swap + 2 * xs * ys + xs + ys + plan.zs - 1 + 2 * (plan.dp - 1) + 2 * (plan.fsdp - 1)


def reduce_kernel(plan, *refs):
    gblob = refs[0]
    rowvars, colvars = refs[1:7], refs[7:13]
    second_wide, second_narrow = refs[13:15]
    outs = dict(zip([piece[0] for piece in PIECES], refs[15:23]))
    row_out, col_out, wide_out, narrow_out = refs[23:27]
    (
        swap_s,
        sum_s,
        first_s,
        second_s,
        along_x_s,
        along_y_s,
        own_s,
        away_s,
        along_z_s,
        grad_s,
        rows_s,
        cols_s,
        part_s,
        norm_s,
        old_s,
        send,
        receive,
    ) = refs[27:]
    me = Place(plan)
    copies = Copies(send, receive)
    group = plan.zs * plan.rows
    half = group // 2
    by_row, by_col = Vectors(plan, True), Vectors(plan, False)
    dp_peers = [{"dp": lax.rem(me.dp + k, plan.dp), "fsdp": me.fsdp} for k in range(1, plan.dp)]
    fsdp_peers = [{"dp": me.dp, "fsdp": lax.rem(me.fsdp + k, plan.fsdp)} for k in range(1, plan.fsdp)]
    greet(dp_peers + fsdp_peers)

    def spot(y, x):
        return pl.ds(pl.multiple_of(me.within(y, x) * group, 16), group)

    spots = sorted(((y, x) for y in range(plan.ys) for x in range(plan.xs)), key=lambda s: -(s[0] > 0) - (s[1] > 0))
    swaps = {}
    for y, x in spots:
        for k in range(1, plan.cores):
            source = gblob.at[pl.ds(me.block(core=k, y=y, x=x), group)]
            swaps[y, x] = copies.start(source, swap_s.at[spot(y, x)], me.device(core=k))

    def chip_sum(y, x):
        total = gblob[pl.ds(me.block(y=y, x=x), group), :].astype(F32)
        if (y, x) in swaps:
            swaps[y, x].wait_recv()
            total = total + swap_s[spot(y, x), :].astype(F32)
        return total

    pairs = [(y, x) for y in range(1, plan.ys) for x in range(1, plan.xs)]
    first, second = {}, {}
    for number, (y, x) in enumerate(pairs):
        here = spot(y, x)
        sum_s[here, :] = chip_sum(y, x).astype(BF16)
        base = me.within(y, x) * group
        low = sum_s.at[pl.ds(pl.multiple_of(base, 16), half)]
        high = sum_s.at[pl.ds(pl.multiple_of(base + half, 16), half)]
        first[y, x] = copies.start(low, first_s.at[number], me.device(y=y))
        second[y, x] = copies.start(high, second_s.at[number], me.device(x=x))
    along_x, along_y = {}, {}
    for x in range(1, plan.xs):
        own_s[...] = chip_sum(0, x)
        for number, (py, px) in enumerate(pairs):
            if px == x:
                first[py, px].wait_recv()
                own_s[:half, :] += first_s[number].astype(F32)
        sum_s[spot(0, x), :] = own_s[...].astype(BF16)
        along_x[x] = copies.start(sum_s.at[spot(0, x)], along_x_s.at[x - 1], me.device(x=x))
    for y in range(1, plan.ys):
        own_s[...] = chip_sum(y, 0)
        for number, (py, px) in enumerate(pairs):
            if py == y:
                second[py, px].wait_recv()
                own_s[half:, :] += second_s[number].astype(F32)
        sum_s[spot(y, 0), :] = own_s[...].astype(BF16)
        along_y[y] = copies.start(sum_s.at[spot(y, 0)], along_y_s.at[y - 1], me.device(y=y))
    own_s[...] = chip_sum(0, 0)
    for x, copy in along_x.items():
        copy.wait_recv()
        own_s[...] += along_x_s[x - 1].astype(F32)
    for y, copy in along_y.items():
        copy.wait_recv()
        own_s[...] += along_y_s[y - 1].astype(F32)

    away_s[...] = own_s[...].astype(BF16)
    along_z = [
        copies.start(away_s.at[pl.ds(me.blob(k), plan.rows)], along_z_s.at[k - 1], me.device(z=k))
        for k in range(1, plan.zs)
    ]
    total = own_s[pl.ds(me.blob(), plan.rows), :]
    for k, copy in enumerate(along_z):
        copy.wait_recv()
        total = total + along_z_s[k].astype(F32)
    grad_s[...] = total
    grads = {}
    for name, (height, width) in plan.shard.items():
        lines = {}
        for owner, tile, at, tall, wide, row, col in plan.chunks:
            if owner == name:
                lines.setdefault(row, []).append(
                    grad_s[16 * tile : 16 * tile + tall, at : at + wide]
                )
        lines = [parts[0] if len(parts) == 1 else jnp.concatenate(parts, axis=1) for parts in lines.values()]
        grads[name] = lines[0] if len(lines) == 1 else jnp.concatenate(lines, axis=0)

    decay_two = 1.0 - STEP ** (-0.8)

    def exchange(buffer, mine, peers):
        started = [copies.start(buffer.at[mine], buffer.at[mine], peer) for peer in peers]
        return started

    def gathered(buffer, started):
        for copy in started:
            copy.wait_recv()
        total = buffer[0]
        for number in range(1, buffer.shape[0]):
            total = total + buffer[number]
        return total

    full = {}
    own_rows, own_cols = rows_s.at[me.fsdp], cols_s.at[me.dp]
    own_rows[...] = jnp.zeros(own_rows.shape, F32)
    own_cols[...] = jnp.zeros(own_cols.shape, F32)
    for name in NAMES:
        height, width = plan.shard[name]
        square = grads[name] * grads[name] + SQUARE_EPS
        over_rows = jnp.sum(square, axis=0, keepdims=True)
        over_cols = jnp.sum(square, axis=1, keepdims=True)
        if name in TURNED:
            full[name] = (width * plan.dp, height * plan.fsdp)
            row_part, col_part = over_rows, over_cols
        else:
            full[name] = (height * plan.dp, width * plan.fsdp)
            row_part, col_part = over_cols, over_rows
        by_row.put(own_rows, name, row_part * ((1.0 - decay_two) / full[name][1]))
        by_col.put(own_cols, name, col_part * ((1.0 - decay_two) / full[name][0]))
    height, width = plan.shard["narrow"]
    own_cols[by_col.rows : by_col.rows + height, 0:width] = grads["narrow"]
    row_copies = exchange(rows_s, me.fsdp, fsdp_peers)
    col_copies = exchange(cols_s, me.dp, dp_peers)
    old_s[...] = jnp.zeros_like(old_s)
    for name, ref in zip(NAMES, rowvars):
        by_row.put(old_s, name, ref[...].reshape(1, ref.shape[0]))
    for name, ref in zip(NAMES, colvars):
        by_col.put(old_s, name, ref[...].reshape(1, ref.shape[0]), by_row.rows)
    wide = grads["wide"]
    wide_second = decay_two * second_wide[...] + (1.0 - decay_two) * (wide * wide + SQUARE_EPS)
    wide_out[...] = wide_second
    wide_update = wide * lax.rsqrt(wide_second)
    row_new = decay_two * old_s[: by_row.rows, :] + gathered(rows_s, row_copies)
    row_out[...] = row_new
    all_cols = gathered(cols_s, col_copies)[: by_col.rows, :]
    col_new = decay_two * old_s[by_row.rows :, :] + all_cols
    col_out[...] = col_new
    narrow = cols_s[0, by_col.rows : by_col.rows + height, 0:width]
    narrow_second = decay_two * second_narrow[...] + (1.0 - decay_two) * (narrow * narrow + SQUARE_EPS)
    narrow_out[...] = narrow_second
    narrow_update = narrow * lax.rsqrt(narrow_second)

    lane = lax.broadcasted_iota(jnp.int32, (16, D), 1)
    count = len(NAMES)

    def whole_sum(values):
        return jnp.sum(jnp.sum(values, axis=1, keepdims=True), axis=0, keepdims=True)

    def row_norm(values):
        norm = jnp.sum(values * values, axis=1, keepdims=True)
        return jnp.concatenate([norm, jnp.zeros((16 - norm.shape[0], 1), F32)], axis=0)

    updates = {}
    part = jnp.where(lane == 2 * count, row_norm(wide_update), 0.0)
    for number, name in enumerate(NAMES):
        lanes = by_row.get_lanes(row_new, name)
        if name in TURNED:
            row_scale = lax.rsqrt(lanes)
            col_scale = lax.rsqrt(by_col.get_column(col_new, name))
        else:
            row_scale = lax.rsqrt(by_row.get_column(row_new, name))
            col_scale = lax.rsqrt(by_col.get_lanes(col_new, name))
        update = grads[name] * row_scale * col_scale
        updates[name] = update
        part = jnp.where(lane == number, whole_sum(update * update), part)
        part = jnp.where(lane == count + number, whole_sum(lanes), part)
    part_s[me.dp] = part
    sums = gathered(part_s, exchange(part_s, me.dp, dp_peers))
    norm_s[me.fsdp] = jnp.where(lane == 2 * count + 1, row_norm(narrow_update), sums)
    norms = gathered(norm_s, exchange(norm_s, me.fsdp, fsdp_peers))
    for number, name in enumerate(NAMES):
        mean = sums[0:1, count + number : count + number + 1] / full[name][0]
        norm = norms[0:1, number : number + 1] / (full[name][0] * full[name][1])
        clip = jnp.maximum(1.0, jnp.sqrt(mean * norm) / CLIP_RMS)
        outs[name][...] = updates[name] * (jnp.sqrt(mean) / clip)
    for number, name, update in ((0, "wide", wide_update), (1, "narrow", narrow_update)):
        size = FF if name == "wide" else D
        norm = norms[: update.shape[0], 2 * count + number : 2 * count + number + 1] / size
        outs[name][...] = update / jnp.maximum(1.0, jnp.sqrt(norm) / CLIP_RMS)
    copies.finish()


def reduce_all(plan, gblobs, rowvars, colvars, second_wide, second_narrow):
    vm = pl.BlockSpec(memory_space=pltpu.VMEM)
    count = reduce_count(plan)
    by_row, by_col = Vectors(plan, True), Vectors(plan, False)
    group = plan.zs * plan.rows
    mine = plan.ys * plan.xs * group
    pairs = max(1, (plan.ys - 1) * (plan.xs - 1))
    thin = by_col.rows + 16
    out_shape = [jax.ShapeDtypeStruct(plan.shard[piece[0]], F32) for piece in PIECES]
    out_shape += [jax.ShapeDtypeStruct((by_row.rows, D), F32), jax.ShapeDtypeStruct((by_col.rows, D), F32)]
    out_shape += [jax.ShapeDtypeStruct(plan.shard[name], F32) for name in ("wide", "narrow")]
    return pl.pallas_call(
        functools.partial(reduce_kernel, plan),
        out_shape=out_shape,
        in_specs=[vm] * 15,
        out_specs=[vm] * 12,
        scratch_shapes=[
            pltpu.VMEM((mine, D), BF16),
            pltpu.VMEM((mine, D), BF16),
            pltpu.VMEM((pairs, group // 2, D), BF16),
            pltpu.VMEM((pairs, group // 2, D), BF16),
            pltpu.VMEM((max(1, plan.xs - 1), group, D), BF16),
            pltpu.VMEM((max(1, plan.ys - 1), group, D), BF16),
            pltpu.VMEM((group, D), F32),
            pltpu.VMEM((group, D), BF16),
            pltpu.VMEM((max(1, plan.zs - 1), plan.rows, D), BF16),
            pltpu.VMEM((plan.rows, D), F32),
            pltpu.VMEM((plan.fsdp, by_row.rows, D), F32),
            pltpu.VMEM((plan.dp, thin, D), F32),
            pltpu.VMEM((plan.dp, 16, D), F32),
            pltpu.VMEM((plan.fsdp, 16, D), F32),
            pltpu.VMEM((by_row.rows + by_col.rows, D), F32),
            pltpu.SemaphoreType.DMA((count,)),
            pltpu.SemaphoreType.DMA((count,)),
        ],
        compiler_params=pltpu.CompilerParams(
            collective_id=2, has_side_effects=True, vmem_limit_bytes=62 * 1024 * 1024
        ),
    )(gblobs, *rowvars, *colvars, second_wide, second_narrow)


def update_kernel(plan, *refs):
    order = [piece[0] for piece in PIECES]
    updates, moments, weights = (dict(zip(order, refs[8 * n : 8 * n + 8])) for n in range(3))
    row_new, col_new, second_wide, second_narrow = refs[24:28]
    new_moments, new_weights = (dict(zip(order, refs[8 * n + 28 : 8 * n + 36])) for n in range(2))
    row_outs, col_outs, wide_out, narrow_out = refs[44:50], refs[50:56], refs[56], refs[57]
    for name in order:
        moment = BETA_ONE * moments[name][...] + (1.0 - BETA_ONE) * updates[name][...]
        new_moments[name][...] = moment
        new_weights[name][...] = weights[name][...] * (1.0 - RATE * DECAY_RATE) - RATE * moment
    by_row, by_col = Vectors(plan, True), Vectors(plan, False)
    for vectors, source, targets in ((by_row, row_new, row_outs), (by_col, col_new, col_outs)):
        for name, ref in zip(NAMES, targets):
            for row, at, size, start in vectors.of(name):
                ref[start : start + size] = source[row : row + 1, at : at + size].reshape(size)
    wide_out[...] = second_wide[...]
    narrow_out[...] = second_narrow[...]


def update_all(plan, reduced, moments, weights):
    vm = pl.BlockSpec(memory_space=pltpu.VMEM)
    order = [piece[0] for piece in PIECES]
    pieces = [jax.ShapeDtypeStruct(plan.shard[name], F32) for name in order]
    row_shapes, col_shapes = [], []
    for name in NAMES:
        height, width = plan.shard[name]
        if name in TURNED:
            height, width = width, height
        row_shapes.append(jax.ShapeDtypeStruct((height,), F32))
        col_shapes.append(jax.ShapeDtypeStruct((width,), F32))
    seconds = [jax.ShapeDtypeStruct(plan.shard[name], F32) for name in ("wide", "narrow")]
    out_shape = pieces + pieces + row_shapes + col_shapes + seconds
    found = pl.pallas_call(
        functools.partial(update_kernel, plan),
        out_shape=out_shape,
        in_specs=[vm] * 28,
        out_specs=[vm] * len(out_shape),
    )(*reduced[:8], *(moments[name] for name in order), *(weights[name] for name in order), *reduced[8:])
    next_moment, next_weight = dict(zip(order, found[:8])), dict(zip(order, found[8:16]))
    return next_moment, next_weight, found[16:22], found[22:28], found[28], found[29]


def body(plan, tokens_in, cotangent, crop_ids, *state):
    weights, moments, rowvars, colvars = {}, {}, [], []
    for number, name in enumerate(NAMES):
        weights[name], moments[name], row, col = state[4 * number : 4 * number + 4]
        rowvars.append(row)
        colvars.append(col)
    weights["narrow"], moments["narrow"], second_narrow = state[24:27]
    weights["wide"], moments["wide"], second_wide = state[27:30]

    def turned(values):
        return {name: value.T if name in TURNED else value for name, value in values.items()}

    weights, moments = turned(weights), turned(moments)
    micro, local, length, width = tokens_in.shape
    flat = (micro * local, length, width)
    blobs, tokens, cots = gather(plan, tokens_in.reshape(flat), cotangent.reshape(flat), weights)
    result, input_grad, gblobs = compute(plan, flat, tokens, cots, crop_ids, blobs)
    reduced = reduce_all(plan, gblobs, rowvars, colvars, second_wide, second_narrow)
    next_moment, next_weight, row_new, col_new, wide_new, narrow_new = update_all(
        plan, reduced, moments, weights
    )
    next_moment, next_weight = turned(next_moment), turned(next_weight)
    results = [result.reshape(tokens_in.shape), input_grad.reshape(tokens_in.shape)]
    for number, name in enumerate(NAMES):
        results += [next_moment[name], row_new[number], col_new[number], next_weight[name]]
    for name, second in (("narrow", narrow_new), ("wide", wide_new)):
        results += [next_moment[name], second, next_weight[name]]
    return tuple(results)


def solution(mesh):
    plan = Plan(mesh.shape["dp"], mesh.shape["fsdp"])
    tokens = P(None, ("dp", "fsdp"), None, None)
    matrix = P("dp", "fsdp")
    by_rows, by_cols = P("dp"), P("fsdp")
    thin, broad = P(None, "fsdp"), P(None, ("dp", "fsdp"))
    state = (matrix, matrix, by_rows, by_cols) * 6 + (thin,) * 3 + (broad,) * 3
    in_specs = (tokens, tokens, P(None, ("dp", "fsdp"), None)) + state
    moved = (matrix, by_rows, by_cols, matrix) * 6 + (thin,) * 3 + (broad,) * 3
    return jax.shard_map(
        functools.partial(body, plan),
        mesh=mesh,
        in_specs=in_specs,
        out_specs=(tokens, tokens) + moved,
        check_vma=False,
    )
```
